32 devices in a mesh: band: 4 (over y, core), grid: 8 (over z, x).
Axes of the slice: x: 2, y: 2, z: 4, core: 2. Of those that a mesh axis runs over, the one named last changes fastest.
Arguments:
- orbitals: float32 [32, 8, 6, 128], P(('band', 'grid')), may hold values from -6 to 6
- region: int32 [8, 6, 128], replicated, may hold values from 0 to 15
- potential_table: float32 [16], replicated, may hold values from -3 to 3
- counts: int32 [4], replicated, may hold values from 2 to 8, as said below
- ritz: float32 [32, 32], P('band', 'grid'), may hold values from -1.5 to 1.5
Outputs:
- rotated: float32 [32, 6144], P('band', 'grid')
The draws below stay inside these ranges and needn't reach their ends.
Inputs may be any that keep to these rules, and one draw needn't show every extreme that they name: Some band block is full (counts equal to 8) in every draw.
All inputs are finite; a program needn't handle non-finite values.
Results may differ from the reference program's by a relative error of at most 0.000071.
Values sent between devices are 32-bit elements; how exact they have to be, the bound alone decides.
No kernel may reach another device: no remote copies, remote signals or barrier semaphores. Data moves between devices by JAX's collectives and lax.ppermute only.
A program may use at most 64 MiB of HBM per device.

```python
import jax
import jax.numpy as jnp
from jax import lax

PL = 8
GX = 128
DEGREE = 4
NREG = 16
NORB = 32
GY = 6
N_BAND = 4


def draw_counts(key, part):
    key = jax.random.fold_in(key, 7)
    first_key, second_key = jax.random.split(key)
    block_slots = NORB // N_BAND
    drawn = jax.random.randint(first_key, (N_BAND,), block_slots // 3, block_slots + 1)
    full_block = jax.random.randint(second_key, (), 0, N_BAND)
    return jnp.where(jnp.arange(N_BAND) == full_block, block_slots, drawn).astype(jnp.int32)


def place_ends(array, key, smallest, high):
    spot = [jax.random.randint(jax.random.fold_in(key, axis), (), 0, length) for axis, length in enumerate(array.shape)]
    widest = array.shape.index(max(array.shape))
    beside = spot[:widest] + [(spot[widest] + 1) % array.shape[widest]] + spot[widest + 1:]
    return array.at[tuple(spot)].set(smallest).at[tuple(beside)].set(high)


def raised(array, rng, source, target, shards_of, factor):
    owner, partner = [(jnp.arange(array.shape[dim]) // (array.shape[dim] // shards_of)).reshape([-1 if axis == dim else 1 for axis in range(array.ndim)]) for dim in (source, target)]
    chosen = jax.random.permutation(rng, shards_of)[partner]
    strong = (owner == chosen) | (owner == (partner + shards_of // 2) % shards_of)
    return jnp.where(strong, factor * array, array)


def block_scale(stream_key, shape, cuts, least, largest):
    def one(dim, shards_of):
        heights = jax.random.uniform(jax.random.fold_in(jax.random.fold_in(stream_key, 6), dim), (shards_of,), jnp.float32, least / len(cuts), largest / len(cuts))
        return jnp.repeat(jnp.exp(heights), shape[dim] // shards_of).reshape((-1,) + (1,) * (len(shape) - dim - 1))

    gain = one(*cuts[0])
    for cut in cuts[1:]:
        gain = gain * one(*cut)
    return gain


def centred(key, dims, scale, reach, pieces=(), kind=jnp.bfloat16):
    array = jax.random.normal(key, dims, jnp.float32) * scale
    if len(pieces) > 0:
        array = block_scale(key, dims, pieces, -0.22, 0.18) * array
    return jnp.clip(array, min=-reach, max=reach).astype(kind)


def bell_draw_with(rng, dims, scale, reach, shards, heavy, held_as=jnp.bfloat16):
    entries = scale * jax.random.normal(rng, dims, jnp.float32)
    if shards:
        entries = entries * block_scale(rng, dims, shards, -0.22, 0.18)
    return jnp.clip(raised(entries, jax.random.fold_in(rng, 3), *heavy), -reach, reach).astype(held_as)


def setup_inputs(seed: int = 0) -> dict:
    keys = jax.random.split(jax.random.key(seed), 6)
    return {
        "orbitals": centred(keys[0], (NORB, PL, GY, GX), 1.0, 6.0, ((0, 32),), jnp.float32),
        "region": place_ends(jax.random.randint(keys[1], (PL, GY, GX), 0, NREG), jax.random.fold_in(keys[1], 1), 0, NREG - 1).astype(jnp.int32),
        "potential_table": jnp.clip(jax.random.uniform(keys[2], (NREG,), jnp.float32, -3.0, 3.0), -3.0, 3.0),
        "counts": draw_counts(jax.random.fold_in(keys[5], 71), 0),
        "ritz": bell_draw_with(keys[4], (NORB, NORB), NORB ** -0.5, 1.5, ((0, 4), (1, 8)), (0, 1, 8, 2.0), jnp.float32),
    }


COEFFICIENTS = (-5369.0 / 1800.0, 12.0 / 7.0, -15.0 / 56.0, 10.0 / 189.0, -1.0 / 112.0, 2.0 / 1925.0, -1.0 / 16632.0)
SPACING = 0.5
LOWER = 6.0
UPPER = 46.0


def laplace(field):
    summed = (3.0 * COEFFICIENTS[0]) * field
    for offset in range(1, 7):
        for axis in (-3, -2, -1):
            summed = summed + COEFFICIENTS[offset] * (jnp.roll(field, offset, axis) + jnp.roll(field, -offset, axis))
    return summed / (SPACING * SPACING)


def apply_hamiltonian(field, potential):
    return -0.5 * laplace(field) + potential * field


def chebyshev(start_field, potential):
    half_width = (UPPER - LOWER) / 2.0
    centre = (UPPER + LOWER) / 2.0
    previous = start_field
    current = (apply_hamiltonian(start_field, potential) - centre * start_field) / half_width
    for step in range(DEGREE - 1):
        following = (2.0 / half_width) * (apply_hamiltonian(current, potential) - centre * current) - previous
        previous = current
        current = following
    return current


def reference(orbitals, region, potential_table, counts, ritz):
    block_slots = NORB // N_BAND
    orbital_ids = jnp.arange(NORB, dtype=jnp.int32)
    live = (orbital_ids % block_slots) < counts[orbital_ids // block_slots]
    masked = orbitals * live.astype(jnp.float32)[:, None, None, None]
    potential = potential_table[region]
    blocks = masked.reshape(N_BAND, block_slots, PL, GY, GX)
    filtered = lax.map(lambda block: chebyshev(block, potential), blocks)
    filtered = filtered.reshape(NORB, PL * GY * GX)
    return lax.dot_general(ritz, filtered, (((0,), (0,)), ((), ())), precision=lax.Precision.HIGHEST, preferred_element_type=jnp.float32)
```

```python
import functools

import jax
import jax.numpy as jnp
from jax import lax
from jax.experimental import pallas as pl
from jax.experimental.pallas import tpu as pltpu
from jax.sharding import PartitionSpec as P

DEGREE = 4

COEFFICIENTS = (
    -5369.0 / 1800.0,
    12.0 / 7.0,
    -15.0 / 56.0,
    10.0 / 189.0,
    -1.0 / 112.0,
    2.0 / 1925.0,
    -1.0 / 16632.0,
)
SPACING = 0.5
LOWER = 6.0
UPPER = 46.0
HALF = (UPPER - LOWER) / 2.0
CENTRE = (UPPER + LOWER) / 2.0
LANES = 128
SUBLANES = 8


def ring_weights(length):
    weights = [0.0] * length
    for offset in range(1, 7):
        weights[offset % length] += COEFFICIENTS[offset]
        weights[-offset % length] += COEFFICIENTS[offset]
    return weights


def pair_weights(length):
    weights = ring_weights(length)
    pairs = []
    for distance in range(1, length // 2 + 1):
        if weights[distance] != 0.0:
            pairs.append((sorted({distance, length - distance}), weights[distance]))
    return weights[0], pairs


def off_diagonal(field, planes, xs):
    ys = len(field)
    _, x_pairs = pair_weights(xs)
    _, y_pairs = pair_weights(ys)
    _, p_pairs = pair_weights(planes)
    results = []
    for y in range(ys):
        tile = field[y]
        total = None
        terms = []
        for shifts, weight in x_pairs:
            terms.append((weight, [pltpu.roll(tile, shift, 1) for shift in shifts]))
        for shifts, weight in p_pairs:
            terms.append((weight, [pltpu.roll(tile, shift, 0) for shift in shifts]))
        for shifts, weight in y_pairs:
            terms.append((weight, [field[(y - shift) % ys] for shift in shifts]))
        for weight, parts in terms:
            value = weight * functools.reduce(jnp.add, parts)
            total = value if total is None else total + value
        results.append(total)
    return results


def filter_kernel(nb, ng, rows, run, width, orb_ref, region_ref, ritz_ref, table_ref, counts_ref, out_ref):
    ys, planes, xs = orb_ref.shape
    band_pos = lax.axis_index("band")
    grid_pos = lax.axis_index("grid")
    live = (grid_pos < counts_ref[band_pos]).astype(jnp.float32)

    centre_weight = 3.0 * COEFFICIENTS[0] + sum(pair_weights(n)[0] for n in (planes, ys, xs))
    scale = 2.0 / HALF
    hop = -0.5 / (SPACING * SPACING) * scale
    diagonal = []
    for y in range(ys):
        region = region_ref[y]
        potential = jnp.zeros((planes, xs), jnp.float32)
        for index in range(table_ref.shape[0]):
            potential = jnp.where(region == index, table_ref[index], potential)
        diagonal.append(scale * potential + (hop * centre_weight - scale * CENTRE))

    def doubled(field):
        away = off_diagonal(field, planes, xs)
        return [diagonal[y] * field[y] + hop * away[y] for y in range(ys)]

    previous = [orb_ref[y] * live for y in range(ys)]
    current = [0.5 * value for value in doubled(previous)]
    for _ in range(DEGREE - 1):
        following = [value - before for value, before in zip(doubled(current), previous)]
        previous, current = current, following

    blocks = ys // run
    for b in range(nb):
        for y in range(ys):
            start = (b * ng + y // run) * rows + y % run
            out_ref[pl.ds(start, planes, stride=blocks * rows), :] = current[y]

    columns, panel = ritz_ref.shape
    per_row = LANES // width
    lane = lax.broadcasted_iota(jnp.int32, (1, LANES), 1)
    for row in range(-(-columns // per_row)):
        line = jnp.zeros((1, LANES), jnp.float32)
        for slot in range(min(per_row, columns - row * per_row)):
            piece = jnp.concatenate(
                [ritz_ref[pl.ds(row * per_row + slot, 1), :], jnp.zeros((1, LANES - panel), jnp.float32)], axis=1
            )
            line = line + (pltpu.roll(piece, slot * width, 1) if slot else piece)
        out_ref[pl.ds(run + row, nb * ng, stride=rows), :] = jnp.broadcast_to(line, (nb * ng, LANES))


def rotate_kernel(nb, ng, run, width, columns, got_ref, out_ref):
    wanted = out_ref.shape[0]
    panel = ng
    holders = wanted // columns
    first = lax.axis_index("band") * holders
    sublane = lax.broadcasted_iota(jnp.int32, (wanted, LANES), 0)
    lane = lax.broadcasted_iota(jnp.int32, (wanted, LANES), 1)
    own = lane // width == sublane % columns
    acc = [jnp.zeros((wanted, LANES), jnp.float32) for _ in range(run)]
    for b in range(nb):
        lines = jnp.zeros((wanted, LANES), jnp.float32)
        for k in range(holders):
            line = got_ref[b * ng + first + k, pl.ds(run, 1), :]
            lines = jnp.where(sublane // columns == k, jnp.broadcast_to(line, (wanted, LANES)), lines)
        lines = jnp.where(own, lines, 0.0)
        gathered = lines
        for slot in range(1, columns):
            gathered = gathered + pltpu.roll(lines, LANES - slot * width, 1)
        for r in range(panel):
            weight = jnp.broadcast_to(gathered[:, r : r + 1], (wanted, LANES))
            for y in range(run):
                acc[y] = acc[y] + weight * got_ref[b * ng + r, pl.ds(y, 1), :]
    for y in range(run):
        out_ref[:, pl.ds(y * LANES, LANES)] = acc[y]


def shards(nb, ng, orbitals, region, potential_table, counts, ritz):
    _, planes, ys, xs = orbitals.shape
    cells = planes * ys * xs
    panel, columns = ritz.shape
    run = cells // ng // xs
    width = 1
    while width < panel:
        width *= 2
    per_row = LANES // width
    ritz_rows = -(-columns // per_row)
    rows = -(-(run + ritz_rows) // SUBLANES) * SUBLANES
    devices = nb * ng
    vmem = pl.BlockSpec(memory_space=pltpu.VMEM)
    smem = pl.BlockSpec(memory_space=pltpu.SMEM)
    packed = pl.pallas_call(
        functools.partial(filter_kernel, nb, ng, rows, run, width),
        out_shape=jax.ShapeDtypeStruct((devices * rows, LANES), jnp.float32),
        in_specs=[vmem, vmem, vmem, smem, smem],
        out_specs=vmem,
        name="chebyshev_filter",
    )(
        jnp.transpose(orbitals[0], (1, 0, 2)),
        jnp.transpose(region, (1, 0, 2)),
        ritz.T,
        potential_table,
        counts,
    )
    got = lax.all_to_all(
        packed.reshape(devices, rows, LANES), ("band", "grid"), split_axis=0, concat_axis=0, tiled=True
    )
    if columns * width <= LANES and devices <= 64 and panel == ng:
        return pl.pallas_call(
            functools.partial(rotate_kernel, nb, ng, run, width, columns),
            out_shape=jax.ShapeDtypeStruct((panel, run * LANES), jnp.float32),
            in_specs=[vmem],
            out_specs=vmem,
            name="ritz_rotation",
        )(got)
    holders = panel // columns
    mine = lax.dynamic_slice_in_dim(
        got[:, run : run + ritz_rows].reshape(nb, ng, ritz_rows * per_row, width),
        lax.axis_index("band") * holders,
        holders,
        axis=1,
    )
    weights = jnp.transpose(mine[:, :, :columns, :panel], (0, 3, 1, 2)).reshape(devices, panel)
    return lax.dot_general(
        weights,
        got[:, :run].reshape(devices, run * LANES),
        (((0,), (0,)), ((), ())),
        precision=lax.Precision.HIGHEST,
        preferred_element_type=jnp.float32,
    )


def solution(mesh):
    return jax.shard_map(
        functools.partial(shards, mesh.shape["band"], mesh.shape["grid"]),
        mesh=mesh,
        in_specs=(P(("band", "grid"), None, None, None), P(), P(), P(), P("band", "grid")),
        out_specs=P("band", "grid"),
        check_vma=False,
    )
```

```python
import functools

import jax
import jax.numpy as jnp
from jax import lax
from jax.experimental import pallas as pl
from jax.experimental.pallas import tpu as pltpu
from jax.sharding import PartitionSpec as P

DEGREE = 4

COEFFICIENTS = (
    -5369.0 / 1800.0,
    12.0 / 7.0,
    -15.0 / 56.0,
    10.0 / 189.0,
    -1.0 / 112.0,
    2.0 / 1925.0,
    -1.0 / 16632.0,
)
SPACING = 0.5
LOWER = 6.0
UPPER = 46.0
HALF = (UPPER - LOWER) / 2.0
CENTRE = (UPPER + LOWER) / 2.0
LANES = 128
SUBLANES = 8


def ring_weights(length):
    weights = [0.0] * length
    for offset in range(1, 7):
        weights[offset % length] += COEFFICIENTS[offset]
        weights[-offset % length] += COEFFICIENTS[offset]
    return weights


def pair_weights(length):
    weights = ring_weights(length)
    pairs = []
    for distance in range(1, length // 2 + 1):
        if weights[distance] != 0.0:
            pairs.append((sorted({distance, length - distance}), weights[distance]))
    return weights[0], pairs


def off_diagonal(field, planes, xs):
    ys = len(field)
    _, x_pairs = pair_weights(xs)
    _, y_pairs = pair_weights(ys)
    _, p_pairs = pair_weights(planes)
    results = []
    for y in range(ys):
        tile = field[y]
        total = None
        terms = []
        for shifts, weight in x_pairs:
            terms.append((weight, [pltpu.roll(tile, shift, 1) for shift in shifts]))
        for shifts, weight in p_pairs:
            terms.append((weight, [pltpu.roll(tile, shift, 0) for shift in shifts]))
        for shifts, weight in y_pairs:
            terms.append((weight, [field[(y - shift) % ys] for shift in shifts]))
        for weight, parts in terms:
            value = weight * functools.reduce(jnp.add, parts)
            total = value if total is None else total + value
        results.append(total)
    return results


def filter_kernel(nb, ng, rows, run, width, *refs):
    sources, out_ref, held, sems = refs[:5], refs[5], refs[6:11], refs[11]
    orb_ref, region_ref, ritz_ref, table_ref, counts_ref = held
    copies = [
        pltpu.make_async_copy(source, target, sems.at[index])
        for index, (source, target) in enumerate(zip(sources, held))
    ]
    for copy in copies:
        copy.start()
    for copy in copies:
        copy.wait()
    ys, planes, xs = orb_ref.shape
    band_pos = lax.axis_index("band")
    grid_pos = lax.axis_index("grid")
    live = (grid_pos < counts_ref[band_pos]).astype(jnp.float32)

    centre_weight = 3.0 * COEFFICIENTS[0] + sum(pair_weights(n)[0] for n in (planes, ys, xs))
    scale = 2.0 / HALF
    hop = -0.5 / (SPACING * SPACING) * scale
    diagonal = []
    for y in range(ys):
        region = region_ref[y]
        potential = jnp.zeros((planes, xs), jnp.float32)
        for index in range(table_ref.shape[0]):
            potential = jnp.where(region == index, table_ref[index], potential)
        diagonal.append(scale * potential + (hop * centre_weight - scale * CENTRE))

    def doubled(field):
        away = off_diagonal(field, planes, xs)
        return [diagonal[y] * field[y] + hop * away[y] for y in range(ys)]

    previous = [orb_ref[y] * live for y in range(ys)]
    current = [0.5 * value for value in doubled(previous)]
    for _ in range(DEGREE - 1):
        following = [value - before for value, before in zip(doubled(current), previous)]
        previous, current = current, following

    blocks = ys // run
    for b in range(nb):
        for y in range(ys):
            start = (b * ng + y // run) * rows + y % run
            out_ref[pl.ds(start, planes, stride=blocks * rows), :] = current[y]

    columns, panel = ritz_ref.shape
    per_row = LANES // width
    lane = lax.broadcasted_iota(jnp.int32, (1, LANES), 1)
    for row in range(-(-columns // per_row)):
        line = jnp.zeros((1, LANES), jnp.float32)
        for slot in range(min(per_row, columns - row * per_row)):
            piece = jnp.concatenate(
                [ritz_ref[pl.ds(row * per_row + slot, 1), :], jnp.zeros((1, LANES - panel), jnp.float32)], axis=1
            )
            line = line + (pltpu.roll(piece, slot * width, 1) if slot else piece)
        out_ref[pl.ds(run + row, nb * ng, stride=rows), :] = jnp.broadcast_to(line, (nb * ng, LANES))


def rotate_kernel(nb, ng, run, width, columns, got_ref, out_ref):
    wanted = out_ref.shape[0]
    panel = ng
    holders = wanted // columns
    first = lax.axis_index("band") * holders
    sublane = lax.broadcasted_iota(jnp.int32, (wanted, LANES), 0)
    lane = lax.broadcasted_iota(jnp.int32, (wanted, LANES), 1)
    own = lane // width == sublane % columns
    acc = [jnp.zeros((wanted, LANES), jnp.float32) for _ in range(run)]
    for b in range(nb):
        lines = jnp.zeros((wanted, LANES), jnp.float32)
        for k in range(holders):
            line = got_ref[b * ng + first + k, pl.ds(run, 1), :]
            lines = jnp.where(sublane // columns == k, jnp.broadcast_to(line, (wanted, LANES)), lines)
        lines = jnp.where(own, lines, 0.0)
        gathered = lines
        for slot in range(1, columns):
            gathered = gathered + pltpu.roll(lines, LANES - slot * width, 1)
        for r in range(panel):
            weight = jnp.broadcast_to(gathered[:, r : r + 1], (wanted, LANES))
            for y in range(run):
                acc[y] = acc[y] + weight * got_ref[b * ng + r, pl.ds(y, 1), :]
    for y in range(run):
        out_ref[:, pl.ds(y * LANES, LANES)] = acc[y]


def shards(nb, ng, orbitals, region, potential_table, counts, ritz):
    _, planes, ys, xs = orbitals.shape
    cells = planes * ys * xs
    panel, columns = ritz.shape
    run = cells // ng // xs
    width = 1
    while width < panel:
        width *= 2
    per_row = LANES // width
    ritz_rows = -(-columns // per_row)
    rows = -(-(run + ritz_rows) // SUBLANES) * SUBLANES
    devices = nb * ng
    vmem = pl.BlockSpec(memory_space=pltpu.VMEM)
    hbm = pl.BlockSpec(memory_space=pltpu.HBM)
    packed_bytes = 4 * devices * rows * LANES
    packed = pl.pallas_call(
        functools.partial(filter_kernel, nb, ng, rows, run, width),
        out_shape=jax.ShapeDtypeStruct((devices * rows, LANES), jnp.float32),
        in_specs=[hbm] * 5,
        out_specs=vmem,
        scratch_shapes=[
            pltpu.VMEM((ys, planes, xs), jnp.float32),
            pltpu.VMEM((ys, planes, xs), jnp.int32),
            pltpu.VMEM((columns, panel), jnp.float32),
            pltpu.SMEM(potential_table.shape, jnp.float32),
            pltpu.SMEM(counts.shape, jnp.int32),
            pltpu.SemaphoreType.DMA((5,)),
        ],
        compiler_params=pltpu.CompilerParams(vmem_limit_bytes=packed_bytes + 32 * cells + 2**20),
        name="chebyshev_filter",
    )(
        jnp.transpose(orbitals[0], (1, 0, 2)),
        jnp.transpose(region, (1, 0, 2)),
        ritz.T,
        potential_table,
        counts,
    )
    got = lax.all_to_all(
        packed.reshape(devices, rows, LANES), ("band", "grid"), split_axis=0, concat_axis=0, tiled=True
    )
    if columns * width <= LANES and devices <= 64 and panel == ng:
        return pl.pallas_call(
            functools.partial(rotate_kernel, nb, ng, run, width, columns),
            out_shape=jax.ShapeDtypeStruct((panel, run * LANES), jnp.float32),
            in_specs=[vmem],
            out_specs=vmem,
            compiler_params=pltpu.CompilerParams(vmem_limit_bytes=packed_bytes + 2**20),
            name="ritz_rotation",
        )(got)
    holders = panel // columns
    mine = lax.dynamic_slice_in_dim(
        got[:, run : run + ritz_rows].reshape(nb, ng, ritz_rows * per_row, width),
        lax.axis_index("band") * holders,
        holders,
        axis=1,
    )
    weights = jnp.transpose(mine[:, :, :columns, :panel], (0, 3, 1, 2)).reshape(devices, panel)
    return lax.dot_general(
        weights,
        got[:, :run].reshape(devices, run * LANES),
        (((0,), (0,)), ((), ())),
        precision=lax.Precision.HIGHEST,
        preferred_element_type=jnp.float32,
    )


def solution(mesh):
    return jax.shard_map(
        functools.partial(shards, mesh.shape["band"], mesh.shape["grid"]),
        mesh=mesh,
        in_specs=(P(("band", "grid"), None, None, None), P(), P(), P(), P("band", "grid")),
        out_specs=P("band", "grid"),
        check_vma=False,
    )
```

```python
import functools

import jax
import jax.numpy as jnp
from jax import lax
from jax.experimental import pallas as pl
from jax.experimental.pallas import tpu as pltpu
from jax.sharding import PartitionSpec as P

DEGREE = 4

COEFFICIENTS = (
    -5369.0 / 1800.0,
    12.0 / 7.0,
    -15.0 / 56.0,
    10.0 / 189.0,
    -1.0 / 112.0,
    2.0 / 1925.0,
    -1.0 / 16632.0,
)
SPACING = 0.5
LOWER = 6.0
UPPER = 46.0
HALF = (UPPER - LOWER) / 2.0
CENTRE = (UPPER + LOWER) / 2.0
LANES = 128
SUBLANES = 8


def ring_weights(length):
    weights = [0.0] * length
    for offset in range(1, 7):
        weights[offset % length] += COEFFICIENTS[offset]
        weights[-offset % length] += COEFFICIENTS[offset]
    return weights


def pair_weights(length):
    weights = ring_weights(length)
    pairs = []
    for distance in range(1, length // 2 + 1):
        if weights[distance] != 0.0:
            pairs.append((sorted({distance, length - distance}), weights[distance]))
    return weights[0], pairs


def off_diagonal(field, planes, xs):
    ys = len(field)
    _, x_pairs = pair_weights(xs)
    _, y_pairs = pair_weights(ys)
    _, p_pairs = pair_weights(planes)
    results = []
    for y in range(ys):
        tile = field[y]
        total = None
        terms = []
        for shifts, weight in x_pairs:
            terms.append((weight, [pltpu.roll(tile, shift, 1) for shift in shifts]))
        for shifts, weight in p_pairs:
            terms.append((weight, [pltpu.roll(tile, shift, 0) for shift in shifts]))
        for shifts, weight in y_pairs:
            terms.append((weight, [field[(y - shift) % ys] for shift in shifts]))
        for weight, parts in terms:
            value = weight * functools.reduce(jnp.add, parts)
            total = value if total is None else total + value
        results.append(total)
    return results


def filter_kernel(nb, ng, rows, run, width, pairwise, *refs):
    sources, outs, held, sems = refs[:5], refs[5:-6], refs[-6:-1], refs[-1]
    out_ref = outs[-1]
    copies_of_tiles = 1 if pairwise else nb
    orb_ref, region_ref, ritz_ref, table_ref, counts_ref = held
    copies = [
        pltpu.make_async_copy(source, target, sems.at[index])
        for index, (source, target) in enumerate(zip(sources, held))
    ]
    for copy in copies:
        copy.start()
    for copy in copies:
        copy.wait()
    ys, planes, xs = orb_ref.shape
    band_pos = lax.axis_index("band")
    grid_pos = lax.axis_index("grid")
    live = (grid_pos < counts_ref[band_pos]).astype(jnp.float32)

    centre_weight = 3.0 * COEFFICIENTS[0] + sum(pair_weights(n)[0] for n in (planes, ys, xs))
    scale = 2.0 / HALF
    hop = -0.5 / (SPACING * SPACING) * scale
    diagonal = []
    for y in range(ys):
        region = region_ref[y]
        potential = jnp.zeros((planes, xs), jnp.float32)
        for index in range(table_ref.shape[0]):
            potential = jnp.where(region == index, table_ref[index], potential)
        diagonal.append(scale * potential + (hop * centre_weight - scale * CENTRE))

    def doubled(field):
        away = off_diagonal(field, planes, xs)
        return [diagonal[y] * field[y] + hop * away[y] for y in range(ys)]

    previous = [orb_ref[y] * live for y in range(ys)]
    current = [0.5 * value for value in doubled(previous)]
    for _ in range(DEGREE - 1):
        following = [value - before for value, before in zip(doubled(current), previous)]
        previous, current = current, following

    blocks = ys // run
    for b in range(copies_of_tiles):
        for y in range(ys):
            start = (b * ng + y // run) * rows + y % run
            out_ref[pl.ds(start, planes, stride=blocks * rows), :] = current[y]

    columns, panel = ritz_ref.shape
    per_row = LANES // width
    lane = lax.broadcasted_iota(jnp.int32, (1, LANES), 1)
    for row in range(-(-columns // per_row)):
        line = jnp.zeros((1, LANES), jnp.float32)
        for slot in range(min(per_row, columns - row * per_row)):
            piece = jnp.concatenate(
                [ritz_ref[pl.ds(row * per_row + slot, 1), :], jnp.zeros((1, LANES - panel), jnp.float32)], axis=1
            )
            line = line + (pltpu.roll(piece, slot * width, 1) if slot else piece)
        tiles = copies_of_tiles * ng
        out_ref[pl.ds(run + row, tiles, stride=rows), :] = jnp.broadcast_to(line, (tiles, LANES))
    if pairwise:
        for distance, tile_ref in enumerate(outs[:-1]):
            start = pl.multiple_of((grid_pos ^ distance) * rows, rows)
            tile_ref[...] = out_ref[pl.ds(start, rows), :]


def partial_kernel(nb, ng, run, width, columns, *refs):
    tiles, outs, held_ref = refs[:ng], refs[ng:-1], refs[-1]
    band_pos = lax.axis_index("band")
    grid_pos = lax.axis_index("grid")
    for distance, tile_ref in enumerate(tiles):
        held_ref[grid_pos ^ distance] = tile_ref[...]
    wanted = outs[0].shape[0]
    holders = wanted // columns
    sublane = lax.broadcasted_iota(jnp.int32, (wanted, LANES), 0)
    lane = lax.broadcasted_iota(jnp.int32, (wanted, LANES), 1)
    own = lane // width == sublane % columns
    for distance, out_ref in enumerate(outs):
        first = (band_pos ^ distance) * holders
        lines = jnp.zeros((wanted, LANES), jnp.float32)
        for k in range(holders):
            line = held_ref[first + k, pl.ds(run, 1), :]
            lines = jnp.where(sublane // columns == k, jnp.broadcast_to(line, (wanted, LANES)), lines)
        lines = jnp.where(own, lines, 0.0)
        gathered = lines
        for slot in range(1, columns):
            gathered = gathered + pltpu.roll(lines, LANES - slot * width, 1)
        acc = [jnp.zeros((wanted, LANES), jnp.float32) for _ in range(run)]
        for r in range(ng):
            weight = jnp.broadcast_to(gathered[:, r : r + 1], (wanted, LANES))
            for y in range(run):
                acc[y] = acc[y] + weight * held_ref[r, pl.ds(y, 1), :]
        for y in range(run):
            out_ref[:, pl.ds(y * LANES, LANES)] = acc[y]


def sum_kernel(*refs):
    refs[-1][...] = functools.reduce(jnp.add, [ref[...] for ref in refs[:-1]])


def exchange(value, axis, size, distance):
    return lax.ppermute(value, axis, [(place, place ^ distance) for place in range(size)])


def shards(nb, ng, orbitals, region, potential_table, counts, ritz):
    _, planes, ys, xs = orbitals.shape
    cells = planes * ys * xs
    panel, columns = ritz.shape
    run = cells // ng // xs
    width = 1
    while width < panel:
        width *= 2
    per_row = LANES // width
    ritz_rows = -(-columns // per_row)
    rows = -(-(run + ritz_rows) // SUBLANES) * SUBLANES
    devices = nb * ng
    vmem = pl.BlockSpec(memory_space=pltpu.VMEM)
    hbm = pl.BlockSpec(memory_space=pltpu.HBM)
    pairwise = (
        columns * width <= LANES and panel == ng and run + 1 <= rows == SUBLANES
        and ng & (ng - 1) == 0 and nb & (nb - 1) == 0 and devices <= 64
    )
    inputs = [
        pltpu.with_memory_space_constraint(value, pltpu.HBM)
        for value in (
            jnp.transpose(orbitals[0], (1, 0, 2)), jnp.transpose(region, (1, 0, 2)), ritz.T, potential_table, counts
        )
    ]
    packed_bytes = 4 * devices * rows * LANES
    packed = jax.ShapeDtypeStruct((devices * rows, LANES), jnp.float32)
    tile = jax.ShapeDtypeStruct((rows, LANES), jnp.float32)
    filtered = pl.pallas_call(
        functools.partial(filter_kernel, nb, ng, rows, run, width, pairwise),
        out_shape=[tile] * ng if pairwise else [packed],
        in_specs=[hbm] * 5,
        out_specs=[vmem] * (ng if pairwise else 1),
        scratch_shapes=[pltpu.VMEM((ng * rows, LANES), jnp.float32)] * int(pairwise)
        + [
            pltpu.VMEM((ys, planes, xs), jnp.float32),
            pltpu.VMEM((ys, planes, xs), jnp.int32),
            pltpu.VMEM((columns, panel), jnp.float32),
            pltpu.SMEM(potential_table.shape, jnp.float32),
            pltpu.SMEM(counts.shape, jnp.int32),
            pltpu.SemaphoreType.DMA((5,)),
        ],
        compiler_params=pltpu.CompilerParams(vmem_limit_bytes=packed_bytes + 32 * cells + 2**20),
        name="chebyshev_filter",
    )(*inputs)
    if pairwise:
        tiles = [filtered[0]] + [exchange(filtered[d], "grid", ng, d) for d in range(1, ng)]
        sums = pl.pallas_call(
            functools.partial(partial_kernel, nb, ng, run, width, columns),
            out_shape=[jax.ShapeDtypeStruct((panel, run * LANES), jnp.float32)] * nb,
            in_specs=[vmem] * ng,
            out_specs=[vmem] * nb,
            scratch_shapes=[pltpu.VMEM((ng, rows, LANES), jnp.float32)],
            compiler_params=pltpu.CompilerParams(vmem_limit_bytes=packed_bytes + 2**20),
            name="ritz_partial_sums",
        )(*tiles)
        terms = [sums[0]] + [exchange(sums[d], "band", nb, d) for d in range(1, nb)]
        return pl.pallas_call(
            sum_kernel,
            out_shape=jax.ShapeDtypeStruct((panel, run * LANES), jnp.float32),
            in_specs=[vmem] * nb,
            out_specs=vmem,
            compiler_params=pltpu.CompilerParams(vmem_limit_bytes=packed_bytes + 2**20),
            name="band_sum",
        )(*terms)
    packed = filtered[0]
    got = lax.all_to_all(
        packed.reshape(devices, rows, LANES), ("band", "grid"), split_axis=0, concat_axis=0, tiled=True
    )
    holders = panel // columns
    mine = lax.dynamic_slice_in_dim(
        got[:, run : run + ritz_rows].reshape(nb, ng, ritz_rows * per_row, width),
        lax.axis_index("band") * holders,
        holders,
        axis=1,
    )
    weights = jnp.transpose(mine[:, :, :columns, :panel], (0, 3, 1, 2)).reshape(devices, panel)
    return lax.dot_general(
        weights,
        got[:, :run].reshape(devices, run * LANES),
        (((0,), (0,)), ((), ())),
        precision=lax.Precision.HIGHEST,
        preferred_element_type=jnp.float32,
    )


def solution(mesh):
    return jax.shard_map(
        functools.partial(shards, mesh.shape["band"], mesh.shape["grid"]),
        mesh=mesh,
        in_specs=(P(("band", "grid"), None, None, None), P(), P(), P(), P("band", "grid")),
        out_specs=P("band", "grid"),
        check_vma=False,
    )
```

```python
import functools

import jax
import jax.numpy as jnp
from jax import lax
from jax.experimental import pallas as pl
from jax.experimental.pallas import tpu as pltpu
from jax.sharding import PartitionSpec as P

DEGREE = 4

COEFFICIENTS = (
    -5369.0 / 1800.0,
    12.0 / 7.0,
    -15.0 / 56.0,
    10.0 / 189.0,
    -1.0 / 112.0,
    2.0 / 1925.0,
    -1.0 / 16632.0,
)
SPACING = 0.5
LOWER = 6.0
UPPER = 46.0
HALF = (UPPER - LOWER) / 2.0
CENTRE = (UPPER + LOWER) / 2.0
LANES = 128
SUBLANES = 8


def ring_weights(length):
    weights = [0.0] * length
    for offset in range(1, 7):
        weights[offset % length] += COEFFICIENTS[offset]
        weights[-offset % length] += COEFFICIENTS[offset]
    return weights


def pair_weights(length):
    weights = ring_weights(length)
    pairs = []
    for distance in range(1, length // 2 + 1):
        if weights[distance] != 0.0:
            pairs.append((sorted({distance, length - distance}), weights[distance]))
    return weights[0], pairs


def off_diagonal(field, planes, xs):
    ys = len(field)
    _, x_pairs = pair_weights(xs)
    _, y_pairs = pair_weights(ys)
    _, p_pairs = pair_weights(planes)
    results = []
    for y in range(ys):
        tile = field[y]
        total = None
        terms = []
        for shifts, weight in x_pairs:
            terms.append((weight, [pltpu.roll(tile, shift, 1) for shift in shifts]))
        for shifts, weight in p_pairs:
            terms.append((weight, [pltpu.roll(tile, shift, 0) for shift in shifts]))
        for shifts, weight in y_pairs:
            terms.append((weight, [field[(y - shift) % ys] for shift in shifts]))
        for weight, parts in terms:
            value = weight * functools.reduce(jnp.add, parts)
            total = value if total is None else total + value
        results.append(total)
    return results


def filter_kernel(ng, copies, rows, run, width, cores, *refs):
    sources, out_ref, held, sems = refs[:5], refs[5], refs[6:11], refs[11]
    orb_ref, region_ref, ritz_ref, table_ref, counts_ref = held
    transfers = [
        pltpu.make_async_copy(source, target, sems.at[index])
        for index, (source, target) in enumerate(zip(sources, held))
    ]
    for transfer in transfers:
        transfer.start()
    for transfer in transfers:
        transfer.wait()
    ys, planes, xs = orb_ref.shape
    band_pos = lax.axis_index("row") * cores + lax.axis_index("core")
    live = (lax.axis_index("grid") < counts_ref[band_pos]).astype(jnp.float32)

    centre_weight = 3.0 * COEFFICIENTS[0] + sum(pair_weights(n)[0] for n in (planes, ys, xs))
    scale = 2.0 / HALF
    hop = -0.5 / (SPACING * SPACING) * scale
    diagonal = []
    for y in range(ys):
        region = region_ref[y]
        potential = jnp.zeros((planes, xs), jnp.float32)
        for index in range(table_ref.shape[0]):
            potential = jnp.where(region == index, table_ref[index], potential)
        diagonal.append(scale * potential + (hop * centre_weight - scale * CENTRE))

    def doubled(field):
        away = off_diagonal(field, planes, xs)
        return [diagonal[y] * field[y] + hop * away[y] for y in range(ys)]

    previous = [orb_ref[y] * live for y in range(ys)]
    current = [0.5 * value for value in doubled(previous)]
    for _ in range(DEGREE - 1):
        following = [value - before for value, before in zip(doubled(current), previous)]
        previous, current = current, following

    blocks = ys // run
    for copy in range(copies):
        for y in range(ys):
            start = (copy * ng + y // run) * rows + y % run
            out_ref[pl.ds(start, planes, stride=blocks * rows), :] = current[y]

    columns, panel = ritz_ref.shape
    per_row = LANES // width
    tiles = copies * ng
    for row in range(-(-columns // per_row)):
        line = jnp.zeros((1, LANES), jnp.float32)
        for slot in range(min(per_row, columns - row * per_row)):
            piece = jnp.concatenate(
                [ritz_ref[pl.ds(row * per_row + slot, 1), :], jnp.zeros((1, LANES - panel), jnp.float32)], axis=1
            )
            line = line + (pltpu.roll(piece, slot * width, 1) if slot else piece)
        out_ref[pl.ds(run + row, tiles, stride=rows), :] = jnp.broadcast_to(line, (tiles, LANES))


def partial_kernel(nrow, ng, run, width, columns, cores, got_ref, *outs):
    wanted = outs[0].shape[0]
    holders = wanted // columns
    sublane = lax.broadcasted_iota(jnp.int32, (wanted, LANES), 0)
    lane = lax.broadcasted_iota(jnp.int32, (wanted, LANES), 1)
    own = lane // width == sublane % columns
    weights = []
    for distance in range(cores):
        block = lax.axis_index("row") * cores + lax.rem(lax.axis_index("core") + distance, cores)
        gathered = []
        for row in range(nrow):
            lines = jnp.zeros((wanted, LANES), jnp.float32)
            for k in range(holders):
                line = got_ref[row * ng + block * holders + k, pl.ds(run, 1), :]
                lines = jnp.where(sublane // columns == k, jnp.broadcast_to(line, (wanted, LANES)), lines)
            lines = jnp.where(own, lines, 0.0)
            total = lines
            for slot in range(1, columns):
                total = total + pltpu.roll(lines, LANES - slot * width, 1)
            gathered.append(total)
        weights.append(gathered)
    for distance, out_ref in enumerate(outs):
        acc = [jnp.zeros((wanted, LANES), jnp.float32) for _ in range(run)]
        for row in range(nrow):
            for r in range(ng):
                weight = jnp.broadcast_to(weights[distance][row][:, r : r + 1], (wanted, LANES))
                for y in range(run):
                    acc[y] = acc[y] + weight * got_ref[row * ng + r, pl.ds(y, 1), :]
        for y in range(run):
            out_ref[:, pl.ds(y * LANES, LANES)] = acc[y]


def sum_kernel(*refs):
    refs[-1][...] = functools.reduce(jnp.add, [ref[...] for ref in refs[:-1]])


def shards(nrow, cores, ng, orbitals, region, potential_table, counts, ritz):
    _, planes, ys, xs = orbitals.shape
    cells = planes * ys * xs
    panel, columns = ritz.shape
    run = cells // ng // xs
    width = 1
    while width < panel:
        width *= 2
    per_row = LANES // width
    ritz_rows = -(-columns // per_row)
    rows = -(-(run + ritz_rows) // SUBLANES) * SUBLANES
    tiles = nrow * ng
    vmem = pl.BlockSpec(memory_space=pltpu.VMEM)
    hbm = pl.BlockSpec(memory_space=pltpu.HBM)
    inputs = [
        pltpu.with_memory_space_constraint(value, pltpu.HBM)
        for value in (
            jnp.transpose(orbitals[0], (1, 0, 2)), jnp.transpose(region, (1, 0, 2)), ritz.T, potential_table, counts
        )
    ]
    packed_bytes = 4 * tiles * rows * LANES
    packed = pl.pallas_call(
        functools.partial(filter_kernel, ng, nrow, rows, run, width, cores),
        out_shape=jax.ShapeDtypeStruct((tiles * rows, LANES), jnp.float32),
        in_specs=[hbm] * 5,
        out_specs=vmem,
        scratch_shapes=[
            pltpu.VMEM((ys, planes, xs), jnp.float32),
            pltpu.VMEM((ys, planes, xs), jnp.int32),
            pltpu.VMEM((columns, panel), jnp.float32),
            pltpu.SMEM(potential_table.shape, jnp.float32),
            pltpu.SMEM(counts.shape, jnp.int32),
            pltpu.SemaphoreType.DMA((5,)),
        ],
        compiler_params=pltpu.CompilerParams(vmem_limit_bytes=packed_bytes + 32 * cells + 2**20),
        name="chebyshev_filter",
    )(*inputs)
    got = lax.all_to_all(
        packed.reshape(tiles, rows, LANES), ("row", "grid"), split_axis=0, concat_axis=0, tiled=True
    )
    sum_shape = jax.ShapeDtypeStruct((panel, run * LANES), jnp.float32)
    if columns * width <= LANES and tiles <= 64 and panel == ng and panel <= 16:
        sums = pl.pallas_call(
            functools.partial(partial_kernel, nrow, ng, run, width, columns, cores),
            out_shape=[sum_shape] * cores,
            in_specs=[vmem],
            out_specs=[vmem] * cores,
            compiler_params=pltpu.CompilerParams(vmem_limit_bytes=packed_bytes + 2**20),
            name="ritz_partial_sums",
        )(got)
    else:
        holders = panel // columns
        by_source = got.reshape(nrow, ng, rows, LANES)
        fields = by_source[:, :, :run].reshape(tiles, run * LANES)
        blocks = by_source[:, :, run : run + ritz_rows].reshape(nrow, ng, ritz_rows * per_row, width)
        sums = []
        for distance in range(cores):
            block = lax.axis_index("row") * cores + lax.rem(lax.axis_index("core") + distance, cores)
            mine = lax.dynamic_slice_in_dim(blocks, block * holders, holders, axis=1)
            weights = jnp.transpose(mine[:, :, :columns, :panel], (0, 3, 1, 2)).reshape(tiles, panel)
            sums.append(
                lax.dot_general(
                    weights,
                    fields,
                    (((0,), (0,)), ((), ())),
                    precision=lax.Precision.HIGHEST,
                    preferred_element_type=jnp.float32,
                )
            )
    terms = [sums[0]]
    for distance in range(1, cores):
        pairs = [(core, (core + distance) % cores) for core in range(cores)]
        terms.append(lax.ppermute(sums[distance], "core", pairs))
    return pl.pallas_call(
        sum_kernel,
        out_shape=sum_shape,
        in_specs=[vmem] * cores,
        out_specs=vmem,
        compiler_params=pltpu.CompilerParams(vmem_limit_bytes=4 * (cores + 1) * panel * run * LANES + 2**20),
        name="core_sum",
    )(*terms)


def solution(mesh):
    bands, ng = mesh.shape["band"], mesh.shape["grid"]
    cores = 2 if bands % 2 == 0 else 1
    nrow = bands // cores
    split = jax.sharding.Mesh(mesh.devices.reshape(nrow, cores, ng), ("row", "core", "grid"))
    return jax.shard_map(
        functools.partial(shards, nrow, cores, ng),
        mesh=split,
        in_specs=(P(("row", "core", "grid"), None, None, None), P(), P(), P(), P(("row", "core"), "grid")),
        out_specs=P(("row", "core"), "grid"),
        check_vma=False,
    )
```

```python
import functools

import jax
import jax.numpy as jnp
from jax import lax
from jax.experimental import pallas as pl
from jax.experimental.pallas import tpu as pltpu
from jax.sharding import PartitionSpec as P

DEGREE = 4

COEFFICIENTS = (
    -5369.0 / 1800.0,
    12.0 / 7.0,
    -15.0 / 56.0,
    10.0 / 189.0,
    -1.0 / 112.0,
    2.0 / 1925.0,
    -1.0 / 16632.0,
)
SPACING = 0.5
LOWER = 6.0
UPPER = 46.0
HALF = (UPPER - LOWER) / 2.0
CENTRE = (UPPER + LOWER) / 2.0
LANES = 128
SUBLANES = 8


def ring_weights(length):
    weights = [0.0] * length
    for offset in range(1, 7):
        weights[offset % length] += COEFFICIENTS[offset]
        weights[-offset % length] += COEFFICIENTS[offset]
    return weights


def pair_weights(length):
    weights = ring_weights(length)
    pairs = []
    for distance in range(1, length // 2 + 1):
        if weights[distance] != 0.0:
            pairs.append((sorted({distance, length - distance}), weights[distance]))
    return weights[0], pairs


def off_diagonal(field, planes, xs):
    ys = len(field)
    _, x_pairs = pair_weights(xs)
    _, y_pairs = pair_weights(ys)
    _, p_pairs = pair_weights(planes)
    results = []
    for y in range(ys):
        tile = field[y]
        total = None
        terms = []
        for shifts, weight in x_pairs:
            terms.append((weight, [pltpu.roll(tile, shift, 1) for shift in shifts]))
        for shifts, weight in p_pairs:
            terms.append((weight, [pltpu.roll(tile, shift, 0) for shift in shifts]))
        for shifts, weight in y_pairs:
            terms.append((weight, [field[(y - shift) % ys] for shift in shifts]))
        for weight, parts in terms:
            value = weight * functools.reduce(jnp.add, parts)
            total = value if total is None else total + value
        results.append(total)
    return results


def filter_kernel(ng, copies, rows, run, width, *refs):
    sources, out_ref, held, sems = refs[:5], refs[5], refs[6:11], refs[11]
    orb_ref, region_ref, ritz_ref, table_ref, counts_ref = held
    transfers = [
        pltpu.make_async_copy(source, target, sems.at[index])
        for index, (source, target) in enumerate(zip(sources, held))
    ]
    for transfer in transfers:
        transfer.start()
    for transfer in transfers:
        transfer.wait()
    ys, planes, xs = orb_ref.shape
    band_pos = lax.axis_index("band")
    live = (lax.axis_index("grid") < counts_ref[band_pos]).astype(jnp.float32)

    centre_weight = 3.0 * COEFFICIENTS[0] + sum(pair_weights(n)[0] for n in (planes, ys, xs))
    scale = 2.0 / HALF
    hop = -0.5 / (SPACING * SPACING) * scale
    diagonal = []
    for y in range(ys):
        region = region_ref[y]
        potential = jnp.zeros((planes, xs), jnp.float32)
        for index in range(table_ref.shape[0]):
            potential = jnp.where(region == index, table_ref[index], potential)
        diagonal.append(scale * potential + (hop * centre_weight - scale * CENTRE))

    def doubled(field):
        away = off_diagonal(field, planes, xs)
        return [diagonal[y] * field[y] + hop * away[y] for y in range(ys)]

    previous = [orb_ref[y] * live for y in range(ys)]
    current = [0.5 * value for value in doubled(previous)]
    for _ in range(DEGREE - 1):
        following = [value - before for value, before in zip(doubled(current), previous)]
        previous, current = current, following

    blocks = ys // run
    for copy in range(copies):
        for y in range(ys):
            start = (copy * ng + y // run) * rows + y % run
            out_ref[pl.ds(start, planes, stride=blocks * rows), :] = current[y]

    columns, panel = ritz_ref.shape
    per_row = LANES // width
    tiles = copies * ng
    for row in range(-(-columns // per_row)):
        line = jnp.zeros((1, LANES), jnp.float32)
        for slot in range(min(per_row, columns - row * per_row)):
            piece = jnp.concatenate(
                [ritz_ref[pl.ds(row * per_row + slot, 1), :], jnp.zeros((1, LANES - panel), jnp.float32)], axis=1
            )
            line = line + (pltpu.roll(piece, slot * width, 1) if slot else piece)
        out_ref[pl.ds(run + row, tiles, stride=rows), :] = jnp.broadcast_to(line, (tiles, LANES))


def start_kernel(packed_ref, out_ref):
    out_ref[...] = jnp.zeros_like(out_ref)


def rotate_kernel(nb, ng, run, width, columns, got_ref, start_ref, out_ref):
    wanted = out_ref.shape[0]
    holders = wanted // columns
    sublane = lax.broadcasted_iota(jnp.int32, (wanted, LANES), 0)
    lane = lax.broadcasted_iota(jnp.int32, (wanted, LANES), 1)
    own = lane // width == sublane % columns
    block = lax.axis_index("band")
    acc = [start_ref[:, pl.ds(y * LANES, LANES)] for y in range(run)]
    for b in range(nb):
        lines = jnp.zeros((wanted, LANES), jnp.float32)
        for k in range(holders):
            line = got_ref[b * ng + block * holders + k, pl.ds(run, 1), :]
            lines = jnp.where(sublane // columns == k, jnp.broadcast_to(line, (wanted, LANES)), lines)
        lines = jnp.where(own, lines, 0.0)
        gathered = lines
        for slot in range(1, columns):
            gathered = gathered + pltpu.roll(lines, LANES - slot * width, 1)
        for r in range(ng):
            weight = jnp.broadcast_to(gathered[:, r : r + 1], (wanted, LANES))
            for y in range(run):
                acc[y] = acc[y] + weight * got_ref[b * ng + r, pl.ds(y, 1), :]
    for y in range(run):
        out_ref[:, pl.ds(y * LANES, LANES)] = acc[y]


def shards(nb, ng, orbitals, region, potential_table, counts, ritz):
    _, planes, ys, xs = orbitals.shape
    cells = planes * ys * xs
    panel, columns = ritz.shape
    run = cells // ng // xs
    width = 1
    while width < panel:
        width *= 2
    per_row = LANES // width
    ritz_rows = -(-columns // per_row)
    rows = -(-(run + ritz_rows) // SUBLANES) * SUBLANES
    tiles = nb * ng
    vmem = pl.BlockSpec(memory_space=pltpu.VMEM)
    hbm = pl.BlockSpec(memory_space=pltpu.HBM)
    inputs = [
        pltpu.with_memory_space_constraint(value, pltpu.HBM)
        for value in (
            jnp.transpose(orbitals[0], (1, 0, 2)), jnp.transpose(region, (1, 0, 2)), ritz.T, potential_table, counts
        )
    ]
    packed_bytes = 4 * tiles * rows * LANES
    packed = pl.pallas_call(
        functools.partial(filter_kernel, ng, nb, rows, run, width),
        out_shape=jax.ShapeDtypeStruct((tiles * rows, LANES), jnp.float32),
        in_specs=[hbm] * 5,
        out_specs=vmem,
        scratch_shapes=[
            pltpu.VMEM((ys, planes, xs), jnp.float32),
            pltpu.VMEM((ys, planes, xs), jnp.int32),
            pltpu.VMEM((columns, panel), jnp.float32),
            pltpu.SMEM(potential_table.shape, jnp.float32),
            pltpu.SMEM(counts.shape, jnp.int32),
            pltpu.SemaphoreType.DMA((5,)),
        ],
        compiler_params=pltpu.CompilerParams(vmem_limit_bytes=packed_bytes + 32 * cells + 2**20),
        name="chebyshev_filter",
    )(*inputs)
    got = lax.all_to_all(
        packed.reshape(tiles, rows, LANES), ("band", "grid"), split_axis=0, concat_axis=0, tiled=True
    )
    if columns * width <= LANES and tiles <= 64 and panel == ng and panel <= 16:
        sum_shape = jax.ShapeDtypeStruct((panel, run * LANES), jnp.float32)
        limit = pltpu.CompilerParams(vmem_limit_bytes=packed_bytes + 2**20)
        start = pl.pallas_call(
            start_kernel,
            out_shape=sum_shape,
            in_specs=[pl.BlockSpec(memory_space=pl.ANY)],
            out_specs=vmem,
            compiler_params=limit,
            name="sums_start",
        )(packed)
        return pl.pallas_call(
            functools.partial(rotate_kernel, nb, ng, run, width, columns),
            out_shape=sum_shape,
            in_specs=[vmem] * 2,
            out_specs=vmem,
            compiler_params=limit,
            name="ritz_rotation",
        )(got, start)
    holders = panel // columns
    by_source = got.reshape(nb, ng, rows, LANES)
    blocks = by_source[:, :, run : run + ritz_rows].reshape(nb, ng, ritz_rows * per_row, width)
    mine = lax.dynamic_slice_in_dim(blocks, lax.axis_index("band") * holders, holders, axis=1)
    return lax.dot_general(
        jnp.transpose(mine[:, :, :columns, :panel], (0, 3, 1, 2)).reshape(tiles, panel),
        by_source[:, :, :run].reshape(tiles, run * LANES),
        (((0,), (0,)), ((), ())),
        precision=lax.Precision.HIGHEST,
        preferred_element_type=jnp.float32,
    )


def solution(mesh):
    return jax.shard_map(
        functools.partial(shards, mesh.shape["band"], mesh.shape["grid"]),
        mesh=mesh,
        in_specs=(P(("band", "grid"), None, None, None), P(), P(), P(), P("band", "grid")),
        out_specs=P("band", "grid"),
        check_vma=False,
    )
```

```python
import functools

import jax
import jax.numpy as jnp
from jax import lax
from jax.experimental import pallas as pl
from jax.experimental.pallas import tpu as pltpu
from jax.sharding import PartitionSpec as P

DEGREE = 4

COEFFICIENTS = (
    -5369.0 / 1800.0,
    12.0 / 7.0,
    -15.0 / 56.0,
    10.0 / 189.0,
    -1.0 / 112.0,
    2.0 / 1925.0,
    -1.0 / 16632.0,
)
SPACING = 0.5
LOWER = 6.0
UPPER = 46.0
HALF = (UPPER - LOWER) / 2.0
CENTRE = (UPPER + LOWER) / 2.0
LANES = 128
SUBLANES = 8


def ring_weights(length):
    weights = [0.0] * length
    for offset in range(1, 7):
        weights[offset % length] += COEFFICIENTS[offset]
        weights[-offset % length] += COEFFICIENTS[offset]
    return weights


def pair_weights(length):
    weights = ring_weights(length)
    pairs = []
    for distance in range(1, length // 2 + 1):
        if weights[distance] != 0.0:
            pairs.append((sorted({distance, length - distance}), weights[distance]))
    return weights[0], pairs


def off_diagonal(field, planes, xs):
    ys = len(field)
    _, x_pairs = pair_weights(xs)
    _, y_pairs = pair_weights(ys)
    _, p_pairs = pair_weights(planes)
    results = []
    for y in range(ys):
        tile = field[y]
        total = None
        terms = []
        for shifts, weight in x_pairs:
            terms.append((weight, [pltpu.roll(tile, shift, 1) for shift in shifts]))
        for shifts, weight in p_pairs:
            terms.append((weight, [pltpu.roll(tile, shift, 0) for shift in shifts]))
        for shifts, weight in y_pairs:
            terms.append((weight, [field[(y - shift) % ys] for shift in shifts]))
        for weight, parts in terms:
            value = weight * functools.reduce(jnp.add, parts)
            total = value if total is None else total + value
        results.append(total)
    return results


def filter_kernel(ng, copies, rows, run, width, *refs):
    sources, out_ref, held, sems, natural_ref = refs[:5], refs[5], refs[6:11], refs[11], refs[12]
    orb_ref, region_ref, ritz_ref, table_ref, counts_ref = held
    transfers = [
        pltpu.make_async_copy(source, target, sems.at[index])
        for index, (source, target) in enumerate(zip(sources, held))
    ]
    for transfer in transfers:
        transfer.start()
    for transfer in transfers:
        transfer.wait()
    ys, planes, xs = orb_ref.shape
    band_pos = lax.axis_index("band")
    live = (lax.axis_index("grid") < counts_ref[band_pos]).astype(jnp.float32)

    centre_weight = 3.0 * COEFFICIENTS[0] + sum(pair_weights(n)[0] for n in (planes, ys, xs))
    scale = 2.0 / HALF
    hop = -0.5 / (SPACING * SPACING) * scale
    diagonal = []
    for y in range(ys):
        region = region_ref[y]
        potential = jnp.zeros((planes, xs), jnp.float32)
        for index in range(table_ref.shape[0]):
            potential = jnp.where(region == index, table_ref[index], potential)
        diagonal.append(scale * potential + (hop * centre_weight - scale * CENTRE))

    def doubled(field):
        away = off_diagonal(field, planes, xs)
        return [diagonal[y] * field[y] + hop * away[y] for y in range(ys)]

    previous = [orb_ref[y] * live for y in range(ys)]
    current = [0.5 * value for value in doubled(previous)]
    for _ in range(DEGREE - 1):
        following = [value - before for value, before in zip(doubled(current), previous)]
        previous, current = current, following

    blocks = ys // run
    for y in range(ys):
        natural_ref[pl.ds((y // run) * rows + y % run, planes, stride=blocks * rows), :] = current[y]

    columns, panel = ritz_ref.shape
    per_row = LANES // width
    for row in range(-(-columns // per_row)):
        line = jnp.zeros((1, LANES), jnp.float32)
        for slot in range(min(per_row, columns - row * per_row)):
            piece = jnp.concatenate(
                [ritz_ref[pl.ds(row * per_row + slot, 1), :], jnp.zeros((1, LANES - panel), jnp.float32)], axis=1
            )
            line = line + (pltpu.roll(piece, slot * width, 1) if slot else piece)
        natural_ref[pl.ds(run + row, ng, stride=rows), :] = jnp.broadcast_to(line, (ng, LANES))
    for copy in range(copies):
        for tile in range(ng):
            place = (copies - 1 - copy) * ng + ng - 1 - tile
            out_ref[pl.ds(place * rows, rows), :] = natural_ref[pl.ds(tile * rows, rows), :]


def rotate_kernel(nb, ng, run, width, columns, got_ref, out_ref):
    wanted = out_ref.shape[0]
    holders = wanted // columns
    sublane = lax.broadcasted_iota(jnp.int32, (wanted, LANES), 0)
    lane = lax.broadcasted_iota(jnp.int32, (wanted, LANES), 1)
    own = lane // width == sublane % columns
    block = lax.axis_index("band")
    acc = [jnp.zeros((wanted, LANES), jnp.float32) for _ in range(run)]
    last = nb * ng - 1
    for b in range(nb):
        lines = jnp.zeros((wanted, LANES), jnp.float32)
        for k in range(holders):
            line = got_ref[last - b * ng - block * holders - k, pl.ds(run, 1), :]
            lines = jnp.where(sublane // columns == k, jnp.broadcast_to(line, (wanted, LANES)), lines)
        lines = jnp.where(own, lines, 0.0)
        gathered = lines
        for slot in range(1, columns):
            gathered = gathered + pltpu.roll(lines, LANES - slot * width, 1)
        for r in range(ng):
            weight = jnp.broadcast_to(gathered[:, r : r + 1], (wanted, LANES))
            for y in range(run):
                acc[y] = acc[y] + weight * got_ref[last - b * ng - r, pl.ds(y, 1), :]
    for y in range(run):
        out_ref[:, pl.ds(y * LANES, LANES)] = acc[y]


def shards(nb, ng, orbitals, region, potential_table, counts, ritz):
    _, planes, ys, xs = orbitals.shape
    cells = planes * ys * xs
    panel, columns = ritz.shape
    run = cells // ng // xs
    width = 1
    while width < panel:
        width *= 2
    per_row = LANES // width
    ritz_rows = -(-columns // per_row)
    rows = -(-(run + ritz_rows) // SUBLANES) * SUBLANES
    tiles = nb * ng
    vmem = pl.BlockSpec(memory_space=pltpu.VMEM)
    hbm = pl.BlockSpec(memory_space=pltpu.HBM)
    inputs = [
        pltpu.with_memory_space_constraint(value, pltpu.HBM)
        for value in (
            jnp.transpose(orbitals[0], (1, 0, 2)), jnp.transpose(region, (1, 0, 2)), ritz.T, potential_table, counts
        )
    ]
    packed_bytes = 4 * tiles * rows * LANES
    packed = pl.pallas_call(
        functools.partial(filter_kernel, ng, nb, rows, run, width),
        out_shape=jax.ShapeDtypeStruct((tiles * rows, LANES), jnp.float32),
        in_specs=[hbm] * 5,
        out_specs=vmem,
        scratch_shapes=[
            pltpu.VMEM((ys, planes, xs), jnp.float32),
            pltpu.VMEM((ys, planes, xs), jnp.int32),
            pltpu.VMEM((columns, panel), jnp.float32),
            pltpu.SMEM(potential_table.shape, jnp.float32),
            pltpu.SMEM(counts.shape, jnp.int32),
            pltpu.SemaphoreType.DMA((5,)),
            pltpu.VMEM((ng * rows, LANES), jnp.float32),
        ],
        compiler_params=pltpu.CompilerParams(vmem_limit_bytes=packed_bytes + 32 * cells + 2**20),
        name="chebyshev_filter",
    )(*inputs)
    got = lax.all_to_all(
        packed.reshape(tiles, rows, LANES), ("band", "grid"), split_axis=0, concat_axis=0, tiled=True,
        axis_index_groups=[list(range(tiles))[::-1]],
    )
    if columns * width <= LANES and tiles <= 64 and panel == ng and panel <= 16:
        sum_shape = jax.ShapeDtypeStruct((panel, run * LANES), jnp.float32)
        limit = pltpu.CompilerParams(vmem_limit_bytes=packed_bytes + 2**20)
        return pl.pallas_call(
            functools.partial(rotate_kernel, nb, ng, run, width, columns),
            out_shape=sum_shape,
            in_specs=[vmem],
            out_specs=vmem,
            compiler_params=limit,
            name="ritz_rotation",
        )(got)
    holders = panel // columns
    by_source = got[::-1].reshape(nb, ng, rows, LANES)
    blocks = by_source[:, :, run : run + ritz_rows].reshape(nb, ng, ritz_rows * per_row, width)
    mine = lax.dynamic_slice_in_dim(blocks, lax.axis_index("band") * holders, holders, axis=1)
    return lax.dot_general(
        jnp.transpose(mine[:, :, :columns, :panel], (0, 3, 1, 2)).reshape(tiles, panel),
        by_source[:, :, :run].reshape(tiles, run * LANES),
        (((0,), (0,)), ((), ())),
        precision=lax.Precision.HIGHEST,
        preferred_element_type=jnp.float32,
    )


def solution(mesh):
    return jax.shard_map(
        functools.partial(shards, mesh.shape["band"], mesh.shape["grid"]),
        mesh=mesh,
        in_specs=(P(("band", "grid"), None, None, None), P(), P(), P(), P("band", "grid")),
        out_specs=P("band", "grid"),
        check_vma=False,
    )
```

```python
import functools

import jax
import jax.numpy as jnp
from jax import lax
from jax.experimental import pallas as pl
from jax.experimental.pallas import tpu as pltpu
from jax.sharding import PartitionSpec as P

DEGREE = 4

COEFFICIENTS = (
    -5369.0 / 1800.0,
    12.0 / 7.0,
    -15.0 / 56.0,
    10.0 / 189.0,
    -1.0 / 112.0,
    2.0 / 1925.0,
    -1.0 / 16632.0,
)
SPACING = 0.5
LOWER = 6.0
UPPER = 46.0
HALF = (UPPER - LOWER) / 2.0
CENTRE = (UPPER + LOWER) / 2.0
LANES = 128
SUBLANES = 8


def ring_weights(length):
    weights = [0.0] * length
    for offset in range(1, 7):
        weights[offset % length] += COEFFICIENTS[offset]
        weights[-offset % length] += COEFFICIENTS[offset]
    return weights


def pair_weights(length):
    weights = ring_weights(length)
    pairs = []
    for distance in range(1, length // 2 + 1):
        if weights[distance] != 0.0:
            pairs.append((sorted({distance, length - distance}), weights[distance]))
    return weights[0], pairs


def off_diagonal(field, planes, xs):
    ys = len(field)
    _, x_pairs = pair_weights(xs)
    _, y_pairs = pair_weights(ys)
    _, p_pairs = pair_weights(planes)
    results = []
    for y in range(ys):
        tile = field[y]
        total = None
        terms = []
        for shifts, weight in x_pairs:
            terms.append((weight, [pltpu.roll(tile, shift, 1) for shift in shifts]))
        for shifts, weight in p_pairs:
            terms.append((weight, [pltpu.roll(tile, shift, 0) for shift in shifts]))
        for shifts, weight in y_pairs:
            terms.append((weight, [field[(y - shift) % ys] for shift in shifts]))
        for weight, parts in terms:
            value = weight * functools.reduce(jnp.add, parts)
            total = value if total is None else total + value
        results.append(total)
    return results


def filter_kernel(ng, copies, rows, run, width, cores, *refs):
    sources, out_ref, held, sems, natural_ref = refs[:5], refs[5], refs[6:11], refs[11], refs[12]
    orb_ref, region_ref, ritz_ref, table_ref, counts_ref = held
    transfers = [
        pltpu.make_async_copy(source, target, sems.at[index])
        for index, (source, target) in enumerate(zip(sources, held))
    ]
    for transfer in transfers:
        transfer.start()
    for transfer in transfers:
        transfer.wait()
    ys, planes, xs = orb_ref.shape
    band_pos = lax.axis_index("row") * cores + lax.axis_index("core")
    live = (lax.axis_index("grid") < counts_ref[band_pos]).astype(jnp.float32)

    centre_weight = 3.0 * COEFFICIENTS[0] + sum(pair_weights(n)[0] for n in (planes, ys, xs))
    scale = 2.0 / HALF
    hop = -0.5 / (SPACING * SPACING) * scale
    diagonal = []
    for y in range(ys):
        region = region_ref[y]
        potential = jnp.zeros((planes, xs), jnp.float32)
        for index in range(table_ref.shape[0]):
            potential = jnp.where(region == index, table_ref[index], potential)
        diagonal.append(scale * potential + (hop * centre_weight - scale * CENTRE))

    def doubled(field):
        away = off_diagonal(field, planes, xs)
        return [diagonal[y] * field[y] + hop * away[y] for y in range(ys)]

    previous = [orb_ref[y] * live for y in range(ys)]
    current = [0.5 * value for value in doubled(previous)]
    for _ in range(DEGREE - 1):
        following = [value - before for value, before in zip(doubled(current), previous)]
        previous, current = current, following

    blocks = ys // run
    for y in range(ys):
        natural_ref[pl.ds((y // run) * rows + y % run, planes, stride=blocks * rows), :] = current[y]

    columns, panel = ritz_ref.shape
    per_row = LANES // width
    for row in range(-(-columns // per_row)):
        line = jnp.zeros((1, LANES), jnp.float32)
        for slot in range(min(per_row, columns - row * per_row)):
            piece = jnp.concatenate(
                [ritz_ref[pl.ds(row * per_row + slot, 1), :], jnp.zeros((1, LANES - panel), jnp.float32)], axis=1
            )
            line = line + (pltpu.roll(piece, slot * width, 1) if slot else piece)
        natural_ref[pl.ds(run + row, ng, stride=rows), :] = jnp.broadcast_to(line, (ng, LANES))
    for copy in range(copies):
        for tile in range(ng):
            place = (copies - 1 - copy) * ng + ng - 1 - tile
            out_ref[pl.ds(place * rows, rows), :] = natural_ref[pl.ds(tile * rows, rows), :]


def partial_kernel(nrow, ng, run, width, columns, cores, got_ref, *outs):
    wanted = outs[0].shape[0]
    last = nrow * ng - 1
    holders = wanted // columns
    sublane = lax.broadcasted_iota(jnp.int32, (wanted, LANES), 0)
    lane = lax.broadcasted_iota(jnp.int32, (wanted, LANES), 1)
    own = lane // width == sublane % columns
    weights = []
    for distance in range(cores):
        block = lax.axis_index("row") * cores + lax.rem(lax.axis_index("core") + distance, cores)
        gathered = []
        for row in range(nrow):
            lines = jnp.zeros((wanted, LANES), jnp.float32)
            for k in range(holders):
                line = got_ref[last - row * ng - block * holders - k, pl.ds(run, 1), :]
                lines = jnp.where(sublane // columns == k, jnp.broadcast_to(line, (wanted, LANES)), lines)
            lines = jnp.where(own, lines, 0.0)
            total = lines
            for slot in range(1, columns):
                total = total + pltpu.roll(lines, LANES - slot * width, 1)
            gathered.append(total)
        weights.append(gathered)
    for distance, out_ref in enumerate(outs):
        acc = [jnp.zeros((wanted, LANES), jnp.float32) for _ in range(run)]
        for row in range(nrow):
            for r in range(ng):
                weight = jnp.broadcast_to(weights[distance][row][:, r : r + 1], (wanted, LANES))
                for y in range(run):
                    acc[y] = acc[y] + weight * got_ref[last - row * ng - r, pl.ds(y, 1), :]
        for y in range(run):
            out_ref[:, pl.ds(y * LANES, LANES)] = acc[y]


def sum_kernel(*refs):
    refs[-1][...] = functools.reduce(jnp.add, [ref[...] for ref in refs[:-1]])


def shards(nrow, cores, ng, orbitals, region, potential_table, counts, ritz):
    _, planes, ys, xs = orbitals.shape
    cells = planes * ys * xs
    panel, columns = ritz.shape
    run = cells // ng // xs
    width = 1
    while width < panel:
        width *= 2
    per_row = LANES // width
    ritz_rows = -(-columns // per_row)
    rows = -(-(run + ritz_rows) // SUBLANES) * SUBLANES
    tiles = nrow * ng
    vmem = pl.BlockSpec(memory_space=pltpu.VMEM)
    hbm = pl.BlockSpec(memory_space=pltpu.HBM)
    inputs = [
        pltpu.with_memory_space_constraint(value, pltpu.HBM)
        for value in (
            jnp.transpose(orbitals[0], (1, 0, 2)), jnp.transpose(region, (1, 0, 2)), ritz.T, potential_table, counts
        )
    ]
    packed_bytes = 4 * tiles * rows * LANES
    packed = pl.pallas_call(
        functools.partial(filter_kernel, ng, nrow, rows, run, width, cores),
        out_shape=jax.ShapeDtypeStruct((tiles * rows, LANES), jnp.float32),
        in_specs=[hbm] * 5,
        out_specs=vmem,
        scratch_shapes=[
            pltpu.VMEM((ys, planes, xs), jnp.float32),
            pltpu.VMEM((ys, planes, xs), jnp.int32),
            pltpu.VMEM((columns, panel), jnp.float32),
            pltpu.SMEM(potential_table.shape, jnp.float32),
            pltpu.SMEM(counts.shape, jnp.int32),
            pltpu.SemaphoreType.DMA((5,)),
            pltpu.VMEM((ng * rows, LANES), jnp.float32),
        ],
        compiler_params=pltpu.CompilerParams(vmem_limit_bytes=packed_bytes + 32 * cells + 2**20),
        name="chebyshev_filter",
    )(*inputs)
    got = lax.all_to_all(
        packed.reshape(tiles, rows, LANES), ("row", "grid"), split_axis=0, concat_axis=0, tiled=True,
        axis_index_groups=[list(range(tiles))[::-1]],
    )
    sum_shape = jax.ShapeDtypeStruct((panel, run * LANES), jnp.float32)
    if columns * width <= LANES and tiles <= 64 and panel == ng and panel <= 16:
        sums = pl.pallas_call(
            functools.partial(partial_kernel, nrow, ng, run, width, columns, cores),
            out_shape=[sum_shape] * cores,
            in_specs=[vmem],
            out_specs=[vmem] * cores,
            compiler_params=pltpu.CompilerParams(vmem_limit_bytes=packed_bytes + 2**20),
            name="ritz_partial_sums",
        )(got)
    else:
        holders = panel // columns
        by_source = got[::-1].reshape(nrow, ng, rows, LANES)
        fields = by_source[:, :, :run].reshape(tiles, run * LANES)
        blocks = by_source[:, :, run : run + ritz_rows].reshape(nrow, ng, ritz_rows * per_row, width)
        sums = []
        for distance in range(cores):
            block = lax.axis_index("row") * cores + lax.rem(lax.axis_index("core") + distance, cores)
            mine = lax.dynamic_slice_in_dim(blocks, block * holders, holders, axis=1)
            weights = jnp.transpose(mine[:, :, :columns, :panel], (0, 3, 1, 2)).reshape(tiles, panel)
            sums.append(
                lax.dot_general(
                    weights,
                    fields,
                    (((0,), (0,)), ((), ())),
                    precision=lax.Precision.HIGHEST,
                    preferred_element_type=jnp.float32,
                )
            )
    terms = [sums[0]]
    for distance in range(1, cores):
        pairs = [(core, (core + distance) % cores) for core in range(cores)]
        terms.append(lax.ppermute(sums[distance], "core", pairs))
    return pl.pallas_call(
        sum_kernel,
        out_shape=sum_shape,
        in_specs=[vmem] * cores,
        out_specs=vmem,
        compiler_params=pltpu.CompilerParams(vmem_limit_bytes=4 * (cores + 1) * panel * run * LANES + 2**20),
        name="core_sum",
    )(*terms)


def solution(mesh):
    bands, ng = mesh.shape["band"], mesh.shape["grid"]
    cores = 2 if bands % 2 == 0 else 1
    nrow = bands // cores
    split = jax.sharding.Mesh(mesh.devices.reshape(nrow, cores, ng), ("row", "core", "grid"))
    return jax.shard_map(
        functools.partial(shards, nrow, cores, ng),
        mesh=split,
        in_specs=(P(("row", "core", "grid"), None, None, None), P(), P(), P(), P(("row", "core"), "grid")),
        out_specs=P(("row", "core"), "grid"),
        check_vma=False,
    )
```

```python
import functools

import jax
import jax.numpy as jnp
from jax import lax
from jax.experimental import pallas as pl
from jax.experimental.pallas import tpu as pltpu
from jax.sharding import PartitionSpec as P

DEGREE = 4

COEFFICIENTS = (
    -5369.0 / 1800.0,
    12.0 / 7.0,
    -15.0 / 56.0,
    10.0 / 189.0,
    -1.0 / 112.0,
    2.0 / 1925.0,
    -1.0 / 16632.0,
)
SPACING = 0.5
LOWER = 6.0
UPPER = 46.0
HALF = (UPPER - LOWER) / 2.0
CENTRE = (UPPER + LOWER) / 2.0
LANES = 128
SUBLANES = 8


def ring_weights(length):
    weights = [0.0] * length
    for offset in range(1, 7):
        weights[offset % length] += COEFFICIENTS[offset]
        weights[-offset % length] += COEFFICIENTS[offset]
    return weights


def pair_weights(length):
    weights = ring_weights(length)
    pairs = []
    for distance in range(1, length // 2 + 1):
        if weights[distance] != 0.0:
            pairs.append((sorted({distance, length - distance}), weights[distance]))
    return weights[0], pairs


def off_diagonal(field, planes, xs):
    ys = len(field)
    _, x_pairs = pair_weights(xs)
    _, y_pairs = pair_weights(ys)
    _, p_pairs = pair_weights(planes)
    results = []
    for y in range(ys):
        tile = field[y]
        total = None
        terms = []
        for shifts, weight in x_pairs:
            terms.append((weight, [pltpu.roll(tile, shift, 1) for shift in shifts]))
        for shifts, weight in p_pairs:
            terms.append((weight, [pltpu.roll(tile, shift, 0) for shift in shifts]))
        for shifts, weight in y_pairs:
            terms.append((weight, [field[(y - shift) % ys] for shift in shifts]))
        for weight, parts in terms:
            value = weight * functools.reduce(jnp.add, parts)
            total = value if total is None else total + value
        results.append(total)
    return results


def filter_kernel(ng, rows, run, width, *refs):
    sources, out_ref, held, sems, natural_ref = refs[:5], refs[5], refs[6:11], refs[11], refs[12]
    orb_ref, region_ref, ritz_ref, table_ref, counts_ref = held
    transfers = [
        pltpu.make_async_copy(source, target, sems.at[index])
        for index, (source, target) in enumerate(zip(sources, held))
    ]
    for transfer in transfers:
        transfer.start()
    for transfer in transfers:
        transfer.wait()
    ys, planes, xs = orb_ref.shape
    live = (lax.axis_index("grid") < counts_ref[lax.axis_index("band")]).astype(jnp.float32)

    centre_weight = 3.0 * COEFFICIENTS[0] + sum(pair_weights(n)[0] for n in (planes, ys, xs))
    scale = 2.0 / HALF
    hop = -0.5 / (SPACING * SPACING) * scale
    diagonal = []
    for y in range(ys):
        region = region_ref[y]
        potential = jnp.zeros((planes, xs), jnp.float32)
        for index in range(table_ref.shape[0]):
            potential = jnp.where(region == index, table_ref[index], potential)
        diagonal.append(scale * potential + (hop * centre_weight - scale * CENTRE))

    def doubled(field):
        away = off_diagonal(field, planes, xs)
        return [diagonal[y] * field[y] + hop * away[y] for y in range(ys)]

    previous = [orb_ref[y] * live for y in range(ys)]
    current = [0.5 * value for value in doubled(previous)]
    for _ in range(DEGREE - 1):
        following = [value - before for value, before in zip(doubled(current), previous)]
        previous, current = current, following

    blocks = ys // run
    for y in range(ys):
        natural_ref[pl.ds((y // run) * rows + y % run, planes, stride=blocks * rows), :] = current[y]

    columns, panel = ritz_ref.shape
    per_row = LANES // width
    for row in range(-(-columns // per_row)):
        line = jnp.zeros((1, LANES), jnp.float32)
        for slot in range(min(per_row, columns - row * per_row)):
            piece = jnp.concatenate(
                [ritz_ref[pl.ds(row * per_row + slot, 1), :], jnp.zeros((1, LANES - panel), jnp.float32)], axis=1
            )
            line = line + (pltpu.roll(piece, slot * width, 1) if slot else piece)
        natural_ref[pl.ds(run + row, ng, stride=rows), :] = jnp.broadcast_to(line, (ng, LANES))
    for tile in range(ng):
        out_ref[pl.ds((ng - 1 - tile) * rows, rows), :] = natural_ref[pl.ds(tile * rows, rows), :]


def partial_kernel(order, ng, run, width, columns, got_ref, out_ref):
    wanted = out_ref.shape[1]
    holders = wanted // columns
    sublane = lax.broadcasted_iota(jnp.int32, (wanted, LANES), 0)
    lane = lax.broadcasted_iota(jnp.int32, (wanted, LANES), 1)
    own = lane // width == sublane % columns
    for place, block in enumerate(order):
        lines = jnp.zeros((wanted, LANES), jnp.float32)
        for k in range(holders):
            line = got_ref[ng - 1 - block * holders - k, pl.ds(run, 1), :]
            lines = jnp.where(sublane // columns == k, jnp.broadcast_to(line, (wanted, LANES)), lines)
        lines = jnp.where(own, lines, 0.0)
        weights = lines
        for slot in range(1, columns):
            weights = weights + pltpu.roll(lines, LANES - slot * width, 1)
        acc = [jnp.zeros((wanted, LANES), jnp.float32) for _ in range(run)]
        for r in range(ng):
            weight = jnp.broadcast_to(weights[:, r : r + 1], (wanted, LANES))
            for y in range(run):
                acc[y] = acc[y] + weight * got_ref[ng - 1 - r, pl.ds(y, 1), :]
        for y in range(run):
            out_ref[place, :, pl.ds(y * LANES, LANES)] = acc[y]


def sum_kernel(parts_ref, out_ref):
    out_ref[...] = functools.reduce(jnp.add, [parts_ref[place] for place in range(parts_ref.shape[0])])


def shards(nb, ng, orbitals, region, potential_table, counts, ritz):
    _, planes, ys, xs = orbitals.shape
    cells = planes * ys * xs
    panel, columns = ritz.shape
    run = cells // ng // xs
    width = 1
    while width < panel:
        width *= 2
    per_row = LANES // width
    ritz_rows = -(-columns // per_row)
    rows = -(-(run + ritz_rows) // SUBLANES) * SUBLANES
    vmem = pl.BlockSpec(memory_space=pltpu.VMEM)
    hbm = pl.BlockSpec(memory_space=pltpu.HBM)
    inputs = [
        pltpu.with_memory_space_constraint(value, pltpu.HBM)
        for value in (
            jnp.transpose(orbitals[0], (1, 0, 2)), jnp.transpose(region, (1, 0, 2)), ritz.T, potential_table, counts
        )
    ]
    packed_bytes = 4 * ng * rows * LANES
    packed = pl.pallas_call(
        functools.partial(filter_kernel, ng, rows, run, width),
        out_shape=jax.ShapeDtypeStruct((ng * rows, LANES), jnp.float32),
        in_specs=[hbm] * 5,
        out_specs=vmem,
        scratch_shapes=[
            pltpu.VMEM((ys, planes, xs), jnp.float32),
            pltpu.VMEM((ys, planes, xs), jnp.int32),
            pltpu.VMEM((columns, panel), jnp.float32),
            pltpu.SMEM(potential_table.shape, jnp.float32),
            pltpu.SMEM(counts.shape, jnp.int32),
            pltpu.SemaphoreType.DMA((5,)),
            pltpu.VMEM((ng * rows, LANES), jnp.float32),
        ],
        compiler_params=pltpu.CompilerParams(vmem_limit_bytes=2 * packed_bytes + 64 * cells + 2**20),
        name="chebyshev_filter",
    )(*inputs)
    got = lax.all_to_all(
        packed.reshape(ng, rows, LANES), "grid", split_axis=0, concat_axis=0, tiled=True,
        axis_index_groups=[list(range(ng))[::-1]],
    )
    order = sorted(range(nb), key=lambda band: (-(band // 2), band % 2))
    parts_shape = (nb, panel, run * LANES)
    if columns * width <= LANES and panel == ng and panel <= 16 and nb <= 8:
        parts = pl.pallas_call(
            functools.partial(partial_kernel, order, ng, run, width, columns),
            out_shape=jax.ShapeDtypeStruct(parts_shape, jnp.float32),
            in_specs=[vmem],
            out_specs=vmem,
            compiler_params=pltpu.CompilerParams(vmem_limit_bytes=2**21),
            name="ritz_partial_sums",
        )(got)
    else:
        by_source = got[::-1]
        lines = by_source[:, run : run + ritz_rows].reshape(ng, ritz_rows * per_row, width)[:, :columns, :panel]
        weights = jnp.transpose(lines, (2, 0, 1)).reshape(panel, nb, panel)
        parts = lax.dot_general(
            weights[:, jnp.array(order)].reshape(panel, nb * panel),
            by_source[:, :run].reshape(ng, run * LANES),
            (((0,), (0,)), ((), ())),
            precision=lax.Precision.HIGHEST,
            preferred_element_type=jnp.float32,
        ).reshape(parts_shape)
    parts = lax.all_to_all(parts, "band", split_axis=0, concat_axis=0, tiled=True, axis_index_groups=[order])
    return pl.pallas_call(
        sum_kernel,
        out_shape=jax.ShapeDtypeStruct(parts_shape[1:], jnp.float32),
        in_specs=[vmem],
        out_specs=vmem,
        compiler_params=pltpu.CompilerParams(vmem_limit_bytes=4 * (nb + 1) * panel * run * LANES + 2**20),
        name="band_sum",
    )(parts)


def solution(mesh):
    return jax.shard_map(
        functools.partial(shards, mesh.shape["band"], mesh.shape["grid"]),
        mesh=mesh,
        in_specs=(P(("band", "grid"), None, None, None), P(), P(), P(), P("band", "grid")),
        out_specs=P("band", "grid"),
        check_vma=False,
    )
```

```python
import functools

import jax
import jax.numpy as jnp
from jax import lax
from jax.experimental import pallas as pl
from jax.experimental.pallas import tpu as pltpu
from jax.sharding import PartitionSpec as P

DEGREE = 4

COEFFICIENTS = (
    -5369.0 / 1800.0,
    12.0 / 7.0,
    -15.0 / 56.0,
    10.0 / 189.0,
    -1.0 / 112.0,
    2.0 / 1925.0,
    -1.0 / 16632.0,
)
SPACING = 0.5
LOWER = 6.0
UPPER = 46.0
HALF = (UPPER - LOWER) / 2.0
CENTRE = (UPPER + LOWER) / 2.0
LANES = 128
SUBLANES = 8


def ring_weights(length):
    weights = [0.0] * length
    for offset in range(1, 7):
        weights[offset % length] += COEFFICIENTS[offset]
        weights[-offset % length] += COEFFICIENTS[offset]
    return weights


def pair_weights(length):
    weights = ring_weights(length)
    pairs = []
    for distance in range(1, length // 2 + 1):
        if weights[distance] != 0.0:
            pairs.append((sorted({distance, length - distance}), weights[distance]))
    return weights[0], pairs


def off_diagonal(field, planes, xs):
    ys = len(field)
    _, x_pairs = pair_weights(xs)
    _, y_pairs = pair_weights(ys)
    _, p_pairs = pair_weights(planes)
    results = []
    for y in range(ys):
        tile = field[y]
        total = None
        terms = []
        for shifts, weight in x_pairs:
            terms.append((weight, [pltpu.roll(tile, shift, 1) for shift in shifts]))
        for shifts, weight in p_pairs:
            terms.append((weight, [pltpu.roll(tile, shift, 0) for shift in shifts]))
        for shifts, weight in y_pairs:
            terms.append((weight, [field[(y - shift) % ys] for shift in shifts]))
        for weight, parts in terms:
            value = weight * functools.reduce(jnp.add, parts)
            total = value if total is None else total + value
        results.append(total)
    return results


def filter_kernel(ng, copies, rows, run, width, cores, order, *refs):
    sources, out_ref, held, sems, natural_ref = refs[:5], refs[5], refs[6:11], refs[11], refs[12]
    orb_ref, region_ref, ritz_ref, table_ref, counts_ref = held
    transfers = [
        pltpu.make_async_copy(source, target, sems.at[index])
        for index, (source, target) in enumerate(zip(sources, held))
    ]
    for transfer in transfers:
        transfer.start()
    for transfer in transfers:
        transfer.wait()
    ys, planes, xs = orb_ref.shape
    band_pos = lax.axis_index("row") * cores + lax.axis_index("core")
    live = (lax.axis_index("grid") < counts_ref[band_pos]).astype(jnp.float32)

    centre_weight = 3.0 * COEFFICIENTS[0] + sum(pair_weights(n)[0] for n in (planes, ys, xs))
    scale = 2.0 / HALF
    hop = -0.5 / (SPACING * SPACING) * scale
    diagonal = []
    for y in range(ys):
        region = region_ref[y]
        potential = jnp.zeros((planes, xs), jnp.float32)
        for index in range(table_ref.shape[0]):
            potential = jnp.where(region == index, table_ref[index], potential)
        diagonal.append(scale * potential + (hop * centre_weight - scale * CENTRE))

    def doubled(field):
        away = off_diagonal(field, planes, xs)
        return [diagonal[y] * field[y] + hop * away[y] for y in range(ys)]

    previous = [orb_ref[y] * live for y in range(ys)]
    current = [0.5 * value for value in doubled(previous)]
    for _ in range(DEGREE - 1):
        following = [value - before for value, before in zip(doubled(current), previous)]
        previous, current = current, following

    blocks = ys // run
    for y in range(ys):
        natural_ref[pl.ds((y // run) * rows + y % run, planes, stride=blocks * rows), :] = current[y]

    columns, panel = ritz_ref.shape
    per_row = LANES // width
    for row in range(-(-columns // per_row)):
        line = jnp.zeros((1, LANES), jnp.float32)
        for slot in range(min(per_row, columns - row * per_row)):
            piece = jnp.concatenate(
                [ritz_ref[pl.ds(row * per_row + slot, 1), :], jnp.zeros((1, LANES - panel), jnp.float32)], axis=1
            )
            line = line + (pltpu.roll(piece, slot * width, 1) if slot else piece)
        natural_ref[pl.ds(run + row, ng, stride=rows), :] = jnp.broadcast_to(line, (ng, LANES))
    for copy in range(copies):
        for tile in range(ng):
            place = order.index(copy * ng + tile)
            out_ref[pl.ds(place * rows, rows), :] = natural_ref[pl.ds(tile * rows, rows), :]


def partial_kernel(nrow, ng, run, width, columns, cores, order, got_ref, *refs):
    outs, ritz_ref = refs[:-1], refs[-1]
    for place, source in enumerate(order):
        ritz_ref[source] = got_ref[place, pl.ds(run, 1), :]
    wanted = outs[0].shape[0]
    holders = wanted // columns
    sublane = lax.broadcasted_iota(jnp.int32, (wanted, LANES), 0)
    lane = lax.broadcasted_iota(jnp.int32, (wanted, LANES), 1)
    own = lane // width == sublane % columns
    weights = []
    for distance in range(cores):
        block = lax.axis_index("row") * cores + lax.rem(lax.axis_index("core") + distance, cores)
        gathered = []
        for row in range(nrow):
            lines = jnp.zeros((wanted, LANES), jnp.float32)
            for k in range(holders):
                line = ritz_ref[row * ng + block * holders + k]
                lines = jnp.where(sublane // columns == k, jnp.broadcast_to(line, (wanted, LANES)), lines)
            lines = jnp.where(own, lines, 0.0)
            total = lines
            for slot in range(1, columns):
                total = total + pltpu.roll(lines, LANES - slot * width, 1)
            gathered.append(total)
        weights.append(gathered)
    for distance, out_ref in enumerate(outs):
        acc = [jnp.zeros((wanted, LANES), jnp.float32) for _ in range(run)]
        for row in range(nrow):
            for r in range(ng):
                weight = jnp.broadcast_to(weights[distance][row][:, r : r + 1], (wanted, LANES))
                for y in range(run):
                    acc[y] = acc[y] + weight * got_ref[order.index(row * ng + r), pl.ds(y, 1), :]
        for y in range(run):
            out_ref[:, pl.ds(y * LANES, LANES)] = acc[y]


def sum_kernel(*refs):
    refs[-1][...] = functools.reduce(jnp.add, [ref[...] for ref in refs[:-1]])


def shards(nrow, cores, ng, orbitals, region, potential_table, counts, ritz):
    _, planes, ys, xs = orbitals.shape
    cells = planes * ys * xs
    panel, columns = ritz.shape
    run = cells // ng // xs
    width = 1
    while width < panel:
        width *= 2
    per_row = LANES // width
    ritz_rows = -(-columns // per_row)
    rows = -(-(run + ritz_rows) // SUBLANES) * SUBLANES
    tiles = nrow * ng
    vmem = pl.BlockSpec(memory_space=pltpu.VMEM)
    hbm = pl.BlockSpec(memory_space=pltpu.HBM)
    inputs = [
        pltpu.with_memory_space_constraint(value, pltpu.HBM)
        for value in (
            jnp.transpose(orbitals[0], (1, 0, 2)), jnp.transpose(region, (1, 0, 2)), ritz.T, potential_table, counts
        )
    ]
    late = sorted(range(tiles), key=lambda place: (place % ng // (ng // 2), place // ng, place % ng), reverse=True)
    order = [place for pair in zip(late, late[::-1]) for place in pair][:tiles]
    packed_bytes = 4 * tiles * rows * LANES
    packed = pl.pallas_call(
        functools.partial(filter_kernel, ng, nrow, rows, run, width, cores, order),
        out_shape=jax.ShapeDtypeStruct((tiles * rows, LANES), jnp.float32),
        in_specs=[hbm] * 5,
        out_specs=vmem,
        scratch_shapes=[
            pltpu.VMEM((ys, planes, xs), jnp.float32),
            pltpu.VMEM((ys, planes, xs), jnp.int32),
            pltpu.VMEM((columns, panel), jnp.float32),
            pltpu.SMEM(potential_table.shape, jnp.float32),
            pltpu.SMEM(counts.shape, jnp.int32),
            pltpu.SemaphoreType.DMA((5,)),
            pltpu.VMEM((ng * rows, LANES), jnp.float32),
        ],
        compiler_params=pltpu.CompilerParams(vmem_limit_bytes=2 * packed_bytes + 64 * cells + 2**20),
        name="chebyshev_filter",
    )(*inputs)
    got = lax.all_to_all(
        packed.reshape(tiles, rows, LANES), ("row", "grid"), split_axis=0, concat_axis=0, tiled=True,
        axis_index_groups=[order],
    )
    sum_shape = jax.ShapeDtypeStruct((panel, run * LANES), jnp.float32)
    if columns * width <= LANES and tiles <= 64 and panel == ng and panel <= 16:
        sums = pl.pallas_call(
            functools.partial(partial_kernel, nrow, ng, run, width, columns, cores, order),
            out_shape=[sum_shape] * cores,
            in_specs=[vmem],
            out_specs=[vmem] * cores,
            scratch_shapes=[pltpu.VMEM((tiles, 1, LANES), jnp.float32)],
            compiler_params=pltpu.CompilerParams(vmem_limit_bytes=packed_bytes + 2**20),
            name="ritz_partial_sums",
        )(got)
    else:
        holders = panel // columns
        by_source = got[jnp.argsort(jnp.array(order))].reshape(nrow, ng, rows, LANES)
        fields = by_source[:, :, :run].reshape(tiles, run * LANES)
        blocks = by_source[:, :, run : run + ritz_rows].reshape(nrow, ng, ritz_rows * per_row, width)
        sums = []
        for distance in range(cores):
            block = lax.axis_index("row") * cores + lax.rem(lax.axis_index("core") + distance, cores)
            mine = lax.dynamic_slice_in_dim(blocks, block * holders, holders, axis=1)
            weights = jnp.transpose(mine[:, :, :columns, :panel], (0, 3, 1, 2)).reshape(tiles, panel)
            sums.append(
                lax.dot_general(
                    weights,
                    fields,
                    (((0,), (0,)), ((), ())),
                    precision=lax.Precision.HIGHEST,
                    preferred_element_type=jnp.float32,
                )
            )
    terms = [sums[0]]
    for distance in range(1, cores):
        pairs = [(core, (core + distance) % cores) for core in range(cores)]
        terms.append(lax.ppermute(sums[distance], "core", pairs))
    return pl.pallas_call(
        sum_kernel,
        out_shape=sum_shape,
        in_specs=[vmem] * cores,
        out_specs=vmem,
        compiler_params=pltpu.CompilerParams(vmem_limit_bytes=4 * (cores + 1) * panel * run * LANES + 2**20),
        name="core_sum",
    )(*terms)


def solution(mesh):
    bands, ng = mesh.shape["band"], mesh.shape["grid"]
    cores = 2 if bands % 2 == 0 else 1
    nrow = bands // cores
    split = jax.sharding.Mesh(mesh.devices.reshape(nrow, cores, ng), ("row", "core", "grid"))
    return jax.shard_map(
        functools.partial(shards, nrow, cores, ng),
        mesh=split,
        in_specs=(P(("row", "core", "grid"), None, None, None), P(), P(), P(), P(("row", "core"), "grid")),
        out_specs=P(("row", "core"), "grid"),
        check_vma=False,
    )
```

```python
import functools

import jax
import jax.numpy as jnp
from jax import lax
from jax.experimental import pallas as pl
from jax.experimental.pallas import tpu as pltpu
from jax.sharding import PartitionSpec as P

DEGREE = 4

COEFFICIENTS = (
    -5369.0 / 1800.0,
    12.0 / 7.0,
    -15.0 / 56.0,
    10.0 / 189.0,
    -1.0 / 112.0,
    2.0 / 1925.0,
    -1.0 / 16632.0,
)
SPACING = 0.5
LOWER = 6.0
UPPER = 46.0
HALF = (UPPER - LOWER) / 2.0
CENTRE = (UPPER + LOWER) / 2.0
LANES = 128
SUBLANES = 8


def ring_weights(length):
    weights = [0.0] * length
    for offset in range(1, 7):
        weights[offset % length] += COEFFICIENTS[offset]
        weights[-offset % length] += COEFFICIENTS[offset]
    return weights


def pair_weights(length):
    weights = ring_weights(length)
    pairs = []
    for distance in range(1, length // 2 + 1):
        if weights[distance] != 0.0:
            pairs.append((sorted({distance, length - distance}), weights[distance]))
    return weights[0], pairs


def off_diagonal(field, planes, xs):
    ys = len(field)
    _, x_pairs = pair_weights(xs)
    _, y_pairs = pair_weights(ys)
    _, p_pairs = pair_weights(planes)
    results = []
    for y in range(ys):
        tile = field[y]
        total = None
        terms = []
        for shifts, weight in x_pairs:
            terms.append((weight, [pltpu.roll(tile, shift, 1) for shift in shifts]))
        for shifts, weight in p_pairs:
            terms.append((weight, [pltpu.roll(tile, shift, 0) for shift in shifts]))
        for shifts, weight in y_pairs:
            terms.append((weight, [field[(y - shift) % ys] for shift in shifts]))
        for weight, parts in terms:
            value = weight * functools.reduce(jnp.add, parts)
            total = value if total is None else total + value
        results.append(total)
    return results


def filter_kernel(ng, copies, rows, run, width, *refs):
    sources, out_ref, held, sems, natural_ref = refs[:5], refs[5], refs[6:11], refs[11], refs[12]
    orb_ref, region_ref, ritz_ref, table_ref, counts_ref = held
    transfers = [
        pltpu.make_async_copy(source, target, sems.at[index])
        for index, (source, target) in enumerate(zip(sources, held))
    ]
    for transfer in transfers:
        transfer.start()
    for transfer in transfers:
        transfer.wait()
    ys, planes, xs = orb_ref.shape
    band_pos = lax.axis_index("band")
    live = (lax.axis_index("grid") < counts_ref[band_pos]).astype(jnp.float32)

    centre_weight = 3.0 * COEFFICIENTS[0] + sum(pair_weights(n)[0] for n in (planes, ys, xs))
    scale = 2.0 / HALF
    hop = -0.5 / (SPACING * SPACING) * scale
    diagonal = []
    for y in range(ys):
        region = region_ref[y]
        potential = jnp.zeros((planes, xs), jnp.float32)
        for index in range(table_ref.shape[0]):
            potential = jnp.where(region == index, table_ref[index], potential)
        diagonal.append(scale * potential + (hop * centre_weight - scale * CENTRE))

    def doubled(field):
        away = off_diagonal(field, planes, xs)
        return [diagonal[y] * field[y] + hop * away[y] for y in range(ys)]

    previous = [orb_ref[y] * live for y in range(ys)]
    current = [0.5 * value for value in doubled(previous)]
    for _ in range(DEGREE - 1):
        following = [value - before for value, before in zip(doubled(current), previous)]
        previous, current = current, following

    blocks = ys // run
    for y in range(ys):
        natural_ref[pl.ds((y // run) * rows + y % run, planes, stride=blocks * rows), :] = current[y]

    columns, panel = ritz_ref.shape
    per_row = LANES // width
    for row in range(-(-columns // per_row)):
        line = jnp.zeros((1, LANES), jnp.float32)
        for slot in range(min(per_row, columns - row * per_row)):
            piece = jnp.concatenate(
                [ritz_ref[pl.ds(row * per_row + slot, 1), :], jnp.zeros((1, LANES - panel), jnp.float32)], axis=1
            )
            line = line + (pltpu.roll(piece, slot * width, 1) if slot else piece)
        natural_ref[pl.ds(run + row, ng, stride=rows), :] = jnp.broadcast_to(line, (ng, LANES))
    for copy in range(copies):
        for tile in range(ng):
            place = (copies - 1 - copy) * ng + ng - 1 - tile
            out_ref[pl.ds(place * rows, rows), :] = natural_ref[pl.ds(tile * rows, rows), :]


def start_kernel(packed_ref, out_ref):
    out_ref[...] = jnp.zeros_like(out_ref)


def rotate_kernel(nb, ng, run, width, columns, got_ref, start_ref, out_ref):
    wanted = out_ref.shape[0]
    holders = wanted // columns
    sublane = lax.broadcasted_iota(jnp.int32, (wanted, LANES), 0)
    lane = lax.broadcasted_iota(jnp.int32, (wanted, LANES), 1)
    own = lane // width == sublane % columns
    block = lax.axis_index("band")
    acc = [start_ref[:, pl.ds(y * LANES, LANES)] for y in range(run)]
    last = nb * ng - 1
    for b in range(nb):
        lines = jnp.zeros((wanted, LANES), jnp.float32)
        for k in range(holders):
            line = got_ref[last - b * ng - block * holders - k, pl.ds(run, 1), :]
            lines = jnp.where(sublane // columns == k, jnp.broadcast_to(line, (wanted, LANES)), lines)
        lines = jnp.where(own, lines, 0.0)
        gathered = lines
        for slot in range(1, columns):
            gathered = gathered + pltpu.roll(lines, LANES - slot * width, 1)
        for r in range(ng):
            weight = jnp.broadcast_to(gathered[:, r : r + 1], (wanted, LANES))
            for y in range(run):
                acc[y] = acc[y] + weight * got_ref[last - b * ng - r, pl.ds(y, 1), :]
    for y in range(run):
        out_ref[:, pl.ds(y * LANES, LANES)] = acc[y]


def shards(nb, ng, orbitals, region, potential_table, counts, ritz):
    _, planes, ys, xs = orbitals.shape
    cells = planes * ys * xs
    panel, columns = ritz.shape
    run = cells // ng // xs
    width = 1
    while width < panel:
        width *= 2
    per_row = LANES // width
    ritz_rows = -(-columns // per_row)
    rows = -(-(run + ritz_rows) // SUBLANES) * SUBLANES
    tiles = nb * ng
    vmem = pl.BlockSpec(memory_space=pltpu.VMEM)
    hbm = pl.BlockSpec(memory_space=pltpu.HBM)
    inputs = [
        pltpu.with_memory_space_constraint(value, pltpu.HBM)
        for value in (
            jnp.transpose(orbitals[0], (1, 0, 2)), jnp.transpose(region, (1, 0, 2)), ritz.T, potential_table, counts
        )
    ]
    packed_bytes = 4 * tiles * rows * LANES
    packed = pl.pallas_call(
        functools.partial(filter_kernel, ng, nb, rows, run, width),
        out_shape=jax.ShapeDtypeStruct((tiles * rows, LANES), jnp.float32),
        in_specs=[hbm] * 5,
        out_specs=vmem,
        scratch_shapes=[
            pltpu.VMEM((ys, planes, xs), jnp.float32),
            pltpu.VMEM((ys, planes, xs), jnp.int32),
            pltpu.VMEM((columns, panel), jnp.float32),
            pltpu.SMEM(potential_table.shape, jnp.float32),
            pltpu.SMEM(counts.shape, jnp.int32),
            pltpu.SemaphoreType.DMA((5,)),
            pltpu.VMEM((ng * rows, LANES), jnp.float32),
        ],
        compiler_params=pltpu.CompilerParams(vmem_limit_bytes=packed_bytes + 32 * cells + 2**20),
        name="chebyshev_filter",
    )(*inputs)
    got = lax.all_to_all(
        packed.reshape(tiles, rows, LANES), ("band", "grid"), split_axis=0, concat_axis=0, tiled=True,
        axis_index_groups=[list(range(tiles))[::-1]],
    )
    if columns * width <= LANES and tiles <= 64 and panel == ng and panel <= 16:
        sum_shape = jax.ShapeDtypeStruct((panel, run * LANES), jnp.float32)
        limit = pltpu.CompilerParams(vmem_limit_bytes=packed_bytes + 2**20)
        start = pl.pallas_call(
            start_kernel,
            out_shape=sum_shape,
            in_specs=[pl.BlockSpec(memory_space=pl.ANY)],
            out_specs=vmem,
            compiler_params=limit,
            name="sums_start",
        )(packed)
        return pl.pallas_call(
            functools.partial(rotate_kernel, nb, ng, run, width, columns),
            out_shape=sum_shape,
            in_specs=[vmem] * 2,
            out_specs=vmem,
            compiler_params=limit,
            name="ritz_rotation",
        )(got, start)
    holders = panel // columns
    by_source = got[::-1].reshape(nb, ng, rows, LANES)
    blocks = by_source[:, :, run : run + ritz_rows].reshape(nb, ng, ritz_rows * per_row, width)
    mine = lax.dynamic_slice_in_dim(blocks, lax.axis_index("band") * holders, holders, axis=1)
    return lax.dot_general(
        jnp.transpose(mine[:, :, :columns, :panel], (0, 3, 1, 2)).reshape(tiles, panel),
        by_source[:, :, :run].reshape(tiles, run * LANES),
        (((0,), (0,)), ((), ())),
        precision=lax.Precision.HIGHEST,
        preferred_element_type=jnp.float32,
    )


def solution(mesh):
    return jax.shard_map(
        functools.partial(shards, mesh.shape["band"], mesh.shape["grid"]),
        mesh=mesh,
        in_specs=(P(("band", "grid"), None, None, None), P(), P(), P(), P("band", "grid")),
        out_specs=P("band", "grid"),
        check_vma=False,
    )
```

```python
import functools

import jax
import jax.numpy as jnp
from jax import lax
from jax.experimental import pallas as pl
from jax.experimental.pallas import tpu as pltpu
from jax.sharding import PartitionSpec as P

DEGREE = 4

COEFFICIENTS = (
    -5369.0 / 1800.0,
    12.0 / 7.0,
    -15.0 / 56.0,
    10.0 / 189.0,
    -1.0 / 112.0,
    2.0 / 1925.0,
    -1.0 / 16632.0,
)
SPACING = 0.5
LOWER = 6.0
UPPER = 46.0
HALF = (UPPER - LOWER) / 2.0
CENTRE = (UPPER + LOWER) / 2.0
LANES = 128
SUBLANES = 8


def ring_weights(length):
    weights = [0.0] * length
    for offset in range(1, 7):
        weights[offset % length] += COEFFICIENTS[offset]
        weights[-offset % length] += COEFFICIENTS[offset]
    return weights


def pair_weights(length):
    weights = ring_weights(length)
    pairs = []
    for distance in range(1, length // 2 + 1):
        if weights[distance] != 0.0:
            pairs.append((sorted({distance, length - distance}), weights[distance]))
    return weights[0], pairs


def off_diagonal(field, planes, xs):
    ys = len(field)
    _, x_pairs = pair_weights(xs)
    _, y_pairs = pair_weights(ys)
    _, p_pairs = pair_weights(planes)
    results = []
    for y in range(ys):
        tile = field[y]
        total = None
        terms = []
        for shifts, weight in x_pairs:
            terms.append((weight, [pltpu.roll(tile, shift, 1) for shift in shifts]))
        for shifts, weight in p_pairs:
            terms.append((weight, [pltpu.roll(tile, shift, 0) for shift in shifts]))
        for shifts, weight in y_pairs:
            terms.append((weight, [field[(y - shift) % ys] for shift in shifts]))
        for weight, parts in terms:
            value = weight * functools.reduce(jnp.add, parts)
            total = value if total is None else total + value
        results.append(total)
    return results


def filter_kernel(ng, copies, rows, run, width, cores, *refs):
    sources, out_ref, held, sems = refs[:5], refs[5], refs[6:11], refs[11]
    orb_ref, region_ref, table_ref, counts_ref, ritz_ref = held
    transfers = [
        pltpu.make_async_copy(source, target, sems.at[index])
        for index, (source, target) in enumerate(zip(sources, held))
    ]
    for transfer in transfers:
        transfer.start()
    ys, planes, xs = orb_ref.shape
    centre_weight = 3.0 * COEFFICIENTS[0] + sum(pair_weights(n)[0] for n in (planes, ys, xs))
    scale = 2.0 / HALF
    hop = -0.5 / (SPACING * SPACING) * scale

    def doubled(field, away):
        return [diagonal[y] * field[y] + hop * away[y] for y in range(ys)]

    transfers[0].wait()
    previous = [orb_ref[y] for y in range(ys)]
    away = off_diagonal(previous, planes, xs)
    transfers[1].wait()
    transfers[2].wait()
    diagonal = []
    for y in range(ys):
        region = region_ref[y]
        potential = jnp.zeros((planes, xs), jnp.float32)
        for index in range(table_ref.shape[0]):
            potential = jnp.where(region == index, table_ref[index], potential)
        diagonal.append(scale * potential + (hop * centre_weight - scale * CENTRE))
    current = [0.5 * value for value in doubled(previous, away)]
    for _ in range(DEGREE - 1):
        away = off_diagonal(current, planes, xs)
        following = [value - before for value, before in zip(doubled(current, away), previous)]
        previous, current = current, following
    transfers[3].wait()
    transfers[4].wait()
    band_pos = lax.axis_index("row") * cores + lax.axis_index("core")
    live = (lax.axis_index("grid") < counts_ref[band_pos]).astype(jnp.float32)

    blocks = ys // run
    for y in range(ys):
        masked = current[y] * live
        for copy in range(copies):
            first = copy * ng + y // run + 1
            count = planes if copy < copies - 1 or y // run < blocks - 1 else planes - 1
            out_ref[pl.ds(first * rows + y % run, count, stride=blocks * rows), :] = masked[:count]
            if count < planes:
                out_ref[pl.ds(y % run, 1), :] = masked[count:]

    columns, panel = ritz_ref.shape
    per_row = LANES // width
    for row in range(-(-columns // per_row)):
        line = jnp.zeros((1, LANES), jnp.float32)
        for slot in range(min(per_row, columns - row * per_row)):
            piece = jnp.concatenate(
                [ritz_ref[pl.ds(row * per_row + slot, 1), :], jnp.zeros((1, LANES - panel), jnp.float32)], axis=1
            )
            line = line + (pltpu.roll(piece, slot * width, 1) if slot else piece)
        out_ref[pl.ds(run + row, copies * ng, stride=rows), :] = jnp.broadcast_to(line, (copies * ng, LANES))


def partial_kernel(nrow, ng, run, width, columns, cores, order, distance, got_ref, out_ref, ritz_ref):
    for place, source in enumerate(order):
        ritz_ref[source] = got_ref[place, pl.ds(run, 1), :]
    wanted = out_ref.shape[0]
    holders = wanted // columns
    sublane = lax.broadcasted_iota(jnp.int32, (wanted, LANES), 0)
    lane = lax.broadcasted_iota(jnp.int32, (wanted, LANES), 1)
    own = lane // width == sublane % columns
    block = lax.axis_index("row") * cores + lax.rem(lax.axis_index("core") + distance, cores)
    acc = [jnp.zeros((wanted, LANES), jnp.float32) for _ in range(run)]
    for row in range(nrow):
        lines = jnp.zeros((wanted, LANES), jnp.float32)
        for k in range(holders):
            line = ritz_ref[row * ng + block * holders + k]
            lines = jnp.where(sublane // columns == k, jnp.broadcast_to(line, (wanted, LANES)), lines)
        lines = jnp.where(own, lines, 0.0)
        weights = lines
        for slot in range(1, columns):
            weights = weights + pltpu.roll(lines, LANES - slot * width, 1)
        for r in range(ng):
            weight = jnp.broadcast_to(weights[:, r : r + 1], (wanted, LANES))
            for y in range(run):
                acc[y] = acc[y] + weight * got_ref[order.index(row * ng + r), pl.ds(y, 1), :]
    for y in range(run):
        out_ref[:, pl.ds(y * LANES, LANES)] = acc[y]


def sum_kernel(*refs):
    refs[-1][...] = functools.reduce(jnp.add, [ref[...] for ref in refs[:-1]])


def shards(nrow, cores, ng, orbitals, region, potential_table, counts, ritz):
    _, planes, ys, xs = orbitals.shape
    cells = planes * ys * xs
    panel, columns = ritz.shape
    run = cells // ng // xs
    width = 1
    while width < panel:
        width *= 2
    per_row = LANES // width
    ritz_rows = -(-columns // per_row)
    rows = -(-(run + ritz_rows) // SUBLANES) * SUBLANES
    tiles = nrow * ng
    vmem = pl.BlockSpec(memory_space=pltpu.VMEM)
    hbm = pl.BlockSpec(memory_space=pltpu.HBM)
    inputs = [
        pltpu.with_memory_space_constraint(value, pltpu.HBM)
        for value in (
            jnp.transpose(orbitals[0], (1, 0, 2)), jnp.transpose(region, (1, 0, 2)), potential_table, counts, ritz.T
        )
    ]
    order = [tiles - 1] + list(range(tiles - 1))
    packed_bytes = 4 * tiles * rows * LANES
    packed = pl.pallas_call(
        functools.partial(filter_kernel, ng, nrow, rows, run, width, cores),
        out_shape=jax.ShapeDtypeStruct((tiles * rows, LANES), jnp.float32),
        in_specs=[hbm] * 5,
        out_specs=vmem,
        scratch_shapes=[
            pltpu.VMEM((ys, planes, xs), jnp.float32),
            pltpu.VMEM((ys, planes, xs), jnp.int32),
            pltpu.SMEM(potential_table.shape, jnp.float32),
            pltpu.SMEM(counts.shape, jnp.int32),
            pltpu.VMEM((columns, panel), jnp.float32),
            pltpu.SemaphoreType.DMA((5,)),
        ],
        compiler_params=pltpu.CompilerParams(vmem_limit_bytes=2 * packed_bytes + 64 * cells + 2**20),
        name="chebyshev_filter",
    )(*inputs)
    got = lax.all_to_all(
        packed.reshape(tiles, rows, LANES), ("row", "grid"), split_axis=0, concat_axis=0, tiled=True,
        axis_index_groups=[order],
    )
    sum_shape = jax.ShapeDtypeStruct((panel, run * LANES), jnp.float32)
    if columns * width <= LANES and tiles <= 64 and panel == ng and panel <= 16:
        def partial_sums(distance):
            return pl.pallas_call(
                functools.partial(partial_kernel, nrow, ng, run, width, columns, cores, order, distance),
                out_shape=sum_shape,
                in_specs=[vmem],
                out_specs=vmem,
                scratch_shapes=[pltpu.VMEM((tiles, 1, LANES), jnp.float32)],
                compiler_params=pltpu.CompilerParams(vmem_limit_bytes=packed_bytes + 2**20),
                name="ritz_partial_sums",
            )(got)

    else:
        holders = panel // columns
        by_source = got[jnp.argsort(jnp.array(order))].reshape(nrow, ng, rows, LANES)
        fields = by_source[:, :, :run].reshape(tiles, run * LANES)
        blocks = by_source[:, :, run : run + ritz_rows].reshape(nrow, ng, ritz_rows * per_row, width)

        def partial_sums(distance):
            block = lax.axis_index("row") * cores + lax.rem(lax.axis_index("core") + distance, cores)
            mine = lax.dynamic_slice_in_dim(blocks, block * holders, holders, axis=1)
            return lax.dot_general(
                jnp.transpose(mine[:, :, :columns, :panel], (0, 3, 1, 2)).reshape(tiles, panel),
                fields,
                (((0,), (0,)), ((), ())),
                precision=lax.Precision.HIGHEST,
                preferred_element_type=jnp.float32,
            )

    terms = []
    for distance in range(1, cores):
        pairs = [(core, (core + distance) % cores) for core in range(cores)]
        terms.append(lax.ppermute(partial_sums(distance), "core", pairs))
    terms.append(partial_sums(0))
    return pl.pallas_call(
        sum_kernel,
        out_shape=sum_shape,
        in_specs=[vmem] * cores,
        out_specs=vmem,
        compiler_params=pltpu.CompilerParams(vmem_limit_bytes=4 * (cores + 1) * panel * run * LANES + 2**20),
        name="core_sum",
    )(*terms)


def solution(mesh):
    bands, ng = mesh.shape["band"], mesh.shape["grid"]
    cores = 2 if bands % 2 == 0 else 1
    nrow = bands // cores
    split = jax.sharding.Mesh(mesh.devices.reshape(nrow, cores, ng), ("row", "core", "grid"))
    return jax.shard_map(
        functools.partial(shards, nrow, cores, ng),
        mesh=split,
        in_specs=(P(("row", "core", "grid"), None, None, None), P(), P(), P(), P(("row", "core"), "grid")),
        out_specs=P(("row", "core"), "grid"),
        check_vma=False,
    )
```

```python
import functools

import jax
import jax.numpy as jnp
from jax import lax
from jax.experimental import pallas as pl
from jax.experimental.pallas import tpu as pltpu
from jax.sharding import PartitionSpec as P

DEGREE = 4

COEFFICIENTS = (
    -5369.0 / 1800.0,
    12.0 / 7.0,
    -15.0 / 56.0,
    10.0 / 189.0,
    -1.0 / 112.0,
    2.0 / 1925.0,
    -1.0 / 16632.0,
)
SPACING = 0.5
LOWER = 6.0
UPPER = 46.0
HALF = (UPPER - LOWER) / 2.0
CENTRE = (UPPER + LOWER) / 2.0
LANES = 128
SUBLANES = 8


def ring_weights(length):
    weights = [0.0] * length
    for offset in range(1, 7):
        weights[offset % length] += COEFFICIENTS[offset]
        weights[-offset % length] += COEFFICIENTS[offset]
    return weights


def pair_weights(length):
    weights = ring_weights(length)
    pairs = []
    for distance in range(1, length // 2 + 1):
        if weights[distance] != 0.0:
            pairs.append((sorted({distance, length - distance}), weights[distance]))
    return weights[0], pairs


def off_diagonal(field, planes, xs):
    ys = len(field)
    _, x_pairs = pair_weights(xs)
    _, y_pairs = pair_weights(ys)
    _, p_pairs = pair_weights(planes)
    results = []
    for y in range(ys):
        tile = field[y]
        total = None
        terms = []
        for shifts, weight in x_pairs:
            terms.append((weight, [pltpu.roll(tile, shift, 1) for shift in shifts]))
        for shifts, weight in p_pairs:
            terms.append((weight, [pltpu.roll(tile, shift, 0) for shift in shifts]))
        for shifts, weight in y_pairs:
            terms.append((weight, [field[(y - shift) % ys] for shift in shifts]))
        for weight, parts in terms:
            value = weight * functools.reduce(jnp.add, parts)
            total = value if total is None else total + value
        results.append(total)
    return results


def filter_kernel(ng, copies, rows, run, width, cores, order, *refs):
    sources, out_ref, held, sems, natural_ref = refs[:5], refs[5], refs[6:11], refs[11], refs[12]
    orb_ref, region_ref, ritz_ref, table_ref, counts_ref = held
    transfers = [
        pltpu.make_async_copy(source, target, sems.at[index])
        for index, (source, target) in enumerate(zip(sources, held))
    ]
    for transfer in transfers:
        transfer.start()
    for transfer in transfers:
        transfer.wait()
    ys, planes, xs = orb_ref.shape
    band_pos = lax.axis_index("row") * cores + lax.axis_index("core")
    live = (lax.axis_index("grid") < counts_ref[band_pos]).astype(jnp.float32)

    centre_weight = 3.0 * COEFFICIENTS[0] + sum(pair_weights(n)[0] for n in (planes, ys, xs))
    scale = 2.0 / HALF
    hop = -0.5 / (SPACING * SPACING) * scale
    diagonal = []
    for y in range(ys):
        region = region_ref[y]
        potential = jnp.zeros((planes, xs), jnp.float32)
        for index in range(table_ref.shape[0]):
            potential = jnp.where(region == index, table_ref[index], potential)
        diagonal.append(scale * potential + (hop * centre_weight - scale * CENTRE))

    def doubled(field):
        away = off_diagonal(field, planes, xs)
        return [diagonal[y] * field[y] + hop * away[y] for y in range(ys)]

    previous = [orb_ref[y] * live for y in range(ys)]
    current = [0.5 * value for value in doubled(previous)]
    for _ in range(DEGREE - 1):
        following = [value - before for value, before in zip(doubled(current), previous)]
        previous, current = current, following

    blocks = ys // run
    for y in range(ys):
        natural_ref[pl.ds((y // run) * rows + y % run, planes, stride=blocks * rows), :] = current[y]

    columns, panel = ritz_ref.shape
    per_row = LANES // width
    for row in range(-(-columns // per_row)):
        line = jnp.zeros((1, LANES), jnp.float32)
        for slot in range(min(per_row, columns - row * per_row)):
            piece = jnp.concatenate(
                [ritz_ref[pl.ds(row * per_row + slot, 1), :], jnp.zeros((1, LANES - panel), jnp.float32)], axis=1
            )
            line = line + (pltpu.roll(piece, slot * width, 1) if slot else piece)
        natural_ref[pl.ds(run + row, ng, stride=rows), :] = jnp.broadcast_to(line, (ng, LANES))
    for copy in range(copies):
        for tile in range(ng):
            place = order.index(copy * ng + tile)
            out_ref[pl.ds(place * rows, rows), :] = natural_ref[pl.ds(tile * rows, rows), :]


def partial_kernel(nrow, ng, run, width, columns, cores, order, distance, got_ref, out_ref, ritz_ref):
    for place, source in enumerate(order):
        ritz_ref[source] = got_ref[place, pl.ds(run, 1), :]
    wanted = out_ref.shape[0]
    holders = wanted // columns
    sublane = lax.broadcasted_iota(jnp.int32, (wanted, LANES), 0)
    lane = lax.broadcasted_iota(jnp.int32, (wanted, LANES), 1)
    own = lane // width == sublane % columns
    block = lax.axis_index("row") * cores + lax.rem(lax.axis_index("core") + distance, cores)
    acc = [jnp.zeros((wanted, LANES), jnp.float32) for _ in range(run)]
    for row in range(nrow):
        lines = jnp.zeros((wanted, LANES), jnp.float32)
        for k in range(holders):
            line = ritz_ref[row * ng + block * holders + k]
            lines = jnp.where(sublane // columns == k, jnp.broadcast_to(line, (wanted, LANES)), lines)
        lines = jnp.where(own, lines, 0.0)
        weights = lines
        for slot in range(1, columns):
            weights = weights + pltpu.roll(lines, LANES - slot * width, 1)
        for r in range(ng):
            weight = jnp.broadcast_to(weights[:, r : r + 1], (wanted, LANES))
            for y in range(run):
                acc[y] = acc[y] + weight * got_ref[order.index(row * ng + r), pl.ds(y, 1), :]
    for y in range(run):
        out_ref[:, pl.ds(y * LANES, LANES)] = acc[y]


def sum_kernel(*refs):
    refs[-1][...] = functools.reduce(jnp.add, [ref[...] for ref in refs[:-1]])


def shards(nrow, cores, ng, orbitals, region, potential_table, counts, ritz):
    _, planes, ys, xs = orbitals.shape
    cells = planes * ys * xs
    panel, columns = ritz.shape
    run = cells // ng // xs
    width = 1
    while width < panel:
        width *= 2
    per_row = LANES // width
    ritz_rows = -(-columns // per_row)
    rows = -(-(run + ritz_rows) // SUBLANES) * SUBLANES
    tiles = nrow * ng
    vmem = pl.BlockSpec(memory_space=pltpu.VMEM)
    hbm = pl.BlockSpec(memory_space=pltpu.HBM)
    inputs = [
        pltpu.with_memory_space_constraint(value, pltpu.HBM)
        for value in (
            jnp.transpose(orbitals[0], (1, 0, 2)), jnp.transpose(region, (1, 0, 2)), ritz.T, potential_table, counts
        )
    ]
    others = sorted(range(1, tiles - 1), key=lambda chip: (chip % ng // 2, chip), reverse=True)
    order = [tiles - 1, 0] + others
    groups = [
        [(chip // ng * cores + (group + chip // ng) % cores) * ng + chip % ng for chip in order] for group in range(cores)
    ]
    packed_bytes = 4 * tiles * rows * LANES
    packed = pl.pallas_call(
        functools.partial(filter_kernel, ng, nrow, rows, run, width, cores, order),
        out_shape=jax.ShapeDtypeStruct((tiles * rows, LANES), jnp.float32),
        in_specs=[hbm] * 5,
        out_specs=vmem,
        scratch_shapes=[
            pltpu.VMEM((ys, planes, xs), jnp.float32),
            pltpu.VMEM((ys, planes, xs), jnp.int32),
            pltpu.VMEM((columns, panel), jnp.float32),
            pltpu.SMEM(potential_table.shape, jnp.float32),
            pltpu.SMEM(counts.shape, jnp.int32),
            pltpu.SemaphoreType.DMA((5,)),
            pltpu.VMEM((ng * rows, LANES), jnp.float32),
        ],
        compiler_params=pltpu.CompilerParams(vmem_limit_bytes=2 * packed_bytes + 64 * cells + 2**20),
        name="chebyshev_filter",
    )(*inputs)
    got = lax.all_to_all(
        packed.reshape(tiles, rows, LANES), ("row", "core", "grid"), split_axis=0, concat_axis=0, tiled=True,
        axis_index_groups=groups,
    )
    sum_shape = jax.ShapeDtypeStruct((panel, run * LANES), jnp.float32)
    if columns * width <= LANES and tiles <= 64 and panel == ng and panel <= 16:
        def partial_sums(distance):
            return pl.pallas_call(
                functools.partial(partial_kernel, nrow, ng, run, width, columns, cores, order, distance),
                out_shape=sum_shape,
                in_specs=[vmem],
                out_specs=vmem,
                scratch_shapes=[pltpu.VMEM((tiles, 1, LANES), jnp.float32)],
                compiler_params=pltpu.CompilerParams(vmem_limit_bytes=packed_bytes + 2**20),
                name="ritz_partial_sums",
            )(got)

    else:
        holders = panel // columns
        by_source = got[jnp.argsort(jnp.array(order))].reshape(nrow, ng, rows, LANES)
        fields = by_source[:, :, :run].reshape(tiles, run * LANES)
        blocks = by_source[:, :, run : run + ritz_rows].reshape(nrow, ng, ritz_rows * per_row, width)

        def partial_sums(distance):
            block = lax.axis_index("row") * cores + lax.rem(lax.axis_index("core") + distance, cores)
            mine = lax.dynamic_slice_in_dim(blocks, block * holders, holders, axis=1)
            return lax.dot_general(
                jnp.transpose(mine[:, :, :columns, :panel], (0, 3, 1, 2)).reshape(tiles, panel),
                fields,
                (((0,), (0,)), ((), ())),
                precision=lax.Precision.HIGHEST,
                preferred_element_type=jnp.float32,
            )

    terms = []
    for distance in range(1, cores):
        pairs = [(core, (core + distance) % cores) for core in range(cores)]
        terms.append(lax.ppermute(partial_sums(distance), "core", pairs))
    terms.append(partial_sums(0))
    return pl.pallas_call(
        sum_kernel,
        out_shape=sum_shape,
        in_specs=[vmem] * cores,
        out_specs=vmem,
        compiler_params=pltpu.CompilerParams(vmem_limit_bytes=4 * (cores + 1) * panel * run * LANES + 2**20),
        name="core_sum",
    )(*terms)


def solution(mesh):
    bands, ng = mesh.shape["band"], mesh.shape["grid"]
    cores = 2 if bands % 2 == 0 else 1
    nrow = bands // cores
    split = jax.sharding.Mesh(mesh.devices.reshape(nrow, cores, ng), ("row", "core", "grid"))
    return jax.shard_map(
        functools.partial(shards, nrow, cores, ng),
        mesh=split,
        in_specs=(P(("row", "core", "grid"), None, None, None), P(), P(), P(), P(("row", "core"), "grid")),
        out_specs=P(("row", "core"), "grid"),
        check_vma=False,
    )
```

```python
import functools

import jax
import jax.numpy as jnp
from jax import lax
from jax.experimental import pallas as pl
from jax.experimental.pallas import tpu as pltpu
from jax.sharding import PartitionSpec as P

DEGREE = 4

COEFFICIENTS = (
    -5369.0 / 1800.0,
    12.0 / 7.0,
    -15.0 / 56.0,
    10.0 / 189.0,
    -1.0 / 112.0,
    2.0 / 1925.0,
    -1.0 / 16632.0,
)
SPACING = 0.5
LOWER = 6.0
UPPER = 46.0
HALF = (UPPER - LOWER) / 2.0
CENTRE = (UPPER + LOWER) / 2.0
LANES = 128
SUBLANES = 8


def ring_weights(length):
    weights = [0.0] * length
    for offset in range(1, 7):
        weights[offset % length] += COEFFICIENTS[offset]
        weights[-offset % length] += COEFFICIENTS[offset]
    return weights


def pair_weights(length):
    weights = ring_weights(length)
    pairs = []
    for distance in range(1, length // 2 + 1):
        if weights[distance] != 0.0:
            pairs.append((sorted({distance, length - distance}), weights[distance]))
    return weights[0], pairs


def along_x(tile):
    length = tile.shape[1]
    near = {-1: pltpu.roll(tile, length - 1, 1), 0: tile, 1: pltpu.roll(tile, 1, 1)}
    total = COEFFICIENTS[1] * (near[-1] + near[1])
    for m in (-2, -1, 1, 2):
        parts = [COEFFICIENTS[abs(3 * m + r)] * near[r] for r in (-1, 0, 1) if abs(3 * m + r) <= 6]
        total = total + pltpu.roll(functools.reduce(jnp.add, parts), (3 * m) % length, 1)
    return total


def along_planes(tile):
    _, pairs = pair_weights(tile.shape[0])
    one, two, three, four = [weight for _, weight in pairs]
    opposite = pltpu.roll(tile, 4, 0)
    odd = one * tile + three * opposite
    even = two * (tile + opposite)
    return four * opposite + pltpu.roll(odd, 1, 0) + pltpu.roll(odd, 7, 0) + pltpu.roll(even, 2, 0)


def off_diagonal(field):
    ys = len(field)
    _, y_pairs = pair_weights(ys)
    results = []
    for y in range(ys):
        total = along_x(field[y]) + along_planes(field[y])
        for shifts, weight in y_pairs:
            total = total + weight * functools.reduce(jnp.add, [field[(y - shift) % ys] for shift in shifts])
        results.append(total)
    return results


def filter_kernel(ng, copies, rows, run, width, cores, order, *refs):
    sources, out_ref, held, sems, natural_ref = refs[:5], refs[5], refs[6:11], refs[11], refs[12]
    orb_ref, region_ref, ritz_ref, table_ref, counts_ref = held
    transfers = [
        pltpu.make_async_copy(source, target, sems.at[index])
        for index, (source, target) in enumerate(zip(sources, held))
    ]
    for transfer in transfers:
        transfer.start()
    for transfer in transfers:
        transfer.wait()
    ys, planes, xs = orb_ref.shape
    band_pos = lax.axis_index("row") * cores + lax.axis_index("core")
    live = (lax.axis_index("grid") < counts_ref[band_pos]).astype(jnp.float32)

    centre_weight = 3.0 * COEFFICIENTS[0] + sum(pair_weights(n)[0] for n in (planes, ys, xs))
    scale = 2.0 / HALF
    hop = -0.5 / (SPACING * SPACING) * scale
    diagonal = []
    for y in range(ys):
        region = region_ref[y]
        potential = jnp.zeros((planes, xs), jnp.float32)
        for index in range(table_ref.shape[0]):
            potential = jnp.where(region == index, table_ref[index], potential)
        diagonal.append(scale * potential + (hop * centre_weight - scale * CENTRE))

    def doubled(field):
        away = off_diagonal(field)
        return [diagonal[y] * field[y] + hop * away[y] for y in range(ys)]

    previous = [orb_ref[y] * live for y in range(ys)]
    current = [0.5 * value for value in doubled(previous)]
    for _ in range(DEGREE - 1):
        following = [value - before for value, before in zip(doubled(current), previous)]
        previous, current = current, following

    blocks = ys // run
    for y in range(ys):
        natural_ref[pl.ds((y // run) * rows + y % run, planes, stride=blocks * rows), :] = current[y]

    columns, panel = ritz_ref.shape
    per_row = LANES // width
    for row in range(-(-columns // per_row)):
        line = jnp.zeros((1, LANES), jnp.float32)
        for slot in range(min(per_row, columns - row * per_row)):
            piece = jnp.concatenate(
                [ritz_ref[pl.ds(row * per_row + slot, 1), :], jnp.zeros((1, LANES - panel), jnp.float32)], axis=1
            )
            line = line + (pltpu.roll(piece, slot * width, 1) if slot else piece)
        natural_ref[pl.ds(run + row, ng, stride=rows), :] = jnp.broadcast_to(line, (ng, LANES))
    for copy in range(copies):
        for tile in range(ng):
            place = order.index(copy * ng + tile)
            out_ref[pl.ds(place * rows, rows), :] = natural_ref[pl.ds(tile * rows, rows), :]


def partial_kernel(nrow, ng, run, width, columns, cores, order, distance, got_ref, out_ref, ritz_ref):
    for place, source in enumerate(order):
        ritz_ref[source] = got_ref[place, pl.ds(run, 1), :]
    wanted = out_ref.shape[0]
    holders = wanted // columns
    sublane = lax.broadcasted_iota(jnp.int32, (wanted, LANES), 0)
    lane = lax.broadcasted_iota(jnp.int32, (wanted, LANES), 1)
    own = lane // width == sublane % columns
    block = lax.axis_index("row") * cores + lax.rem(lax.axis_index("core") + distance, cores)
    acc = [jnp.zeros((wanted, LANES), jnp.float32) for _ in range(run)]
    for row in range(nrow):
        lines = jnp.zeros((wanted, LANES), jnp.float32)
        for k in range(holders):
            line = ritz_ref[row * ng + block * holders + k]
            lines = jnp.where(sublane // columns == k, jnp.broadcast_to(line, (wanted, LANES)), lines)
        lines = jnp.where(own, lines, 0.0)
        weights = lines
        for slot in range(1, columns):
            weights = weights + pltpu.roll(lines, LANES - slot * width, 1)
        for r in range(ng):
            weight = jnp.broadcast_to(weights[:, r : r + 1], (wanted, LANES))
            for y in range(run):
                acc[y] = acc[y] + weight * got_ref[order.index(row * ng + r), pl.ds(y, 1), :]
    for y in range(run):
        out_ref[:, pl.ds(y * LANES, LANES)] = acc[y]


def sum_kernel(*refs):
    refs[-1][...] = functools.reduce(jnp.add, [ref[...] for ref in refs[:-1]])


def shards(nrow, cores, ng, orbitals, region, potential_table, counts, ritz):
    _, planes, ys, xs = orbitals.shape
    cells = planes * ys * xs
    panel, columns = ritz.shape
    run = cells // ng // xs
    width = 1
    while width < panel:
        width *= 2
    per_row = LANES // width
    ritz_rows = -(-columns // per_row)
    rows = -(-(run + ritz_rows) // SUBLANES) * SUBLANES
    tiles = nrow * ng
    vmem = pl.BlockSpec(memory_space=pltpu.VMEM)
    hbm = pl.BlockSpec(memory_space=pltpu.HBM)
    inputs = [
        pltpu.with_memory_space_constraint(value, pltpu.HBM)
        for value in (
            jnp.transpose(orbitals[0], (1, 0, 2)), jnp.transpose(region, (1, 0, 2)), ritz.T, potential_table, counts
        )
    ]
    late = sorted(range(tiles), key=lambda place: (place % ng // (ng // 2), place // ng, place % ng), reverse=True)
    order = [place for pair in zip(late, late[::-1]) for place in pair][:tiles]
    packed_bytes = 4 * tiles * rows * LANES
    packed = pl.pallas_call(
        functools.partial(filter_kernel, ng, nrow, rows, run, width, cores, order),
        out_shape=jax.ShapeDtypeStruct((tiles * rows, LANES), jnp.float32),
        in_specs=[hbm] * 5,
        out_specs=vmem,
        scratch_shapes=[
            pltpu.VMEM((ys, planes, xs), jnp.float32),
            pltpu.VMEM((ys, planes, xs), jnp.int32),
            pltpu.VMEM((columns, panel), jnp.float32),
            pltpu.SMEM(potential_table.shape, jnp.float32),
            pltpu.SMEM(counts.shape, jnp.int32),
            pltpu.SemaphoreType.DMA((5,)),
            pltpu.VMEM((ng * rows, LANES), jnp.float32),
        ],
        compiler_params=pltpu.CompilerParams(vmem_limit_bytes=2 * packed_bytes + 64 * cells + 2**20),
        name="chebyshev_filter",
    )(*inputs)
    got = lax.all_to_all(
        packed.reshape(tiles, rows, LANES), ("row", "grid"), split_axis=0, concat_axis=0, tiled=True,
        axis_index_groups=[order],
    )
    sum_shape = jax.ShapeDtypeStruct((panel, run * LANES), jnp.float32)
    if columns * width <= LANES and tiles <= 64 and panel == ng and panel <= 16:
        def partial_sums(distance):
            return pl.pallas_call(
                functools.partial(partial_kernel, nrow, ng, run, width, columns, cores, order, distance),
                out_shape=sum_shape,
                in_specs=[vmem],
                out_specs=vmem,
                scratch_shapes=[pltpu.VMEM((tiles, 1, LANES), jnp.float32)],
                compiler_params=pltpu.CompilerParams(vmem_limit_bytes=packed_bytes + 2**20),
                name="ritz_partial_sums",
            )(got)

    else:
        holders = panel // columns
        by_source = got[jnp.argsort(jnp.array(order))].reshape(nrow, ng, rows, LANES)
        fields = by_source[:, :, :run].reshape(tiles, run * LANES)
        blocks = by_source[:, :, run : run + ritz_rows].reshape(nrow, ng, ritz_rows * per_row, width)

        def partial_sums(distance):
            block = lax.axis_index("row") * cores + lax.rem(lax.axis_index("core") + distance, cores)
            mine = lax.dynamic_slice_in_dim(blocks, block * holders, holders, axis=1)
            return lax.dot_general(
                jnp.transpose(mine[:, :, :columns, :panel], (0, 3, 1, 2)).reshape(tiles, panel),
                fields,
                (((0,), (0,)), ((), ())),
                precision=lax.Precision.HIGHEST,
                preferred_element_type=jnp.float32,
            )

    terms = []
    for distance in range(1, cores):
        pairs = [(core, (core + distance) % cores) for core in range(cores)]
        terms.append(lax.ppermute(partial_sums(distance), "core", pairs))
    terms.append(partial_sums(0))
    return pl.pallas_call(
        sum_kernel,
        out_shape=sum_shape,
        in_specs=[vmem] * cores,
        out_specs=vmem,
        compiler_params=pltpu.CompilerParams(vmem_limit_bytes=4 * (cores + 1) * panel * run * LANES + 2**20),
        name="core_sum",
    )(*terms)


def solution(mesh):
    bands, ng = mesh.shape["band"], mesh.shape["grid"]
    cores = 2 if bands % 2 == 0 else 1
    nrow = bands // cores
    split = jax.sharding.Mesh(mesh.devices.reshape(nrow, cores, ng), ("row", "core", "grid"))
    return jax.shard_map(
        functools.partial(shards, nrow, cores, ng),
        mesh=split,
        in_specs=(P(("row", "core", "grid"), None, None, None), P(), P(), P(), P(("row", "core"), "grid")),
        out_specs=P(("row", "core"), "grid"),
        check_vma=False,
    )
```

```python
import functools

import jax
import jax.numpy as jnp
from jax import lax
from jax.experimental import pallas as pl
from jax.experimental.pallas import tpu as pltpu
from jax.sharding import PartitionSpec as P

DEGREE = 4

COEFFICIENTS = (
    -5369.0 / 1800.0,
    12.0 / 7.0,
    -15.0 / 56.0,
    10.0 / 189.0,
    -1.0 / 112.0,
    2.0 / 1925.0,
    -1.0 / 16632.0,
)
SPACING = 0.5
LOWER = 6.0
UPPER = 46.0
HALF = (UPPER - LOWER) / 2.0
CENTRE = (UPPER + LOWER) / 2.0
LANES = 128
SUBLANES = 8


def ring_weights(length):
    weights = [0.0] * length
    for offset in range(1, 7):
        weights[offset % length] += COEFFICIENTS[offset]
        weights[-offset % length] += COEFFICIENTS[offset]
    return weights


def pair_weights(length):
    weights = ring_weights(length)
    pairs = []
    for distance in range(1, length // 2 + 1):
        if weights[distance] != 0.0:
            pairs.append((sorted({distance, length - distance}), weights[distance]))
    return weights[0], pairs


def off_diagonal(field, planes, xs):
    ys = len(field)
    _, x_pairs = pair_weights(xs)
    _, y_pairs = pair_weights(ys)
    _, p_pairs = pair_weights(planes)
    results = []
    for y in range(ys):
        tile = field[y]
        total = None
        terms = []
        for shifts, weight in x_pairs:
            terms.append((weight, [pltpu.roll(tile, shift, 1) for shift in shifts]))
        for shifts, weight in p_pairs:
            terms.append((weight, [pltpu.roll(tile, shift, 0) for shift in shifts]))
        for shifts, weight in y_pairs:
            terms.append((weight, [field[(y - shift) % ys] for shift in shifts]))
        for weight, parts in terms:
            value = weight * functools.reduce(jnp.add, parts)
            total = value if total is None else total + value
        results.append(total)
    return results


def filter_kernel(ng, copies, rows, run, width, cores, order, *refs):
    sources, out_ref, held, sems, natural_ref = refs[:5], refs[5], refs[6:11], refs[11], refs[12]
    orb_ref, region_ref, ritz_ref, table_ref, counts_ref = held
    transfers = [
        pltpu.make_async_copy(source, target, sems.at[index])
        for index, (source, target) in enumerate(zip(sources, held))
    ]
    for transfer in transfers:
        transfer.start()
    for transfer in transfers:
        transfer.wait()
    ys, planes, xs = orb_ref.shape
    band_pos = lax.axis_index("row") * cores + lax.axis_index("core")
    live = (lax.axis_index("grid") < counts_ref[band_pos]).astype(jnp.float32)

    centre_weight = 3.0 * COEFFICIENTS[0] + sum(pair_weights(n)[0] for n in (planes, ys, xs))
    scale = 2.0 / HALF
    hop = -0.5 / (SPACING * SPACING) * scale
    diagonal = []
    for y in range(ys):
        region = region_ref[y]
        potential = jnp.zeros((planes, xs), jnp.float32)
        for index in range(table_ref.shape[0]):
            potential = jnp.where(region == index, table_ref[index], potential)
        diagonal.append(scale * potential + (hop * centre_weight - scale * CENTRE))

    def doubled(field):
        away = off_diagonal(field, planes, xs)
        return [diagonal[y] * field[y] + hop * away[y] for y in range(ys)]

    previous = [orb_ref[y] * live for y in range(ys)]
    current = [0.5 * value for value in doubled(previous)]
    for _ in range(DEGREE - 1):
        following = [value - before for value, before in zip(doubled(current), previous)]
        previous, current = current, following

    blocks = ys // run
    for y in range(ys):
        natural_ref[pl.ds((y // run) * rows + y % run, planes, stride=blocks * rows), :] = current[y]

    columns, panel = ritz_ref.shape
    per_row = LANES // width
    for row in range(-(-columns // per_row)):
        line = jnp.zeros((1, LANES), jnp.float32)
        for slot in range(min(per_row, columns - row * per_row)):
            piece = jnp.concatenate(
                [ritz_ref[pl.ds(row * per_row + slot, 1), :], jnp.zeros((1, LANES - panel), jnp.float32)], axis=1
            )
            line = line + (pltpu.roll(piece, slot * width, 1) if slot else piece)
        natural_ref[pl.ds(run + row, ng, stride=rows), :] = jnp.broadcast_to(line, (ng, LANES))
    for copy in range(copies):
        for tile in range(ng):
            place = order.index(copy * ng + tile)
            out_ref[pl.ds(place * rows, rows), :] = natural_ref[pl.ds(tile * rows, rows), :]


def partial_kernel(nrow, ng, run, width, columns, cores, order, distance, got_ref, out_ref, ritz_ref):
    for place, source in enumerate(order):
        ritz_ref[source] = got_ref[place, pl.ds(run, 1), :]
    wanted = out_ref.shape[0]
    holders = wanted // columns
    sublane = lax.broadcasted_iota(jnp.int32, (wanted, LANES), 0)
    lane = lax.broadcasted_iota(jnp.int32, (wanted, LANES), 1)
    own = lane // width == sublane % columns
    block = lax.axis_index("row") * cores + lax.rem(lax.axis_index("core") + distance, cores)
    acc = [jnp.zeros((wanted, LANES), jnp.float32) for _ in range(run)]
    for row in range(nrow):
        lines = jnp.zeros((wanted, LANES), jnp.float32)
        for k in range(holders):
            line = ritz_ref[row * ng + block * holders + k]
            lines = jnp.where(sublane // columns == k, jnp.broadcast_to(line, (wanted, LANES)), lines)
        lines = jnp.where(own, lines, 0.0)
        weights = lines
        for slot in range(1, columns):
            weights = weights + pltpu.roll(lines, LANES - slot * width, 1)
        for r in range(ng):
            weight = jnp.broadcast_to(weights[:, r : r + 1], (wanted, LANES))
            for y in range(run):
                acc[y] = acc[y] + weight * got_ref[order.index(row * ng + r), pl.ds(y, 1), :]
    for y in range(run):
        out_ref[:, pl.ds(y * LANES, LANES)] = acc[y]


def sum_kernel(*refs):
    refs[-1][...] = functools.reduce(jnp.add, [ref[...] for ref in refs[:-1]])


def shards(nrow, cores, ng, orbitals, region, potential_table, counts, ritz):
    _, planes, ys, xs = orbitals.shape
    cells = planes * ys * xs
    panel, columns = ritz.shape
    run = cells // ng // xs
    width = 1
    while width < panel:
        width *= 2
    per_row = LANES // width
    ritz_rows = -(-columns // per_row)
    rows = -(-(run + ritz_rows) // SUBLANES) * SUBLANES
    tiles = nrow * ng
    vmem = pl.BlockSpec(memory_space=pltpu.VMEM)
    hbm = pl.BlockSpec(memory_space=pltpu.HBM)
    inputs = [
        pltpu.with_memory_space_constraint(value, pltpu.HBM)
        for value in (
            jnp.transpose(orbitals[0], (1, 0, 2)), jnp.transpose(region, (1, 0, 2)), ritz.T, potential_table, counts
        )
    ]
    others = sorted(range(1, tiles - 1), key=lambda chip: (chip % ng // 2, chip), reverse=True)
    order = [tiles - 1, 0] + others
    packed_bytes = 4 * tiles * rows * LANES
    packed = pl.pallas_call(
        functools.partial(filter_kernel, ng, nrow, rows, run, width, cores, order),
        out_shape=jax.ShapeDtypeStruct((tiles * rows, LANES), jnp.float32),
        in_specs=[hbm] * 5,
        out_specs=vmem,
        scratch_shapes=[
            pltpu.VMEM((ys, planes, xs), jnp.float32),
            pltpu.VMEM((ys, planes, xs), jnp.int32),
            pltpu.VMEM((columns, panel), jnp.float32),
            pltpu.SMEM(potential_table.shape, jnp.float32),
            pltpu.SMEM(counts.shape, jnp.int32),
            pltpu.SemaphoreType.DMA((5,)),
            pltpu.VMEM((ng * rows, LANES), jnp.float32),
        ],
        compiler_params=pltpu.CompilerParams(vmem_limit_bytes=2 * packed_bytes + 64 * cells + 2**20),
        name="chebyshev_filter",
    )(*inputs)
    got = lax.all_to_all(
        packed.reshape(tiles, rows, LANES), ("row", "grid"), split_axis=0, concat_axis=0, tiled=True,
        axis_index_groups=[order],
    )
    sum_shape = jax.ShapeDtypeStruct((panel, run * LANES), jnp.float32)
    if columns * width <= LANES and tiles <= 64 and panel == ng and panel <= 16:
        def partial_sums(distance):
            return pl.pallas_call(
                functools.partial(partial_kernel, nrow, ng, run, width, columns, cores, order, distance),
                out_shape=sum_shape,
                in_specs=[vmem],
                out_specs=vmem,
                scratch_shapes=[pltpu.VMEM((tiles, 1, LANES), jnp.float32)],
                compiler_params=pltpu.CompilerParams(vmem_limit_bytes=packed_bytes + 2**20),
                name="ritz_partial_sums",
            )(got)

    else:
        holders = panel // columns
        by_source = got[jnp.argsort(jnp.array(order))].reshape(nrow, ng, rows, LANES)
        fields = by_source[:, :, :run].reshape(tiles, run * LANES)
        blocks = by_source[:, :, run : run + ritz_rows].reshape(nrow, ng, ritz_rows * per_row, width)

        def partial_sums(distance):
            block = lax.axis_index("row") * cores + lax.rem(lax.axis_index("core") + distance, cores)
            mine = lax.dynamic_slice_in_dim(blocks, block * holders, holders, axis=1)
            return lax.dot_general(
                jnp.transpose(mine[:, :, :columns, :panel], (0, 3, 1, 2)).reshape(tiles, panel),
                fields,
                (((0,), (0,)), ((), ())),
                precision=lax.Precision.HIGHEST,
                preferred_element_type=jnp.float32,
            )

    terms = []
    for distance in range(1, cores):
        pairs = [(core, (core + distance) % cores) for core in range(cores)]
        terms.append(lax.ppermute(partial_sums(distance), "core", pairs))
    terms.append(partial_sums(0))
    return pl.pallas_call(
        sum_kernel,
        out_shape=sum_shape,
        in_specs=[vmem] * cores,
        out_specs=vmem,
        compiler_params=pltpu.CompilerParams(vmem_limit_bytes=4 * (cores + 1) * panel * run * LANES + 2**20),
        name="core_sum",
    )(*terms)


def solution(mesh):
    bands, ng = mesh.shape["band"], mesh.shape["grid"]
    cores = 2 if bands % 2 == 0 else 1
    nrow = bands // cores
    split = jax.sharding.Mesh(mesh.devices.reshape(nrow, cores, ng), ("row", "core", "grid"))
    return jax.shard_map(
        functools.partial(shards, nrow, cores, ng),
        mesh=split,
        in_specs=(P(("row", "core", "grid"), None, None, None), P(), P(), P(), P(("row", "core"), "grid")),
        out_specs=P(("row", "core"), "grid"),
        check_vma=False,
    )
```

```python
import functools

import jax
import jax.numpy as jnp
from jax import lax
from jax.experimental import pallas as pl
from jax.experimental.pallas import tpu as pltpu
from jax.sharding import PartitionSpec as P

DEGREE = 4

COEFFICIENTS = (
    -5369.0 / 1800.0,
    12.0 / 7.0,
    -15.0 / 56.0,
    10.0 / 189.0,
    -1.0 / 112.0,
    2.0 / 1925.0,
    -1.0 / 16632.0,
)
SPACING = 0.5
LOWER = 6.0
UPPER = 46.0
HALF = (UPPER - LOWER) / 2.0
CENTRE = (UPPER + LOWER) / 2.0
LANES = 128
SUBLANES = 8


def ring_weights(length):
    weights = [0.0] * length
    for offset in range(1, 7):
        weights[offset % length] += COEFFICIENTS[offset]
        weights[-offset % length] += COEFFICIENTS[offset]
    return weights


def pair_weights(length):
    weights = ring_weights(length)
    pairs = []
    for distance in range(1, length // 2 + 1):
        if weights[distance] != 0.0:
            pairs.append((sorted({distance, length - distance}), weights[distance]))
    return weights[0], pairs


def apply(field, diagonal, hop, before):
    ys = len(field)
    planes, xs = field[0].shape
    along_y, along_planes, along_x = [pair_weights(length)[1] for length in (ys, planes, xs)]
    results = []
    for y in range(ys):
        tile = field[y]
        total = diagonal[y] * tile
        if before is not None:
            total = total - before[y]
        for shifts, weight in along_y:
            total = total + (hop * weight) * functools.reduce(jnp.add, [field[(y - shift) % ys] for shift in shifts])
        for pairs, axis in ((along_planes, 0), (along_x, 1)):
            for shifts, weight in pairs:
                total = total + (hop * weight) * functools.reduce(
                    jnp.add, [pltpu.roll(tile, shift, axis) for shift in shifts]
                )
        results.append(total)
    return results


def filter_kernel(ng, copies, rows, run, width, cores, order, *refs):
    sources, out_ref, held, sems, natural_ref = refs[:5], refs[5], refs[6:11], refs[11], refs[12]
    orb_ref, region_ref, table_ref, counts_ref, ritz_ref = held
    transfers = [
        pltpu.make_async_copy(source, target, sems.at[index])
        for index, (source, target) in enumerate(zip(sources, held))
    ]
    for transfer in transfers:
        transfer.start()
    for transfer in transfers:
        transfer.wait()
    ys, planes, xs = orb_ref.shape
    columns, panel = ritz_ref.shape
    per_row = LANES // width
    for row in range(-(-columns // per_row)):
        line = jnp.zeros((1, LANES), jnp.float32)
        for slot in range(min(per_row, columns - row * per_row)):
            piece = jnp.concatenate(
                [ritz_ref[pl.ds(row * per_row + slot, 1), :], jnp.zeros((1, LANES - panel), jnp.float32)], axis=1
            )
            line = line + (pltpu.roll(piece, slot * width, 1) if slot else piece)
        natural_ref[pl.ds(run + row, ng, stride=rows), :] = jnp.broadcast_to(line, (ng, LANES))

    centre_weight = 3.0 * COEFFICIENTS[0] + sum(pair_weights(n)[0] for n in (planes, ys, xs))
    scale = 2.0 / HALF
    hop = -0.5 / (SPACING * SPACING) * scale
    diagonal = []
    for y in range(ys):
        region = region_ref[y]
        potential = jnp.zeros((planes, xs), jnp.float32)
        for index in range(table_ref.shape[0]):
            potential = jnp.where(region == index, table_ref[index], potential)
        diagonal.append(scale * potential + (hop * centre_weight - scale * CENTRE))
    band_pos = lax.axis_index("row") * cores + lax.axis_index("core")
    live = (lax.axis_index("grid") < counts_ref[band_pos]).astype(jnp.float32)
    previous = [live * orb_ref[y] for y in range(ys)]
    current = apply(previous, [0.5 * value for value in diagonal], 0.5 * hop, None)
    for _ in range(DEGREE - 1):
        previous, current = current, apply(current, diagonal, hop, previous)

    blocks = ys // run
    for y in range(ys):
        natural_ref[pl.ds((y // run) * rows + y % run, planes, stride=blocks * rows), :] = current[y]
    for copy in range(copies):
        for tile in range(ng):
            place = order.index(copy * ng + tile)
            out_ref[pl.ds(place * rows, rows), :] = natural_ref[pl.ds(tile * rows, rows), :]


def partial_kernel(nrow, ng, run, width, columns, cores, order, distance, got_ref, out_ref, ritz_ref):
    for place, source in enumerate(order):
        ritz_ref[source] = got_ref[place, pl.ds(run, 1), :]
    wanted = out_ref.shape[0]
    holders = wanted // columns
    sublane = lax.broadcasted_iota(jnp.int32, (wanted, LANES), 0)
    block = lax.axis_index("row") * cores + lax.rem(lax.axis_index("core") + distance, cores)
    acc = [jnp.zeros((wanted, LANES), jnp.float32) for _ in range(run)]
    for row in range(nrow):
        lines = jnp.zeros((wanted, LANES), jnp.float32)
        for k in range(holders):
            line = ritz_ref[row * ng + block * holders + k]
            lines = jnp.where(sublane // columns == k, jnp.broadcast_to(line, (wanted, LANES)), lines)
        for r in range(ng):
            weight = jnp.take_along_axis(lines, sublane % columns * width + r, axis=1)
            for y in range(run):
                acc[y] = acc[y] + weight * got_ref[order.index(row * ng + r), pl.ds(y, 1), :]
    for y in range(run):
        out_ref[:, pl.ds(y * LANES, LANES)] = acc[y]


def sum_kernel(*refs):
    refs[-1][...] = functools.reduce(jnp.add, [ref[...] for ref in refs[:-1]])


def shards(nrow, cores, ng, orbitals, region, potential_table, counts, ritz):
    _, planes, ys, xs = orbitals.shape
    cells = planes * ys * xs
    panel, columns = ritz.shape
    run = cells // ng // xs
    width = 1
    while width < panel:
        width *= 2
    per_row = LANES // width
    ritz_rows = -(-columns // per_row)
    rows = -(-(run + ritz_rows) // SUBLANES) * SUBLANES
    tiles = nrow * ng
    vmem = pl.BlockSpec(memory_space=pltpu.VMEM)
    hbm = pl.BlockSpec(memory_space=pltpu.HBM)
    inputs = [
        pltpu.with_memory_space_constraint(value, pltpu.HBM)
        for value in (
            jnp.transpose(orbitals[0], (1, 0, 2)), jnp.transpose(region, (1, 0, 2)), potential_table, counts, ritz.T
        )
    ]
    late = sorted(range(tiles), key=lambda place: (place % ng // (ng // 2), place // ng, place % ng), reverse=True)
    order = [place for pair in zip(late, late[::-1]) for place in pair][:tiles]
    packed_bytes = 4 * tiles * rows * LANES
    packed = pl.pallas_call(
        functools.partial(filter_kernel, ng, nrow, rows, run, width, cores, order),
        out_shape=jax.ShapeDtypeStruct((tiles * rows, LANES), jnp.float32),
        in_specs=[hbm] * 5,
        out_specs=vmem,
        scratch_shapes=[
            pltpu.VMEM((ys, planes, xs), jnp.float32),
            pltpu.VMEM((ys, planes, xs), jnp.int32),
            pltpu.SMEM(potential_table.shape, jnp.float32),
            pltpu.SMEM(counts.shape, jnp.int32),
            pltpu.VMEM((columns, panel), jnp.float32),
            pltpu.SemaphoreType.DMA((5,)),
            pltpu.VMEM((ng * rows, LANES), jnp.float32),
        ],
        compiler_params=pltpu.CompilerParams(vmem_limit_bytes=2 * packed_bytes + 64 * cells + 2**20),
        name="chebyshev_filter",
    )(*inputs)
    got = lax.all_to_all(
        packed.reshape(tiles, rows, LANES), ("row", "grid"), split_axis=0, concat_axis=0, tiled=True,
        axis_index_groups=[order],
    )
    sum_shape = jax.ShapeDtypeStruct((panel, run * LANES), jnp.float32)
    if columns * width <= LANES and tiles <= 64 and panel == ng and panel <= 16:
        def partial_sums(distance):
            return pl.pallas_call(
                functools.partial(partial_kernel, nrow, ng, run, width, columns, cores, order, distance),
                out_shape=sum_shape,
                in_specs=[vmem],
                out_specs=vmem,
                scratch_shapes=[pltpu.VMEM((tiles, 1, LANES), jnp.float32)],
                compiler_params=pltpu.CompilerParams(vmem_limit_bytes=packed_bytes + 2**20),
                name="ritz_partial_sums",
            )(got)

    else:
        holders = panel // columns
        by_source = got[jnp.argsort(jnp.array(order))].reshape(nrow, ng, rows, LANES)
        fields = by_source[:, :, :run].reshape(tiles, run * LANES)
        blocks = by_source[:, :, run : run + ritz_rows].reshape(nrow, ng, ritz_rows * per_row, width)

        def partial_sums(distance):
            block = lax.axis_index("row") * cores + lax.rem(lax.axis_index("core") + distance, cores)
            mine = lax.dynamic_slice_in_dim(blocks, block * holders, holders, axis=1)
            return lax.dot_general(
                jnp.transpose(mine[:, :, :columns, :panel], (0, 3, 1, 2)).reshape(tiles, panel),
                fields,
                (((0,), (0,)), ((), ())),
                precision=lax.Precision.HIGHEST,
                preferred_element_type=jnp.float32,
            )

    terms = []
    for distance in range(1, cores):
        pairs = [(core, (core + distance) % cores) for core in range(cores)]
        terms.append(lax.ppermute(partial_sums(distance), "core", pairs))
    terms.append(partial_sums(0))
    return pl.pallas_call(
        sum_kernel,
        out_shape=sum_shape,
        in_specs=[vmem] * cores,
        out_specs=vmem,
        compiler_params=pltpu.CompilerParams(vmem_limit_bytes=4 * (cores + 1) * panel * run * LANES + 2**20),
        name="core_sum",
    )(*terms)


def solution(mesh):
    bands, ng = mesh.shape["band"], mesh.shape["grid"]
    cores = 2 if bands % 2 == 0 else 1
    nrow = bands // cores
    split = jax.sharding.Mesh(mesh.devices.reshape(nrow, cores, ng), ("row", "core", "grid"))
    return jax.shard_map(
        functools.partial(shards, nrow, cores, ng),
        mesh=split,
        in_specs=(P(("row", "core", "grid"), None, None, None), P(), P(), P(), P(("row", "core"), "grid")),
        out_specs=P(("row", "core"), "grid"),
        check_vma=False,
    )
```

```python
import functools

import jax
import jax.numpy as jnp
from jax import lax
from jax.experimental import pallas as pl
from jax.experimental.pallas import tpu as pltpu
from jax.sharding import PartitionSpec as P

DEGREE = 4

COEFFICIENTS = (
    -5369.0 / 1800.0,
    12.0 / 7.0,
    -15.0 / 56.0,
    10.0 / 189.0,
    -1.0 / 112.0,
    2.0 / 1925.0,
    -1.0 / 16632.0,
)
SPACING = 0.5
LOWER = 6.0
UPPER = 46.0
HALF = (UPPER - LOWER) / 2.0
CENTRE = (UPPER + LOWER) / 2.0
LANES = 128
SUBLANES = 8


def ring_weights(length):
    weights = [0.0] * length
    for offset in range(1, 7):
        weights[offset % length] += COEFFICIENTS[offset]
        weights[-offset % length] += COEFFICIENTS[offset]
    return weights


def pair_weights(length):
    weights = ring_weights(length)
    pairs = []
    for distance in range(1, length // 2 + 1):
        if weights[distance] != 0.0:
            pairs.append((sorted({distance, length - distance}), weights[distance]))
    return weights[0], pairs


def apply(field, diagonal, hop, before):
    ys = len(field)
    planes, xs = field[0].shape
    along_y, along_planes, along_x = [pair_weights(length)[1] for length in (ys, planes, xs)]
    results = []
    for y in range(ys):
        tile = field[y]
        total = diagonal[y] * tile
        if before is not None:
            total = total - before[y]
        for shifts, weight in along_y:
            total = total + (hop * weight) * functools.reduce(jnp.add, [field[(y - shift) % ys] for shift in shifts])
        for pairs, axis in ((along_planes, 0), (along_x, 1)):
            for shifts, weight in pairs:
                total = total + (hop * weight) * functools.reduce(
                    jnp.add, [pltpu.roll(tile, shift, axis) for shift in shifts]
                )
        results.append(total)
    return results


def filtered_tiles(rows, run, width, sources, held, sems, natural_ref):
    orb_ref, region_ref, table_ref, counts_ref, ritz_ref = held
    transfers = [
        pltpu.make_async_copy(source, target, sems.at[index])
        for index, (source, target) in enumerate(zip(sources, held))
    ]
    for transfer in transfers:
        transfer.start()
    for transfer in transfers:
        transfer.wait()
    ys, planes, xs = orb_ref.shape
    columns, panel = ritz_ref.shape
    ng = natural_ref.shape[0] // rows
    per_row = LANES // width
    for row in range(-(-columns // per_row)):
        line = jnp.zeros((1, LANES), jnp.float32)
        for slot in range(min(per_row, columns - row * per_row)):
            piece = jnp.concatenate(
                [ritz_ref[pl.ds(row * per_row + slot, 1), :], jnp.zeros((1, LANES - panel), jnp.float32)], axis=1
            )
            line = line + (pltpu.roll(piece, slot * width, 1) if slot else piece)
        natural_ref[pl.ds(run + row, ng, stride=rows), :] = jnp.broadcast_to(line, (ng, LANES))

    centre_weight = 3.0 * COEFFICIENTS[0] + sum(pair_weights(n)[0] for n in (planes, ys, xs))
    scale = 2.0 / HALF
    hop = -0.5 / (SPACING * SPACING) * scale
    diagonal = []
    for y in range(ys):
        region = region_ref[y]
        potential = jnp.zeros((planes, xs), jnp.float32)
        for index in range(table_ref.shape[0]):
            potential = jnp.where(region == index, table_ref[index], potential)
        diagonal.append(scale * potential + (hop * centre_weight - scale * CENTRE))
    live = (lax.axis_index("grid") < counts_ref[lax.axis_index("band")]).astype(jnp.float32)
    previous = [live * orb_ref[y] for y in range(ys)]
    current = apply(previous, [0.5 * value for value in diagonal], 0.5 * hop, None)
    for _ in range(DEGREE - 1):
        previous, current = current, apply(current, diagonal, hop, previous)

    blocks = ys // run
    for y in range(ys):
        natural_ref[pl.ds((y // run) * rows + y % run, planes, stride=blocks * rows), :] = current[y]


def filter_to_all(rows, run, width, order, *refs):
    sources, out_ref, held, sems, natural_ref = refs[:5], refs[5], refs[6:11], refs[11], refs[12]
    filtered_tiles(rows, run, width, sources, held, sems, natural_ref)
    ng = natural_ref.shape[0] // rows
    for place, chip in enumerate(order):
        out_ref[pl.ds(place * rows, rows), :] = natural_ref[pl.ds(chip % ng * rows, rows), :]


def filter_to_lines(rows, run, width, distances, *refs):
    sources, outs, held, sems, natural_ref = refs[:5], refs[5:-7], refs[-7:-2], refs[-2], refs[-1]
    filtered_tiles(rows, run, width, sources, held, sems, natural_ref)
    here = lax.axis_index("grid")
    for distance, out_ref in zip(distances, outs):
        for dx in (0, 1):
            start = pl.multiple_of((here ^ (2 * distance + dx)) * rows, rows)
            out_ref[dx] = natural_ref[pl.ds(start, rows), :]


def turn_kernel(kept_ref, *refs):
    count = len(refs) - 7
    from_late, from_early, outs = refs[: count // 2], refs[count // 2 : count][::-1], refs[count:]
    here = lax.axis_index("grid") // 2
    pairs = [kept_ref[...]]
    for distance, (late_ref, early_ref) in enumerate(zip(from_late, from_early), 1):
        pairs.append(jnp.where((here ^ distance) > here, late_ref[...], early_ref[...]))
    for out_ref, dx in zip(outs, (0, 1, 0, 1, 1, 0, 1)):
        for distance, pair in enumerate(pairs):
            out_ref[distance] = pair[dx]


def gather_sums(run, width, columns, distance, own_ref, x_late, y_late, xy_late, xy_early, y_early, x_early, *refs):
    out_ref, tiles_ref = refs
    depth = own_ref.shape[0]
    band, here = lax.axis_index("band"), lax.axis_index("grid")
    row, z, x = band // 2, here // 2, here % 2
    tiles_ref[0, 0] = own_ref[...]
    tiles_ref[0, 1] = jnp.where(x == 0, x_late[...], x_early[...])
    tiles_ref[1, 0] = jnp.where(row == 0, y_late[...], y_early[...])
    tiles_ref[1, 1] = jnp.where(row == 0, xy_late[...], xy_early[...])
    wanted = out_ref.shape[0]
    holders = wanted // columns
    sublane = lax.broadcasted_iota(jnp.int32, (wanted, LANES), 0)
    block = band ^ distance
    acc = [jnp.zeros((wanted, LANES), jnp.float32) for _ in range(run)]
    for dy in (0, 1):
        lines = jnp.zeros((wanted, LANES), jnp.float32)
        for k in range(holders):
            holder = block * holders + k
            line = tiles_ref[dy, x ^ (holder % 2), z ^ (holder // 2), pl.ds(run, 1), :]
            lines = jnp.where(sublane // columns == k, jnp.broadcast_to(line, (wanted, LANES)), lines)
        for dx in (0, 1):
            for dz in range(depth):
                weight = jnp.take_along_axis(lines, sublane % columns * width + (here ^ (2 * dz + dx)), axis=1)
                for y in range(run):
                    acc[y] = acc[y] + weight * tiles_ref[dy, dx, dz, pl.ds(y, 1), :]
    for y in range(run):
        out_ref[:, pl.ds(y * LANES, LANES)] = acc[y]


def sum_kernel(*refs):
    refs[-1][...] = functools.reduce(jnp.add, [ref[...] for ref in refs[:-1]])


def send(value, axis, size, distance, late):
    pairs = [(place, place ^ distance) for place in range(size)]
    return lax.ppermute(value, axis, [(source, target) for source, target in pairs if (source > target) == late])


def shards(nb, ng, orbitals, region, potential_table, counts, ritz):
    _, planes, ys, xs = orbitals.shape
    cells = planes * ys * xs
    panel, columns = ritz.shape
    run = cells // ng // xs
    width = 1
    while width < panel:
        width *= 2
    per_row = LANES // width
    ritz_rows = -(-columns // per_row)
    rows = -(-(run + ritz_rows) // SUBLANES) * SUBLANES
    cores = 2 if nb % 2 == 0 else 1
    chips = nb // cores * ng
    vmem = pl.BlockSpec(memory_space=pltpu.VMEM)
    hbm = pl.BlockSpec(memory_space=pltpu.HBM)
    inputs = [
        pltpu.with_memory_space_constraint(value, pltpu.HBM)
        for value in (
            jnp.transpose(orbitals[0], (1, 0, 2)), jnp.transpose(region, (1, 0, 2)), potential_table, counts, ritz.T
        )
    ]
    scratch = [
        pltpu.VMEM((ys, planes, xs), jnp.float32),
        pltpu.VMEM((ys, planes, xs), jnp.int32),
        pltpu.SMEM(potential_table.shape, jnp.float32),
        pltpu.SMEM(counts.shape, jnp.int32),
        pltpu.VMEM((columns, panel), jnp.float32),
        pltpu.SemaphoreType.DMA((5,)),
        pltpu.VMEM((ng * rows, LANES), jnp.float32),
    ]
    limit = pltpu.CompilerParams(vmem_limit_bytes=8 * chips * rows * LANES + 64 * cells + 2**20)
    small = pltpu.CompilerParams(vmem_limit_bytes=2**21)
    sum_shape = jax.ShapeDtypeStruct((panel, run * LANES), jnp.float32)
    terms = []

    if (nb, ng, panel) == (4, 8, 8) and columns * width <= LANES and rows == SUBLANES:
        depth = ng // 2
        distances = [0, 1, 2, 3, 3, 2, 1]
        lines = pl.pallas_call(
            functools.partial(filter_to_lines, rows, run, width, distances),
            out_shape=[jax.ShapeDtypeStruct((2, rows, LANES), jnp.float32)] * 7,
            in_specs=[hbm] * 5,
            out_specs=[vmem] * 7,
            scratch_shapes=scratch,
            compiler_params=limit,
            name="chebyshev_filter",
        )(*inputs)
        sent = [
            send(lines[place], "grid", ng, 2 * distances[place], late=place <= 3) for place in range(1, 7)
        ]
        planes_of = pl.pallas_call(
            turn_kernel,
            out_shape=[jax.ShapeDtypeStruct((depth, rows, LANES), jnp.float32)] * 7,
            in_specs=[vmem] * 7,
            out_specs=[vmem] * 7,
            compiler_params=small,
            name="turn",
        )(lines[0], *sent)
        along_x, along_y, across = ("grid", ng, 1), ("band", nb, 2), (("band", "grid"), nb * ng, 2 * ng + 1)
        ways = [along_x, along_y, across, across, along_y, along_x]
        sent = [send(planes_of[place], *ways[place - 1], late=place <= 3) for place in range(1, 7)]

        def partial_sums(distance):
            return pl.pallas_call(
                functools.partial(gather_sums, run, width, columns, distance),
                out_shape=sum_shape,
                in_specs=[vmem] * 7,
                out_specs=vmem,
                scratch_shapes=[pltpu.VMEM((2, 2, depth, rows, LANES), jnp.float32)],
                compiler_params=small,
                name="ritz_partial_sums",
            )(planes_of[0], *sent)
    else:
        order = list(range(chips))[::-1]
        groups = [[(chip // ng * cores + core) * ng + chip % ng for chip in order] for core in range(cores)]
        packed = pl.pallas_call(
            functools.partial(filter_to_all, rows, run, width, order),
            out_shape=jax.ShapeDtypeStruct((chips * rows, LANES), jnp.float32),
            in_specs=[hbm] * 5,
            out_specs=vmem,
            scratch_shapes=scratch,
            compiler_params=limit,
            name="chebyshev_filter",
        )(*inputs)
        got = lax.all_to_all(
            packed.reshape(chips, rows, LANES), ("band", "grid"), split_axis=0, concat_axis=0, tiled=True,
            axis_index_groups=groups,
        )
        by_source = got[::-1].reshape(nb // cores, ng, rows, LANES)
        fields = by_source[:, :, :run].reshape(chips, run * LANES)
        blocks = by_source[:, :, run : run + ritz_rows].reshape(nb // cores, ng, ritz_rows * per_row, width)

        def partial_sums(distance):
            holders = panel // columns
            mine = lax.dynamic_slice_in_dim(blocks, (lax.axis_index("band") ^ distance) * holders, holders, axis=1)
            return lax.dot_general(
                jnp.transpose(mine[:, :, :columns, :panel], (0, 3, 1, 2)).reshape(chips, panel),
                fields,
                (((0,), (0,)), ((), ())),
                precision=lax.Precision.HIGHEST,
                preferred_element_type=jnp.float32,
            )

    if cores == 2:
        terms.append(lax.ppermute(partial_sums(1), "band", [(band, band ^ 1) for band in range(nb)]))
    terms.append(partial_sums(0))
    return pl.pallas_call(
        sum_kernel,
        out_shape=sum_shape,
        in_specs=[vmem] * cores,
        out_specs=vmem,
        compiler_params=pltpu.CompilerParams(vmem_limit_bytes=4 * (cores + 1) * panel * run * LANES + 2**20),
        name="core_sum",
    )(*terms)


def solution(mesh):
    return jax.shard_map(
        functools.partial(shards, mesh.shape["band"], mesh.shape["grid"]),
        mesh=mesh,
        in_specs=(P(("band", "grid"), None, None, None), P(), P(), P(), P("band", "grid")),
        out_specs=P("band", "grid"),
        check_vma=False,
    )
```

```python
import functools

import jax
import jax.numpy as jnp
from jax import lax
from jax.experimental import pallas as pl
from jax.experimental.pallas import tpu as pltpu
from jax.sharding import PartitionSpec as P

DEGREE = 4

COEFFICIENTS = (
    -5369.0 / 1800.0,
    12.0 / 7.0,
    -15.0 / 56.0,
    10.0 / 189.0,
    -1.0 / 112.0,
    2.0 / 1925.0,
    -1.0 / 16632.0,
)
SPACING = 0.5
LOWER = 6.0
UPPER = 46.0
HALF = (UPPER - LOWER) / 2.0
CENTRE = (UPPER + LOWER) / 2.0
LANES = 128
SUBLANES = 8


def ring_weights(length):
    weights = [0.0] * length
    for offset in range(1, 7):
        weights[offset % length] += COEFFICIENTS[offset]
        weights[-offset % length] += COEFFICIENTS[offset]
    return weights


def pair_weights(length):
    weights = ring_weights(length)
    pairs = []
    for distance in range(1, length // 2 + 1):
        if weights[distance] != 0.0:
            pairs.append((sorted({distance, length - distance}), weights[distance]))
    return weights[0], pairs


def apply(field, diagonal, hop, before):
    ys = len(field)
    planes, xs = field[0].shape
    along_y, along_planes, along_x = [pair_weights(length)[1] for length in (ys, planes, xs)]
    results = []
    for y in range(ys):
        tile = field[y]
        total = diagonal[y] * tile
        if before is not None:
            total = total - before[y]
        for shifts, weight in along_y:
            total = total + (hop * weight) * functools.reduce(jnp.add, [field[(y - shift) % ys] for shift in shifts])
        for pairs, axis in ((along_planes, 0), (along_x, 1)):
            for shifts, weight in pairs:
                total = total + (hop * weight) * functools.reduce(
                    jnp.add, [pltpu.roll(tile, shift, axis) for shift in shifts]
                )
        results.append(total)
    return results


def filtered_tiles(rows, run, width, sources, held, sems, natural_ref):
    orb_ref, region_ref, table_ref, counts_ref, ritz_ref = held
    transfers = [
        pltpu.make_async_copy(source, target, sems.at[index])
        for index, (source, target) in enumerate(zip(sources, held))
    ]
    for transfer in transfers:
        transfer.start()
    for transfer in transfers:
        transfer.wait()
    ys, planes, xs = orb_ref.shape
    columns, panel = ritz_ref.shape
    ng = natural_ref.shape[0] // rows
    per_row = LANES // width
    for row in range(-(-columns // per_row)):
        line = jnp.zeros((1, LANES), jnp.float32)
        for slot in range(min(per_row, columns - row * per_row)):
            piece = jnp.concatenate(
                [ritz_ref[pl.ds(row * per_row + slot, 1), :], jnp.zeros((1, LANES - panel), jnp.float32)], axis=1
            )
            line = line + (pltpu.roll(piece, slot * width, 1) if slot else piece)
        natural_ref[pl.ds(run + row, ng, stride=rows), :] = jnp.broadcast_to(line, (ng, LANES))

    centre_weight = 3.0 * COEFFICIENTS[0] + sum(pair_weights(n)[0] for n in (planes, ys, xs))
    scale = 2.0 / HALF
    hop = -0.5 / (SPACING * SPACING) * scale
    diagonal = []
    for y in range(ys):
        region = region_ref[y]
        potential = jnp.zeros((planes, xs), jnp.float32)
        for index in range(table_ref.shape[0]):
            potential = jnp.where(region == index, table_ref[index], potential)
        diagonal.append(scale * potential + (hop * centre_weight - scale * CENTRE))
    live = (lax.axis_index("grid") < counts_ref[lax.axis_index("band")]).astype(jnp.float32)
    previous = [live * orb_ref[y] for y in range(ys)]
    current = apply(previous, [0.5 * value for value in diagonal], 0.5 * hop, None)
    for _ in range(DEGREE - 1):
        previous, current = current, apply(current, diagonal, hop, previous)

    blocks = ys // run
    for y in range(ys):
        natural_ref[pl.ds((y // run) * rows + y % run, planes, stride=blocks * rows), :] = current[y]


def filter_to_all(rows, run, width, order, *refs):
    sources, out_ref, held, sems, natural_ref = refs[:5], refs[5], refs[6:11], refs[11], refs[12]
    filtered_tiles(rows, run, width, sources, held, sems, natural_ref)
    ng = natural_ref.shape[0] // rows
    for place, chip in enumerate(order):
        out_ref[pl.ds(place * rows, rows), :] = natural_ref[pl.ds(chip % ng * rows, rows), :]


def filter_to_lines(rows, run, width, *refs):
    sources, outs, held, sems, natural_ref = refs[:5], refs[5:7], refs[7:12], refs[12], refs[13]
    filtered_tiles(rows, run, width, sources, held, sems, natural_ref)
    here = lax.axis_index("grid")
    for far, out_ref in enumerate(outs):
        for tile in range(4):
            start = pl.multiple_of((here ^ (4 * far + tile)) * rows, rows)
            out_ref[tile] = natural_ref[pl.ds(start, rows), :]


def turn_kernel(kept_ref, came_ref, first_ref, second_ref):
    count = first_ref.shape[0] // 2
    for half, ref in enumerate((kept_ref, came_ref)):
        first_ref[pl.ds(half * count, count)] = ref[pl.ds(0, count)]
        second_ref[pl.ds(half * count, count)] = ref[pl.ds(count, count)]


def split_kernel(kept_ref, came_ref, own_ref, other_ref):
    for half, ref in enumerate((kept_ref, came_ref)):
        for orbital in (0, 1):
            own_ref[2 * orbital + half] = ref[2 * orbital]
            other_ref[2 * orbital + half] = ref[2 * orbital + 1]


def gather_sums(run, width, columns, distance, own_ref, x_ref, xy_ref, y_ref, *refs):
    out_ref, tiles_ref = refs
    depth = own_ref.shape[0]
    band, here = lax.axis_index("band"), lax.axis_index("grid")
    z, x = here // 2, here % 2
    tiles_ref[0, 0] = own_ref[...]
    tiles_ref[0, 1] = x_ref[...]
    tiles_ref[1, 0] = y_ref[...]
    tiles_ref[1, 1] = xy_ref[...]
    wanted = out_ref.shape[0]
    holders = wanted // columns
    sublane = lax.broadcasted_iota(jnp.int32, (wanted, LANES), 0)
    block = band ^ distance
    acc = [jnp.zeros((wanted, LANES), jnp.float32) for _ in range(run)]
    for dy in (0, 1):
        lines = jnp.zeros((wanted, LANES), jnp.float32)
        for k in range(holders):
            holder = block * holders + k
            line = tiles_ref[dy, x ^ (holder % 2), z ^ (holder // 2), pl.ds(run, 1), :]
            lines = jnp.where(sublane // columns == k, jnp.broadcast_to(line, (wanted, LANES)), lines)
        for dx in (0, 1):
            for dz in range(depth):
                weight = jnp.take_along_axis(lines, sublane % columns * width + (here ^ (2 * dz + dx)), axis=1)
                for y in range(run):
                    acc[y] = acc[y] + weight * tiles_ref[dy, dx, dz, pl.ds(y, 1), :]
    for y in range(run):
        out_ref[:, pl.ds(y * LANES, LANES)] = acc[y]


def sum_kernel(*refs):
    refs[-1][...] = functools.reduce(jnp.add, [ref[...] for ref in refs[:-1]])


def swap(value, axis, size, distance):
    return lax.ppermute(value, axis, [(place, place ^ distance) for place in range(size)])


def shards(nb, ng, orbitals, region, potential_table, counts, ritz):
    _, planes, ys, xs = orbitals.shape
    cells = planes * ys * xs
    panel, columns = ritz.shape
    run = cells // ng // xs
    width = 1
    while width < panel:
        width *= 2
    per_row = LANES // width
    ritz_rows = -(-columns // per_row)
    rows = -(-(run + ritz_rows) // SUBLANES) * SUBLANES
    cores = 2 if nb % 2 == 0 else 1
    chips = nb // cores * ng
    vmem = pl.BlockSpec(memory_space=pltpu.VMEM)
    hbm = pl.BlockSpec(memory_space=pltpu.HBM)
    inputs = [
        pltpu.with_memory_space_constraint(value, pltpu.HBM)
        for value in (
            jnp.transpose(orbitals[0], (1, 0, 2)), jnp.transpose(region, (1, 0, 2)), potential_table, counts, ritz.T
        )
    ]
    scratch = [
        pltpu.VMEM((ys, planes, xs), jnp.float32),
        pltpu.VMEM((ys, planes, xs), jnp.int32),
        pltpu.SMEM(potential_table.shape, jnp.float32),
        pltpu.SMEM(counts.shape, jnp.int32),
        pltpu.VMEM((columns, panel), jnp.float32),
        pltpu.SemaphoreType.DMA((5,)),
        pltpu.VMEM((ng * rows, LANES), jnp.float32),
    ]
    limit = pltpu.CompilerParams(vmem_limit_bytes=8 * chips * rows * LANES + 64 * cells + 2**20)
    small = pltpu.CompilerParams(vmem_limit_bytes=2**21)
    sum_shape = jax.ShapeDtypeStruct((panel, run * LANES), jnp.float32)
    terms = []

    if (nb, ng, panel) == (4, 8, 8) and columns * width <= LANES and rows == SUBLANES:
        depth = ng // 2
        four = [jax.ShapeDtypeStruct((depth, rows, LANES), jnp.float32)] * 2
        near, far = pl.pallas_call(
            functools.partial(filter_to_lines, rows, run, width),
            out_shape=four,
            in_specs=[hbm] * 5,
            out_specs=[vmem] * 2,
            scratch_shapes=scratch,
            compiler_params=limit,
            name="chebyshev_filter",
        )(*inputs)

        def repack(kernel, kept, came):
            return pl.pallas_call(
                kernel, out_shape=four, in_specs=[vmem] * 2, out_specs=[vmem] * 2, compiler_params=small, name="repack"
            )(kept, came)

        near, far = repack(turn_kernel, near, swap(far, "grid", ng, 4))
        own, other = repack(split_kernel, near, swap(far, "grid", ng, 2))
        tiles = [
            own,
            swap(other, "grid", ng, 1),
            swap(other, ("band", "grid"), nb * ng, 2 * ng + 1),
            swap(own, "band", nb, 2),
        ]

        def partial_sums(distance):
            return pl.pallas_call(
                functools.partial(gather_sums, run, width, columns, distance),
                out_shape=sum_shape,
                in_specs=[vmem] * 4,
                out_specs=vmem,
                scratch_shapes=[pltpu.VMEM((2, 2, depth, rows, LANES), jnp.float32)],
                compiler_params=small,
                name="ritz_partial_sums",
            )(*tiles)
    else:
        order = list(range(chips))[::-1]
        groups = [[(chip // ng * cores + core) * ng + chip % ng for chip in order] for core in range(cores)]
        packed = pl.pallas_call(
            functools.partial(filter_to_all, rows, run, width, order),
            out_shape=jax.ShapeDtypeStruct((chips * rows, LANES), jnp.float32),
            in_specs=[hbm] * 5,
            out_specs=vmem,
            scratch_shapes=scratch,
            compiler_params=limit,
            name="chebyshev_filter",
        )(*inputs)
        got = lax.all_to_all(
            packed.reshape(chips, rows, LANES), ("band", "grid"), split_axis=0, concat_axis=0, tiled=True,
            axis_index_groups=groups,
        )
        by_source = got[::-1].reshape(nb // cores, ng, rows, LANES)
        fields = by_source[:, :, :run].reshape(chips, run * LANES)
        blocks = by_source[:, :, run : run + ritz_rows].reshape(nb // cores, ng, ritz_rows * per_row, width)

        def partial_sums(distance):
            holders = panel // columns
            mine = lax.dynamic_slice_in_dim(blocks, (lax.axis_index("band") ^ distance) * holders, holders, axis=1)
            return lax.dot_general(
                jnp.transpose(mine[:, :, :columns, :panel], (0, 3, 1, 2)).reshape(chips, panel),
                fields,
                (((0,), (0,)), ((), ())),
                precision=lax.Precision.HIGHEST,
                preferred_element_type=jnp.float32,
            )

    if cores == 2:
        terms.append(lax.ppermute(partial_sums(1), "band", [(band, band ^ 1) for band in range(nb)]))
    terms.append(partial_sums(0))
    return pl.pallas_call(
        sum_kernel,
        out_shape=sum_shape,
        in_specs=[vmem] * cores,
        out_specs=vmem,
        compiler_params=pltpu.CompilerParams(vmem_limit_bytes=4 * (cores + 1) * panel * run * LANES + 2**20),
        name="core_sum",
    )(*terms)


def solution(mesh):
    return jax.shard_map(
        functools.partial(shards, mesh.shape["band"], mesh.shape["grid"]),
        mesh=mesh,
        in_specs=(P(("band", "grid"), None, None, None), P(), P(), P(), P("band", "grid")),
        out_specs=P("band", "grid"),
        check_vma=False,
    )
```

```python
import functools

import jax
import jax.numpy as jnp
from jax import lax
from jax.experimental import pallas as pl
from jax.experimental.pallas import tpu as pltpu
from jax.sharding import PartitionSpec as P

DEGREE = 4

COEFFICIENTS = (
    -5369.0 / 1800.0,
    12.0 / 7.0,
    -15.0 / 56.0,
    10.0 / 189.0,
    -1.0 / 112.0,
    2.0 / 1925.0,
    -1.0 / 16632.0,
)
SPACING = 0.5
LOWER = 6.0
UPPER = 46.0
HALF = (UPPER - LOWER) / 2.0
CENTRE = (UPPER + LOWER) / 2.0
LANES = 128
SUBLANES = 8


def ring_weights(length):
    weights = [0.0] * length
    for offset in range(1, 7):
        weights[offset % length] += COEFFICIENTS[offset]
        weights[-offset % length] += COEFFICIENTS[offset]
    return weights


def pair_weights(length):
    weights = ring_weights(length)
    pairs = []
    for distance in range(1, length // 2 + 1):
        if weights[distance] != 0.0:
            pairs.append((sorted({distance, length - distance}), weights[distance]))
    return weights[0], pairs


def apply(field, diagonal, hop, before):
    ys = len(field)
    planes, xs = field[0].shape
    along_y, along_planes, along_x = [pair_weights(length)[1] for length in (ys, planes, xs)]
    results = []
    for y in range(ys):
        tile = field[y]
        total = diagonal[y] * tile
        if before is not None:
            total = total - before[y]
        for shifts, weight in along_y:
            total = total + (hop * weight) * functools.reduce(jnp.add, [field[(y - shift) % ys] for shift in shifts])
        for pairs, axis in ((along_planes, 0), (along_x, 1)):
            for shifts, weight in pairs:
                total = total + (hop * weight) * functools.reduce(
                    jnp.add, [pltpu.roll(tile, shift, axis) for shift in shifts]
                )
        results.append(total)
    return results


def filter_kernel(ng, copies, rows, run, width, cores, order, *refs):
    sources, out_ref, held, sems, natural_ref = refs[:5], refs[5], refs[6:11], refs[11], refs[12]
    orb_ref, region_ref, table_ref, counts_ref, ritz_ref = held
    transfers = [
        pltpu.make_async_copy(source, target, sems.at[index])
        for index, (source, target) in enumerate(zip(sources, held))
    ]
    for transfer in transfers:
        transfer.start()
    for transfer in transfers:
        transfer.wait()
    ys, planes, xs = orb_ref.shape
    columns, panel = ritz_ref.shape
    per_row = LANES // width
    for row in range(-(-columns // per_row)):
        line = jnp.zeros((1, LANES), jnp.float32)
        for slot in range(min(per_row, columns - row * per_row)):
            piece = jnp.concatenate(
                [ritz_ref[pl.ds(row * per_row + slot, 1), :], jnp.zeros((1, LANES - panel), jnp.float32)], axis=1
            )
            line = line + (pltpu.roll(piece, slot * width, 1) if slot else piece)
        natural_ref[pl.ds(run + row, ng, stride=rows), :] = jnp.broadcast_to(line, (ng, LANES))

    centre_weight = 3.0 * COEFFICIENTS[0] + sum(pair_weights(n)[0] for n in (planes, ys, xs))
    scale = 2.0 / HALF
    hop = -0.5 / (SPACING * SPACING) * scale
    diagonal = []
    for y in range(ys):
        region = region_ref[y]
        potential = jnp.zeros((planes, xs), jnp.float32)
        for index in range(table_ref.shape[0]):
            potential = jnp.where(region == index, table_ref[index], potential)
        diagonal.append(scale * potential + (hop * centre_weight - scale * CENTRE))
    band_pos = lax.axis_index("row") * cores + lax.axis_index("core")
    live = (lax.axis_index("grid") < counts_ref[band_pos]).astype(jnp.float32)
    previous = [live * orb_ref[y] for y in range(ys)]
    current = apply(previous, [0.5 * value for value in diagonal], 0.5 * hop, None)
    for _ in range(DEGREE - 1):
        previous, current = current, apply(current, diagonal, hop, previous)

    blocks = ys // run
    for y in range(ys):
        natural_ref[pl.ds((y // run) * rows + y % run, planes, stride=blocks * rows), :] = current[y]
    for copy in range(copies):
        for tile in range(ng):
            place = order.index(copy * ng + tile)
            out_ref[pl.ds(place * rows, rows), :] = natural_ref[pl.ds(tile * rows, rows), :]


def partial_kernel(nrow, ng, run, width, columns, cores, order, distance, got_ref, out_ref, ritz_ref):
    for place, source in enumerate(order):
        ritz_ref[source] = got_ref[place, pl.ds(run, 1), :]
    wanted = out_ref.shape[0]
    holders = wanted // columns
    sublane = lax.broadcasted_iota(jnp.int32, (wanted, LANES), 0)
    block = lax.axis_index("row") * cores + lax.rem(lax.axis_index("core") + distance, cores)
    acc = [jnp.zeros((wanted, LANES), jnp.float32) for _ in range(run)]
    for row in range(nrow):
        lines = jnp.zeros((wanted, LANES), jnp.float32)
        for k in range(holders):
            line = ritz_ref[row * ng + block * holders + k]
            lines = jnp.where(sublane // columns == k, jnp.broadcast_to(line, (wanted, LANES)), lines)
        for r in range(ng):
            weight = jnp.take_along_axis(lines, sublane % columns * width + r, axis=1)
            for y in range(run):
                acc[y] = acc[y] + weight * got_ref[order.index(row * ng + r), pl.ds(y, 1), :]
    for y in range(run):
        out_ref[:, pl.ds(y * LANES, LANES)] = acc[y]


def shards(nrow, cores, ng, orbitals, region, potential_table, counts, ritz):
    _, planes, ys, xs = orbitals.shape
    cells = planes * ys * xs
    panel, columns = ritz.shape
    run = cells // ng // xs
    width = 1
    while width < panel:
        width *= 2
    per_row = LANES // width
    ritz_rows = -(-columns // per_row)
    rows = -(-(run + ritz_rows) // SUBLANES) * SUBLANES
    tiles = nrow * ng
    vmem = pl.BlockSpec(memory_space=pltpu.VMEM)
    hbm = pl.BlockSpec(memory_space=pltpu.HBM)
    inputs = [
        pltpu.with_memory_space_constraint(value, pltpu.HBM)
        for value in (
            jnp.transpose(orbitals[0], (1, 0, 2)), jnp.transpose(region, (1, 0, 2)), potential_table, counts, ritz.T
        )
    ]
    late = sorted(range(tiles), key=lambda place: (place % ng // (ng // 2), place // ng, place % ng), reverse=True)
    order = [place for pair in zip(late, late[::-1]) for place in pair][:tiles]
    packed_bytes = 4 * tiles * rows * LANES
    packed = pl.pallas_call(
        functools.partial(filter_kernel, ng, nrow, rows, run, width, cores, order),
        out_shape=jax.ShapeDtypeStruct((tiles * rows, LANES), jnp.float32),
        in_specs=[hbm] * 5,
        out_specs=vmem,
        scratch_shapes=[
            pltpu.VMEM((ys, planes, xs), jnp.float32),
            pltpu.VMEM((ys, planes, xs), jnp.int32),
            pltpu.SMEM(potential_table.shape, jnp.float32),
            pltpu.SMEM(counts.shape, jnp.int32),
            pltpu.VMEM((columns, panel), jnp.float32),
            pltpu.SemaphoreType.DMA((5,)),
            pltpu.VMEM((ng * rows, LANES), jnp.float32),
        ],
        compiler_params=pltpu.CompilerParams(vmem_limit_bytes=2 * packed_bytes + 64 * cells + 2**20),
        name="chebyshev_filter",
    )(*inputs)
    got = lax.all_to_all(
        packed.reshape(tiles, rows, LANES), ("row", "grid"), split_axis=0, concat_axis=0, tiled=True,
        axis_index_groups=[order],
    )
    sum_shape = jax.ShapeDtypeStruct((panel, run * LANES), jnp.float32)
    if columns * width <= LANES and tiles <= 64 and panel == ng and panel <= 16:
        def partial_sums(distance):
            return pl.pallas_call(
                functools.partial(partial_kernel, nrow, ng, run, width, columns, cores, order, distance),
                out_shape=sum_shape,
                in_specs=[vmem],
                out_specs=vmem,
                scratch_shapes=[pltpu.VMEM((tiles, 1, LANES), jnp.float32)],
                compiler_params=pltpu.CompilerParams(vmem_limit_bytes=packed_bytes + 2**20),
                name="ritz_partial_sums",
            )(got)

    else:
        holders = panel // columns
        by_source = got[jnp.argsort(jnp.array(order))].reshape(nrow, ng, rows, LANES)
        fields = by_source[:, :, :run].reshape(tiles, run * LANES)
        blocks = by_source[:, :, run : run + ritz_rows].reshape(nrow, ng, ritz_rows * per_row, width)

        def partial_sums(distance):
            block = lax.axis_index("row") * cores + lax.rem(lax.axis_index("core") + distance, cores)
            mine = lax.dynamic_slice_in_dim(blocks, block * holders, holders, axis=1)
            return lax.dot_general(
                jnp.transpose(mine[:, :, :columns, :panel], (0, 3, 1, 2)).reshape(tiles, panel),
                fields,
                (((0,), (0,)), ((), ())),
                precision=lax.Precision.HIGHEST,
                preferred_element_type=jnp.float32,
            )

    terms = []
    for distance in range(1, cores):
        pairs = [(core, (core + distance) % cores) for core in range(cores)]
        terms.append(lax.ppermute(partial_sums(distance), "core", pairs))
    terms.append(partial_sums(0))
    return functools.reduce(jnp.add, terms)


def solution(mesh):
    bands, ng = mesh.shape["band"], mesh.shape["grid"]
    cores = 2 if bands % 2 == 0 else 1
    nrow = bands // cores
    split = jax.sharding.Mesh(mesh.devices.reshape(nrow, cores, ng), ("row", "core", "grid"))
    return jax.shard_map(
        functools.partial(shards, nrow, cores, ng),
        mesh=split,
        in_specs=(P(("row", "core", "grid"), None, None, None), P(), P(), P(), P(("row", "core"), "grid")),
        out_specs=P(("row", "core"), "grid"),
        check_vma=False,
    )
```

```python
import functools

import jax
import jax.numpy as jnp
from jax import lax
from jax.experimental import pallas as pl
from jax.experimental.pallas import tpu as pltpu
from jax.sharding import PartitionSpec as P

DEGREE = 4

COEFFICIENTS = (
    -5369.0 / 1800.0,
    12.0 / 7.0,
    -15.0 / 56.0,
    10.0 / 189.0,
    -1.0 / 112.0,
    2.0 / 1925.0,
    -1.0 / 16632.0,
)
SPACING = 0.5
LOWER = 6.0
UPPER = 46.0
HALF = (UPPER - LOWER) / 2.0
CENTRE = (UPPER + LOWER) / 2.0
LANES = 128
SUBLANES = 8


def ring_weights(length):
    weights = [0.0] * length
    for offset in range(1, 7):
        weights[offset % length] += COEFFICIENTS[offset]
        weights[-offset % length] += COEFFICIENTS[offset]
    return weights


def pair_weights(length):
    weights = ring_weights(length)
    pairs = []
    for distance in range(1, length // 2 + 1):
        if weights[distance] != 0.0:
            pairs.append((sorted({distance, length - distance}), weights[distance]))
    return weights[0], pairs


def apply(field, diagonal, hop, before):
    ys = len(field)
    planes, xs = field[0].shape
    along_y, along_planes, along_x = [pair_weights(length)[1] for length in (ys, planes, xs)]
    results = []
    for y in range(ys):
        tile = field[y]
        total = diagonal[y] * tile
        if before is not None:
            total = total - before[y]
        for shifts, weight in along_y:
            total = total + (hop * weight) * functools.reduce(jnp.add, [field[(y - shift) % ys] for shift in shifts])
        for pairs, axis in ((along_planes, 0), (along_x, 1)):
            for shifts, weight in pairs:
                total = total + (hop * weight) * functools.reduce(
                    jnp.add, [pltpu.roll(tile, shift, axis) for shift in shifts]
                )
        results.append(total)
    return results


def place_of(chip, order):
    place = order.index(chip)
    if place == 0:
        return place
    return jnp.where(lax.axis_index("core") == 0, place, len(order) - place)


def filter_kernel(ng, copies, rows, run, width, cores, order, *refs):
    sources, out_ref, held, sems, natural_ref = refs[:5], refs[5], refs[6:11], refs[11], refs[12]
    orb_ref, region_ref, table_ref, counts_ref, ritz_ref = held
    transfers = [
        pltpu.make_async_copy(source, target, sems.at[index])
        for index, (source, target) in enumerate(zip(sources, held))
    ]
    for transfer in transfers:
        transfer.start()
    for transfer in transfers:
        transfer.wait()
    ys, planes, xs = orb_ref.shape
    columns, panel = ritz_ref.shape
    per_row = LANES // width
    for row in range(-(-columns // per_row)):
        line = jnp.zeros((1, LANES), jnp.float32)
        for slot in range(min(per_row, columns - row * per_row)):
            piece = jnp.concatenate(
                [ritz_ref[pl.ds(row * per_row + slot, 1), :], jnp.zeros((1, LANES - panel), jnp.float32)], axis=1
            )
            line = line + (pltpu.roll(piece, slot * width, 1) if slot else piece)
        natural_ref[pl.ds(run + row, ng, stride=rows), :] = jnp.broadcast_to(line, (ng, LANES))

    centre_weight = 3.0 * COEFFICIENTS[0] + sum(pair_weights(n)[0] for n in (planes, ys, xs))
    scale = 2.0 / HALF
    hop = -0.5 / (SPACING * SPACING) * scale
    diagonal = []
    for y in range(ys):
        region = region_ref[y]
        potential = jnp.zeros((planes, xs), jnp.float32)
        for index in range(table_ref.shape[0]):
            potential = jnp.where(region == index, table_ref[index], potential)
        diagonal.append(scale * potential + (hop * centre_weight - scale * CENTRE))
    band_pos = lax.axis_index("row") * cores + lax.axis_index("core")
    live = (lax.axis_index("grid") < counts_ref[band_pos]).astype(jnp.float32)
    previous = [live * orb_ref[y] for y in range(ys)]
    current = apply(previous, [0.5 * value for value in diagonal], 0.5 * hop, None)
    for _ in range(DEGREE - 1):
        previous, current = current, apply(current, diagonal, hop, previous)

    blocks = ys // run
    for y in range(ys):
        natural_ref[pl.ds((y // run) * rows + y % run, planes, stride=blocks * rows), :] = current[y]
    for copy in range(copies):
        for tile in range(ng):
            start = pl.multiple_of(place_of(copy * ng + tile, order) * rows, rows)
            out_ref[pl.ds(start, rows), :] = natural_ref[pl.ds(tile * rows, rows), :]


def partial_kernel(nrow, ng, run, width, columns, cores, order, distance, got_ref, out_ref, ritz_ref):
    places = [place_of(chip, order) for chip in range(nrow * ng)]
    for chip, place in enumerate(places):
        ritz_ref[chip] = got_ref[place, pl.ds(run, 1), :]
    wanted = out_ref.shape[0]
    holders = wanted // columns
    sublane = lax.broadcasted_iota(jnp.int32, (wanted, LANES), 0)
    block = lax.axis_index("row") * cores + lax.rem(lax.axis_index("core") + distance, cores)
    acc = [jnp.zeros((wanted, LANES), jnp.float32) for _ in range(run)]
    for row in range(nrow):
        lines = jnp.zeros((wanted, LANES), jnp.float32)
        for k in range(holders):
            line = ritz_ref[row * ng + block * holders + k]
            lines = jnp.where(sublane // columns == k, jnp.broadcast_to(line, (wanted, LANES)), lines)
        for r in range(ng):
            weight = jnp.take_along_axis(lines, sublane % columns * width + r, axis=1)
            for y in range(run):
                acc[y] = acc[y] + weight * got_ref[places[row * ng + r], pl.ds(y, 1), :]
    for y in range(run):
        out_ref[:, pl.ds(y * LANES, LANES)] = acc[y]


def shards(nrow, cores, ng, orbitals, region, potential_table, counts, ritz):
    _, planes, ys, xs = orbitals.shape
    cells = planes * ys * xs
    panel, columns = ritz.shape
    run = cells // ng // xs
    width = 1
    while width < panel:
        width *= 2
    per_row = LANES // width
    ritz_rows = -(-columns // per_row)
    rows = -(-(run + ritz_rows) // SUBLANES) * SUBLANES
    tiles = nrow * ng
    vmem = pl.BlockSpec(memory_space=pltpu.VMEM)
    hbm = pl.BlockSpec(memory_space=pltpu.HBM)
    inputs = [
        pltpu.with_memory_space_constraint(value, pltpu.HBM)
        for value in (
            jnp.transpose(orbitals[0], (1, 0, 2)), jnp.transpose(region, (1, 0, 2)), potential_table, counts, ritz.T
        )
    ]
    late = sorted(range(tiles), key=lambda place: (place % ng // (ng // 2), place // ng, place % ng), reverse=True)
    order = [place for pair in zip(late, late[::-1]) for place in pair][:tiles]
    packed_bytes = 4 * tiles * rows * LANES
    packed = pl.pallas_call(
        functools.partial(filter_kernel, ng, nrow, rows, run, width, cores, order),
        out_shape=jax.ShapeDtypeStruct((tiles * rows, LANES), jnp.float32),
        in_specs=[hbm] * 5,
        out_specs=vmem,
        scratch_shapes=[
            pltpu.VMEM((ys, planes, xs), jnp.float32),
            pltpu.VMEM((ys, planes, xs), jnp.int32),
            pltpu.SMEM(potential_table.shape, jnp.float32),
            pltpu.SMEM(counts.shape, jnp.int32),
            pltpu.VMEM((columns, panel), jnp.float32),
            pltpu.SemaphoreType.DMA((5,)),
            pltpu.VMEM((ng * rows, LANES), jnp.float32),
        ],
        compiler_params=pltpu.CompilerParams(vmem_limit_bytes=2 * packed_bytes + 64 * cells + 2**20),
        name="chebyshev_filter",
    )(*inputs)
    got = lax.all_to_all(
        packed.reshape(tiles, rows, LANES), ("row", "core", "grid"), split_axis=0, concat_axis=0, tiled=True,
        axis_index_groups=[
            [(chip // ng * cores + core) * ng + chip % ng for chip in (order[:1] + order[:0:-1] if core else order)]
            for core in range(cores)
        ],
    )
    sum_shape = jax.ShapeDtypeStruct((panel, run * LANES), jnp.float32)
    if columns * width <= LANES and tiles <= 64 and panel == ng and panel <= 16:
        def partial_sums(distance):
            return pl.pallas_call(
                functools.partial(partial_kernel, nrow, ng, run, width, columns, cores, order, distance),
                out_shape=sum_shape,
                in_specs=[vmem],
                out_specs=vmem,
                scratch_shapes=[pltpu.VMEM((tiles, 1, LANES), jnp.float32)],
                compiler_params=pltpu.CompilerParams(vmem_limit_bytes=packed_bytes + 2**20),
                name="ritz_partial_sums",
            )(got)

    else:
        holders = panel // columns
        by_source = got[jnp.stack([place_of(chip, order) for chip in range(tiles)])].reshape(nrow, ng, rows, LANES)
        fields = by_source[:, :, :run].reshape(tiles, run * LANES)
        blocks = by_source[:, :, run : run + ritz_rows].reshape(nrow, ng, ritz_rows * per_row, width)

        def partial_sums(distance):
            block = lax.axis_index("row") * cores + lax.rem(lax.axis_index("core") + distance, cores)
            mine = lax.dynamic_slice_in_dim(blocks, block * holders, holders, axis=1)
            return lax.dot_general(
                jnp.transpose(mine[:, :, :columns, :panel], (0, 3, 1, 2)).reshape(tiles, panel),
                fields,
                (((0,), (0,)), ((), ())),
                precision=lax.Precision.HIGHEST,
                preferred_element_type=jnp.float32,
            )

    terms = []
    for distance in range(1, cores):
        pairs = [(core, (core + distance) % cores) for core in range(cores)]
        terms.append(lax.ppermute(partial_sums(distance), "core", pairs))
    terms.append(partial_sums(0))
    return functools.reduce(jnp.add, terms)


def solution(mesh):
    bands, ng = mesh.shape["band"], mesh.shape["grid"]
    cores = 2 if bands % 2 == 0 else 1
    nrow = bands // cores
    split = jax.sharding.Mesh(mesh.devices.reshape(nrow, cores, ng), ("row", "core", "grid"))
    return jax.shard_map(
        functools.partial(shards, nrow, cores, ng),
        mesh=split,
        in_specs=(P(("row", "core", "grid"), None, None, None), P(), P(), P(), P(("row", "core"), "grid")),
        out_specs=P(("row", "core"), "grid"),
        check_vma=False,
    )
```

```python
import functools

import jax
import jax.numpy as jnp
from jax import lax
from jax.experimental import pallas as pl
from jax.experimental.pallas import tpu as pltpu
from jax.sharding import PartitionSpec as P

DEGREE = 4

COEFFICIENTS = (
    -5369.0 / 1800.0,
    12.0 / 7.0,
    -15.0 / 56.0,
    10.0 / 189.0,
    -1.0 / 112.0,
    2.0 / 1925.0,
    -1.0 / 16632.0,
)
SPACING = 0.5
LOWER = 6.0
UPPER = 46.0
HALF = (UPPER - LOWER) / 2.0
CENTRE = (UPPER + LOWER) / 2.0
LANES = 128
SUBLANES = 8


def ring_weights(length):
    weights = [0.0] * length
    for offset in range(1, 7):
        weights[offset % length] += COEFFICIENTS[offset]
        weights[-offset % length] += COEFFICIENTS[offset]
    return weights


def pair_weights(length):
    weights = ring_weights(length)
    pairs = []
    for distance in range(1, length // 2 + 1):
        if weights[distance] != 0.0:
            pairs.append((sorted({distance, length - distance}), weights[distance]))
    return weights[0], pairs


def apply(field, diagonal, hop, before):
    ys = len(field)
    planes, xs = field[0].shape
    along_y, along_planes, along_x = [pair_weights(length)[1] for length in (ys, planes, xs)]
    results = []
    for y in range(ys):
        tile = field[y]
        total = diagonal[y] * tile
        if before is not None:
            total = total - before[y]
        for shifts, weight in along_y:
            total = total + (hop * weight) * functools.reduce(jnp.add, [field[(y - shift) % ys] for shift in shifts])
        for pairs, axis in ((along_planes, 0), (along_x, 1)):
            for shifts, weight in pairs:
                total = total + (hop * weight) * functools.reduce(
                    jnp.add, [pltpu.roll(tile, shift, axis) for shift in shifts]
                )
        results.append(total)
    return results


def filter_kernel(ng, copies, rows, run, width, cores, order, *refs):
    sources, out_ref, held, sems, natural_ref = refs[:5], refs[5], refs[6:11], refs[11], refs[12]
    orb_ref, region_ref, table_ref, counts_ref, ritz_ref = held
    transfers = [
        pltpu.make_async_copy(source, target, sems.at[index])
        for index, (source, target) in enumerate(zip(sources, held))
    ]
    for transfer in transfers:
        transfer.start()
    for transfer in transfers:
        transfer.wait()
    ys, planes, xs = orb_ref.shape
    columns, panel = ritz_ref.shape
    per_row = LANES // width
    for row in range(-(-columns // per_row)):
        line = jnp.zeros((1, LANES), jnp.float32)
        for slot in range(min(per_row, columns - row * per_row)):
            piece = jnp.concatenate(
                [ritz_ref[pl.ds(row * per_row + slot, 1), :], jnp.zeros((1, LANES - panel), jnp.float32)], axis=1
            )
            line = line + (pltpu.roll(piece, slot * width, 1) if slot else piece)
        natural_ref[pl.ds(run + row, ng, stride=rows), :] = jnp.broadcast_to(line, (ng, LANES))

    centre_weight = 3.0 * COEFFICIENTS[0] + sum(pair_weights(n)[0] for n in (planes, ys, xs))
    scale = 2.0 / HALF
    hop = -0.5 / (SPACING * SPACING) * scale
    diagonal = []
    for y in range(ys):
        region = region_ref[y]
        potential = jnp.zeros((planes, xs), jnp.float32)
        for index in range(table_ref.shape[0]):
            potential = jnp.where(region == index, table_ref[index], potential)
        diagonal.append(scale * potential + (hop * centre_weight - scale * CENTRE))
    band_pos = lax.axis_index("row") * cores + lax.axis_index("core")
    live = (lax.axis_index("grid") < counts_ref[band_pos]).astype(jnp.float32)
    previous = [live * orb_ref[y] for y in range(ys)]
    current = apply(previous, [0.5 * value for value in diagonal], 0.5 * hop, None)
    for _ in range(DEGREE - 1):
        previous, current = current, apply(current, diagonal, hop, previous)

    blocks = ys // run
    for y in range(ys):
        natural_ref[pl.ds((y // run) * rows + y % run, planes, stride=blocks * rows), :] = current[y]
    for copy in range(copies):
        for tile in range(ng):
            place = order.index(copy * ng + tile)
            out_ref[pl.ds(place * rows, rows), :] = natural_ref[pl.ds(tile * rows, rows), :]


def partial_kernel(nrow, ng, run, width, columns, cores, order, distance, got_ref, out_ref, ritz_ref):
    for place, source in enumerate(order):
        ritz_ref[source] = got_ref[place, pl.ds(run, 1), :]
    wanted = out_ref.shape[0]
    holders = wanted // columns
    sublane = lax.broadcasted_iota(jnp.int32, (wanted, LANES), 0)
    block = lax.axis_index("row") * cores + lax.rem(lax.axis_index("core") + distance, cores)
    acc = [jnp.zeros((wanted, LANES), jnp.float32) for _ in range(run)]
    for row in range(nrow):
        lines = jnp.zeros((wanted, LANES), jnp.float32)
        for k in range(holders):
            line = ritz_ref[row * ng + block * holders + k]
            lines = jnp.where(sublane // columns == k, jnp.broadcast_to(line, (wanted, LANES)), lines)
        for r in range(ng):
            weight = jnp.take_along_axis(lines, sublane % columns * width + r, axis=1)
            for y in range(run):
                acc[y] = acc[y] + weight * got_ref[order.index(row * ng + r), pl.ds(y, 1), :]
    for y in range(run):
        out_ref[:, pl.ds(y * LANES, LANES)] = acc[y]


def shards(nrow, cores, ng, orbitals, region, potential_table, counts, ritz):
    _, planes, ys, xs = orbitals.shape
    cells = planes * ys * xs
    panel, columns = ritz.shape
    run = cells // ng // xs
    width = 1
    while width < panel:
        width *= 2
    per_row = LANES // width
    ritz_rows = -(-columns // per_row)
    rows = -(-(run + ritz_rows) // SUBLANES) * SUBLANES
    tiles = nrow * ng
    vmem = pl.BlockSpec(memory_space=pltpu.VMEM)
    hbm = pl.BlockSpec(memory_space=pltpu.HBM)
    inputs = [
        pltpu.with_memory_space_constraint(value, pltpu.HBM)
        for value in (
            jnp.transpose(orbitals[0], (1, 0, 2)), jnp.transpose(region, (1, 0, 2)), potential_table, counts, ritz.T
        )
    ]
    order = [tiles - 1] + sorted(range(tiles - 1), key=lambda chip: (chip % ng // 2, chip))
    packed_bytes = 4 * tiles * rows * LANES
    packed = pl.pallas_call(
        functools.partial(filter_kernel, ng, nrow, rows, run, width, cores, order),
        out_shape=jax.ShapeDtypeStruct((tiles * rows, LANES), jnp.float32),
        in_specs=[hbm] * 5,
        out_specs=vmem,
        scratch_shapes=[
            pltpu.VMEM((ys, planes, xs), jnp.float32),
            pltpu.VMEM((ys, planes, xs), jnp.int32),
            pltpu.SMEM(potential_table.shape, jnp.float32),
            pltpu.SMEM(counts.shape, jnp.int32),
            pltpu.VMEM((columns, panel), jnp.float32),
            pltpu.SemaphoreType.DMA((5,)),
            pltpu.VMEM((ng * rows, LANES), jnp.float32),
        ],
        compiler_params=pltpu.CompilerParams(vmem_limit_bytes=2 * packed_bytes + 64 * cells + 2**20),
        name="chebyshev_filter",
    )(*inputs)
    got = lax.all_to_all(
        packed.reshape(tiles, rows, LANES), ("row", "grid"), split_axis=0, concat_axis=0, tiled=True,
        axis_index_groups=[order],
    )
    sum_shape = jax.ShapeDtypeStruct((panel, run * LANES), jnp.float32)
    if columns * width <= LANES and tiles <= 64 and panel == ng and panel <= 16:
        def partial_sums(distance):
            return pl.pallas_call(
                functools.partial(partial_kernel, nrow, ng, run, width, columns, cores, order, distance),
                out_shape=sum_shape,
                in_specs=[vmem],
                out_specs=vmem,
                scratch_shapes=[pltpu.VMEM((tiles, 1, LANES), jnp.float32)],
                compiler_params=pltpu.CompilerParams(vmem_limit_bytes=packed_bytes + 2**20),
                name="ritz_partial_sums",
            )(got)

    else:
        holders = panel // columns
        by_source = got[jnp.argsort(jnp.array(order))].reshape(nrow, ng, rows, LANES)
        fields = by_source[:, :, :run].reshape(tiles, run * LANES)
        blocks = by_source[:, :, run : run + ritz_rows].reshape(nrow, ng, ritz_rows * per_row, width)

        def partial_sums(distance):
            block = lax.axis_index("row") * cores + lax.rem(lax.axis_index("core") + distance, cores)
            mine = lax.dynamic_slice_in_dim(blocks, block * holders, holders, axis=1)
            return lax.dot_general(
                jnp.transpose(mine[:, :, :columns, :panel], (0, 3, 1, 2)).reshape(tiles, panel),
                fields,
                (((0,), (0,)), ((), ())),
                precision=lax.Precision.HIGHEST,
                preferred_element_type=jnp.float32,
            )

    terms = []
    for distance in range(1, cores):
        pairs = [(core, (core + distance) % cores) for core in range(cores)]
        terms.append(lax.ppermute(partial_sums(distance), "core", pairs))
    terms.append(partial_sums(0))
    return functools.reduce(jnp.add, terms)


def solution(mesh):
    bands, ng = mesh.shape["band"], mesh.shape["grid"]
    cores = 2 if bands % 2 == 0 else 1
    nrow = bands // cores
    split = jax.sharding.Mesh(mesh.devices.reshape(nrow, cores, ng), ("row", "core", "grid"))
    return jax.shard_map(
        functools.partial(shards, nrow, cores, ng),
        mesh=split,
        in_specs=(P(("row", "core", "grid"), None, None, None), P(), P(), P(), P(("row", "core"), "grid")),
        out_specs=P(("row", "core"), "grid"),
        check_vma=False,
    )
```

```python
import functools

import jax
import jax.numpy as jnp
from jax import lax
from jax.experimental import pallas as pl
from jax.experimental.pallas import tpu as pltpu
from jax.sharding import PartitionSpec as P

DEGREE = 4

COEFFICIENTS = (
    -5369.0 / 1800.0,
    12.0 / 7.0,
    -15.0 / 56.0,
    10.0 / 189.0,
    -1.0 / 112.0,
    2.0 / 1925.0,
    -1.0 / 16632.0,
)
SPACING = 0.5
LOWER = 6.0
UPPER = 46.0
HALF = (UPPER - LOWER) / 2.0
CENTRE = (UPPER + LOWER) / 2.0
LANES = 128
SUBLANES = 8


def ring_weights(length):
    weights = [0.0] * length
    for offset in range(1, 7):
        weights[offset % length] += COEFFICIENTS[offset]
        weights[-offset % length] += COEFFICIENTS[offset]
    return weights


def pair_weights(length):
    weights = ring_weights(length)
    pairs = []
    for distance in range(1, length // 2 + 1):
        if weights[distance] != 0.0:
            pairs.append((sorted({distance, length - distance}), weights[distance]))
    return weights[0], pairs


def apply(field, diagonal, hop, before):
    ys = len(field)
    planes, xs = field[0].shape
    along_y, along_planes, along_x = [pair_weights(length)[1] for length in (ys, planes, xs)]
    results = []
    for y in range(ys):
        tile = field[y]
        total = diagonal[y] * tile
        if before is not None:
            total = total - before[y]
        for shifts, weight in along_y:
            total = total + (hop * weight) * functools.reduce(jnp.add, [field[(y - shift) % ys] for shift in shifts])
        for pairs, axis in ((along_planes, 0), (along_x, 1)):
            for shifts, weight in pairs:
                total = total + (hop * weight) * functools.reduce(
                    jnp.add, [pltpu.roll(tile, shift, axis) for shift in shifts]
                )
        results.append(total)
    return results


def place_of(chip, order):
    place = order.index(chip)
    if place == 0:
        return place
    return jnp.where(lax.axis_index("core") == 0, place, len(order) - place)


def filter_kernel(ng, copies, rows, run, width, cores, order, *refs):
    sources, out_ref, held, sems, natural_ref = refs[:5], refs[5], refs[6:11], refs[11], refs[12]
    orb_ref, region_ref, table_ref, counts_ref, ritz_ref = held
    transfers = [
        pltpu.make_async_copy(source, target, sems.at[index])
        for index, (source, target) in enumerate(zip(sources, held))
    ]
    for transfer in transfers:
        transfer.start()
    for transfer in transfers:
        transfer.wait()
    ys, planes, xs = orb_ref.shape
    columns, panel = ritz_ref.shape
    per_row = LANES // width
    for row in range(-(-columns // per_row)):
        line = jnp.zeros((1, LANES), jnp.float32)
        for slot in range(min(per_row, columns - row * per_row)):
            piece = jnp.concatenate(
                [ritz_ref[pl.ds(row * per_row + slot, 1), :], jnp.zeros((1, LANES - panel), jnp.float32)], axis=1
            )
            line = line + (pltpu.roll(piece, slot * width, 1) if slot else piece)
        natural_ref[pl.ds(run + row, ng, stride=rows), :] = jnp.broadcast_to(line, (ng, LANES))

    centre_weight = 3.0 * COEFFICIENTS[0] + sum(pair_weights(n)[0] for n in (planes, ys, xs))
    scale = 2.0 / HALF
    hop = -0.5 / (SPACING * SPACING) * scale
    diagonal = []
    for y in range(ys):
        region = region_ref[y]
        potential = jnp.zeros((planes, xs), jnp.float32)
        for index in range(table_ref.shape[0]):
            potential = jnp.where(region == index, table_ref[index], potential)
        diagonal.append(scale * potential + (hop * centre_weight - scale * CENTRE))
    band_pos = lax.axis_index("row") * cores + lax.axis_index("core")
    live = (lax.axis_index("grid") < counts_ref[band_pos]).astype(jnp.float32)
    previous = [live * orb_ref[y] for y in range(ys)]
    current = apply(previous, [0.5 * value for value in diagonal], 0.5 * hop, None)
    for _ in range(DEGREE - 1):
        previous, current = current, apply(current, diagonal, hop, previous)

    blocks = ys // run
    for y in range(ys):
        natural_ref[pl.ds((y // run) * rows + y % run, planes, stride=blocks * rows), :] = current[y]
    for copy in range(copies):
        for tile in range(ng):
            start = pl.multiple_of(place_of(copy * ng + tile, order) * rows, rows)
            out_ref[pl.ds(start, rows), :] = natural_ref[pl.ds(tile * rows, rows), :]


def start_kernel(packed_ref, out_ref):
    out_ref[...] = jnp.zeros_like(out_ref)


def partial_kernel(nrow, ng, run, width, columns, cores, order, distance, got_ref, start_ref, out_ref, ritz_ref):
    places = [place_of(chip, order) for chip in range(nrow * ng)]
    for chip, place in enumerate(places):
        ritz_ref[chip] = got_ref[place, pl.ds(run, 1), :]
    wanted = out_ref.shape[0]
    holders = wanted // columns
    sublane = lax.broadcasted_iota(jnp.int32, (wanted, LANES), 0)
    block = lax.axis_index("row") * cores + lax.rem(lax.axis_index("core") + distance, cores)
    acc = [start_ref[:, pl.ds(y * LANES, LANES)] for y in range(run)]
    for row in range(nrow):
        lines = jnp.zeros((wanted, LANES), jnp.float32)
        for k in range(holders):
            line = ritz_ref[row * ng + block * holders + k]
            lines = jnp.where(sublane // columns == k, jnp.broadcast_to(line, (wanted, LANES)), lines)
        for r in range(ng):
            weight = jnp.take_along_axis(lines, sublane % columns * width + r, axis=1)
            for y in range(run):
                acc[y] = acc[y] + weight * got_ref[places[row * ng + r], pl.ds(y, 1), :]
    for y in range(run):
        out_ref[:, pl.ds(y * LANES, LANES)] = acc[y]


def shards(nrow, cores, ng, orbitals, region, potential_table, counts, ritz):
    _, planes, ys, xs = orbitals.shape
    cells = planes * ys * xs
    panel, columns = ritz.shape
    run = cells // ng // xs
    width = 1
    while width < panel:
        width *= 2
    per_row = LANES // width
    ritz_rows = -(-columns // per_row)
    rows = -(-(run + ritz_rows) // SUBLANES) * SUBLANES
    tiles = nrow * ng
    vmem = pl.BlockSpec(memory_space=pltpu.VMEM)
    hbm = pl.BlockSpec(memory_space=pltpu.HBM)
    inputs = [
        pltpu.with_memory_space_constraint(value, pltpu.HBM)
        for value in (
            jnp.transpose(orbitals[0], (1, 0, 2)), jnp.transpose(region, (1, 0, 2)), potential_table, counts, ritz.T
        )
    ]
    late = sorted(range(tiles), key=lambda place: (place % ng // (ng // 2), place // ng, place % ng), reverse=True)
    order = [place for pair in zip(late, late[::-1]) for place in pair][:tiles]
    packed_bytes = 4 * tiles * rows * LANES
    packed = pl.pallas_call(
        functools.partial(filter_kernel, ng, nrow, rows, run, width, cores, order),
        out_shape=jax.ShapeDtypeStruct((tiles * rows, LANES), jnp.float32),
        in_specs=[hbm] * 5,
        out_specs=vmem,
        scratch_shapes=[
            pltpu.VMEM((ys, planes, xs), jnp.float32),
            pltpu.VMEM((ys, planes, xs), jnp.int32),
            pltpu.SMEM(potential_table.shape, jnp.float32),
            pltpu.SMEM(counts.shape, jnp.int32),
            pltpu.VMEM((columns, panel), jnp.float32),
            pltpu.SemaphoreType.DMA((5,)),
            pltpu.VMEM((ng * rows, LANES), jnp.float32),
        ],
        compiler_params=pltpu.CompilerParams(vmem_limit_bytes=2 * packed_bytes + 64 * cells + 2**20),
        name="chebyshev_filter",
    )(*inputs)
    got = lax.all_to_all(
        packed.reshape(tiles, rows, LANES), ("row", "core", "grid"), split_axis=0, concat_axis=0, tiled=True,
        axis_index_groups=[
            [(chip // ng * cores + core) * ng + chip % ng for chip in (order[:1] + order[:0:-1] if core else order)]
            for core in range(cores)
        ],
    )
    sum_shape = jax.ShapeDtypeStruct((panel, run * LANES), jnp.float32)
    if columns * width <= LANES and tiles <= 64 and panel == ng and panel <= 16:
        start = pl.pallas_call(
            start_kernel,
            out_shape=sum_shape,
            in_specs=[pl.BlockSpec(memory_space=pl.ANY)],
            out_specs=vmem,
            compiler_params=pltpu.CompilerParams(vmem_limit_bytes=2**20),
            name="sums_start",
        )(packed)

        def partial_sums(distance):
            return pl.pallas_call(
                functools.partial(partial_kernel, nrow, ng, run, width, columns, cores, order, distance),
                out_shape=sum_shape,
                in_specs=[vmem] * 2,
                out_specs=vmem,
                scratch_shapes=[pltpu.VMEM((tiles, 1, LANES), jnp.float32)],
                compiler_params=pltpu.CompilerParams(vmem_limit_bytes=packed_bytes + 2**20),
                name="ritz_partial_sums",
            )(got, start)

    else:
        holders = panel // columns
        by_source = got[jnp.stack([place_of(chip, order) for chip in range(tiles)])].reshape(nrow, ng, rows, LANES)
        fields = by_source[:, :, :run].reshape(tiles, run * LANES)
        blocks = by_source[:, :, run : run + ritz_rows].reshape(nrow, ng, ritz_rows * per_row, width)

        def partial_sums(distance):
            block = lax.axis_index("row") * cores + lax.rem(lax.axis_index("core") + distance, cores)
            mine = lax.dynamic_slice_in_dim(blocks, block * holders, holders, axis=1)
            return lax.dot_general(
                jnp.transpose(mine[:, :, :columns, :panel], (0, 3, 1, 2)).reshape(tiles, panel),
                fields,
                (((0,), (0,)), ((), ())),
                precision=lax.Precision.HIGHEST,
                preferred_element_type=jnp.float32,
            )

    terms = []
    for distance in range(1, cores):
        pairs = [(core, (core + distance) % cores) for core in range(cores)]
        terms.append(lax.ppermute(partial_sums(distance), "core", pairs))
    terms.append(partial_sums(0))
    return functools.reduce(jnp.add, terms)


def solution(mesh):
    bands, ng = mesh.shape["band"], mesh.shape["grid"]
    cores = 2 if bands % 2 == 0 else 1
    nrow = bands // cores
    split = jax.sharding.Mesh(mesh.devices.reshape(nrow, cores, ng), ("row", "core", "grid"))
    return jax.shard_map(
        functools.partial(shards, nrow, cores, ng),
        mesh=split,
        in_specs=(P(("row", "core", "grid"), None, None, None), P(), P(), P(), P(("row", "core"), "grid")),
        out_specs=P(("row", "core"), "grid"),
        check_vma=False,
    )
```

```python
import functools

import jax
import jax.numpy as jnp
from jax import lax
from jax.experimental import pallas as pl
from jax.experimental.pallas import tpu as pltpu
from jax.sharding import PartitionSpec as P

DEGREE = 4

COEFFICIENTS = (
    -5369.0 / 1800.0,
    12.0 / 7.0,
    -15.0 / 56.0,
    10.0 / 189.0,
    -1.0 / 112.0,
    2.0 / 1925.0,
    -1.0 / 16632.0,
)
SPACING = 0.5
LOWER = 6.0
UPPER = 46.0
HALF = (UPPER - LOWER) / 2.0
CENTRE = (UPPER + LOWER) / 2.0
LANES = 128
SUBLANES = 8


def ring_weights(length):
    weights = [0.0] * length
    for offset in range(1, 7):
        weights[offset % length] += COEFFICIENTS[offset]
        weights[-offset % length] += COEFFICIENTS[offset]
    return weights


def pair_weights(length):
    weights = ring_weights(length)
    pairs = []
    for distance in range(1, length // 2 + 1):
        if weights[distance] != 0.0:
            pairs.append((sorted({distance, length - distance}), weights[distance]))
    return weights[0], pairs


def apply(field, diagonal, hop, before):
    ys = len(field)
    planes, xs = field[0].shape
    along_y, along_planes, along_x = [pair_weights(length)[1] for length in (ys, planes, xs)]
    results = []
    for y in range(ys):
        tile = field[y]
        total = diagonal[y] * tile
        if before is not None:
            total = total - before[y]
        for shifts, weight in along_y:
            total = total + (hop * weight) * functools.reduce(jnp.add, [field[(y - shift) % ys] for shift in shifts])
        for pairs, axis in ((along_planes, 0), (along_x, 1)):
            for shifts, weight in pairs:
                total = total + (hop * weight) * functools.reduce(
                    jnp.add, [pltpu.roll(tile, shift, axis) for shift in shifts]
                )
        results.append(total)
    return results


def place_of(chip, order):
    place = order.index(chip)
    if place == 0:
        return place
    return jnp.where(lax.axis_index("core") == 0, place, len(order) - place)


def filter_kernel(ng, copies, rows, run, width, cores, order, *refs):
    sources, out_ref, held, sems, natural_ref = refs[:5], refs[5], refs[6:11], refs[11], refs[12]
    orb_ref, region_ref, table_ref, counts_ref, ritz_ref = held
    transfers = [
        pltpu.make_async_copy(source, target, sems.at[index])
        for index, (source, target) in enumerate(zip(sources, held))
    ]
    for transfer in transfers:
        transfer.start()
    for transfer in transfers:
        transfer.wait()
    ys, planes, xs = orb_ref.shape
    columns, panel = ritz_ref.shape
    per_row = LANES // width
    for row in range(-(-columns // per_row)):
        line = jnp.zeros((1, LANES), jnp.float32)
        for slot in range(min(per_row, columns - row * per_row)):
            piece = jnp.concatenate(
                [ritz_ref[pl.ds(row * per_row + slot, 1), :], jnp.zeros((1, LANES - panel), jnp.float32)], axis=1
            )
            line = line + (pltpu.roll(piece, slot * width, 1) if slot else piece)
        natural_ref[pl.ds(run + row, ng, stride=rows), :] = jnp.broadcast_to(line, (ng, LANES))

    centre_weight = 3.0 * COEFFICIENTS[0] + sum(pair_weights(n)[0] for n in (planes, ys, xs))
    scale = 2.0 / HALF
    hop = -0.5 / (SPACING * SPACING) * scale
    diagonal = []
    for y in range(ys):
        region = region_ref[y]
        potential = jnp.zeros((planes, xs), jnp.float32)
        for index in range(table_ref.shape[0]):
            potential = jnp.where(region == index, table_ref[index], potential)
        diagonal.append(scale * potential + (hop * centre_weight - scale * CENTRE))
    band_pos = lax.axis_index("row") * cores + lax.axis_index("core")
    live = (lax.axis_index("grid") < counts_ref[band_pos]).astype(jnp.float32)
    previous = [live * orb_ref[y] for y in range(ys)]
    current = apply(previous, [0.5 * value for value in diagonal], 0.5 * hop, None)
    for _ in range(DEGREE - 1):
        previous, current = current, apply(current, diagonal, hop, previous)

    blocks = ys // run
    for y in range(ys):
        natural_ref[pl.ds((y // run) * rows + y % run, planes, stride=blocks * rows), :] = current[y]
    for copy in range(copies):
        for tile in range(ng):
            start = pl.multiple_of(place_of(copy * ng + tile, order) * rows, rows)
            out_ref[pl.ds(start, rows), :] = natural_ref[pl.ds(tile * rows, rows), :]


def partial_kernel(nrow, ng, run, width, columns, cores, order, distance, got_ref, out_ref, ritz_ref):
    places = [place_of(chip, order) for chip in range(nrow * ng)]
    for chip, place in enumerate(places):
        ritz_ref[chip] = got_ref[place, pl.ds(run, 1), :]
    wanted = out_ref.shape[0]
    holders = wanted // columns
    sublane = lax.broadcasted_iota(jnp.int32, (wanted, LANES), 0)
    block = lax.axis_index("row") * cores + lax.rem(lax.axis_index("core") + distance, cores)
    acc = [jnp.zeros((wanted, LANES), jnp.float32) for _ in range(run)]
    for row in range(nrow):
        lines = jnp.zeros((wanted, LANES), jnp.float32)
        for k in range(holders):
            line = ritz_ref[row * ng + block * holders + k]
            lines = jnp.where(sublane // columns == k, jnp.broadcast_to(line, (wanted, LANES)), lines)
        for r in range(ng):
            weight = jnp.take_along_axis(lines, sublane % columns * width + r, axis=1)
            for y in range(run):
                acc[y] = acc[y] + weight * got_ref[places[row * ng + r], pl.ds(y, 1), :]
    for y in range(run):
        out_ref[:, pl.ds(y * LANES, LANES)] = acc[y]


def shards(nrow, cores, ng, orbitals, region, potential_table, counts, ritz):
    _, planes, ys, xs = orbitals.shape
    cells = planes * ys * xs
    panel, columns = ritz.shape
    run = cells // ng // xs
    width = 1
    while width < panel:
        width *= 2
    per_row = LANES // width
    ritz_rows = -(-columns // per_row)
    rows = -(-(run + ritz_rows) // SUBLANES) * SUBLANES
    tiles = nrow * ng
    vmem = pl.BlockSpec(memory_space=pltpu.VMEM)
    hbm = pl.BlockSpec(memory_space=pltpu.HBM)
    inputs = [
        pltpu.with_memory_space_constraint(value, pltpu.HBM)
        for value in (
            jnp.transpose(orbitals[0], (1, 0, 2)), jnp.transpose(region, (1, 0, 2)), potential_table, counts, ritz.T
        )
    ]
    late = sorted(range(tiles), key=lambda place: (place % ng // (ng // 2), place // ng, place % ng), reverse=True)
    order = [place for pair in zip(late, late[::-1]) for place in pair][:tiles]
    first = ng - ng // 4 - 1
    order = [first] + [place for place in order if place != first]
    packed_bytes = 4 * tiles * rows * LANES
    packed = pl.pallas_call(
        functools.partial(filter_kernel, ng, nrow, rows, run, width, cores, order),
        out_shape=jax.ShapeDtypeStruct((tiles * rows, LANES), jnp.float32),
        in_specs=[hbm] * 5,
        out_specs=vmem,
        scratch_shapes=[
            pltpu.VMEM((ys, planes, xs), jnp.float32),
            pltpu.VMEM((ys, planes, xs), jnp.int32),
            pltpu.SMEM(potential_table.shape, jnp.float32),
            pltpu.SMEM(counts.shape, jnp.int32),
            pltpu.VMEM((columns, panel), jnp.float32),
            pltpu.SemaphoreType.DMA((5,)),
            pltpu.VMEM((ng * rows, LANES), jnp.float32),
        ],
        compiler_params=pltpu.CompilerParams(vmem_limit_bytes=2 * packed_bytes + 64 * cells + 2**20),
        name="chebyshev_filter",
    )(*inputs)
    got = lax.all_to_all(
        packed.reshape(tiles, rows, LANES), ("row", "core", "grid"), split_axis=0, concat_axis=0, tiled=True,
        axis_index_groups=[
            [(chip // ng * cores + core) * ng + chip % ng for chip in (order[:1] + order[:0:-1] if core else order)]
            for core in range(cores)
        ],
    )
    sum_shape = jax.ShapeDtypeStruct((panel, run * LANES), jnp.float32)
    if columns * width <= LANES and tiles <= 64 and panel == ng and panel <= 16:
        def partial_sums(distance):
            return pl.pallas_call(
                functools.partial(partial_kernel, nrow, ng, run, width, columns, cores, order, distance),
                out_shape=sum_shape,
                in_specs=[vmem],
                out_specs=vmem,
                scratch_shapes=[pltpu.VMEM((tiles, 1, LANES), jnp.float32)],
                compiler_params=pltpu.CompilerParams(vmem_limit_bytes=packed_bytes + 2**20),
                name="ritz_partial_sums",
            )(got)

    else:
        holders = panel // columns
        by_source = got[jnp.stack([place_of(chip, order) for chip in range(tiles)])].reshape(nrow, ng, rows, LANES)
        fields = by_source[:, :, :run].reshape(tiles, run * LANES)
        blocks = by_source[:, :, run : run + ritz_rows].reshape(nrow, ng, ritz_rows * per_row, width)

        def partial_sums(distance):
            block = lax.axis_index("row") * cores + lax.rem(lax.axis_index("core") + distance, cores)
            mine = lax.dynamic_slice_in_dim(blocks, block * holders, holders, axis=1)
            return lax.dot_general(
                jnp.transpose(mine[:, :, :columns, :panel], (0, 3, 1, 2)).reshape(tiles, panel),
                fields,
                (((0,), (0,)), ((), ())),
                precision=lax.Precision.HIGHEST,
                preferred_element_type=jnp.float32,
            )

    terms = []
    for distance in range(1, cores):
        pairs = [(core, (core + distance) % cores) for core in range(cores)]
        terms.append(lax.ppermute(partial_sums(distance), "core", pairs))
    terms.append(partial_sums(0))
    return functools.reduce(jnp.add, terms)


def solution(mesh):
    bands, ng = mesh.shape["band"], mesh.shape["grid"]
    cores = 2 if bands % 2 == 0 else 1
    nrow = bands // cores
    split = jax.sharding.Mesh(mesh.devices.reshape(nrow, cores, ng), ("row", "core", "grid"))
    return jax.shard_map(
        functools.partial(shards, nrow, cores, ng),
        mesh=split,
        in_specs=(P(("row", "core", "grid"), None, None, None), P(), P(), P(), P(("row", "core"), "grid")),
        out_specs=P(("row", "core"), "grid"),
        check_vma=False,
    )
```

```python
import functools

import jax
import jax.numpy as jnp
from jax import lax
from jax.experimental import pallas as pl
from jax.experimental.pallas import tpu as pltpu
from jax.sharding import PartitionSpec as P

DEGREE = 4

COEFFICIENTS = (
    -5369.0 / 1800.0,
    12.0 / 7.0,
    -15.0 / 56.0,
    10.0 / 189.0,
    -1.0 / 112.0,
    2.0 / 1925.0,
    -1.0 / 16632.0,
)
SPACING = 0.5
LOWER = 6.0
UPPER = 46.0
HALF = (UPPER - LOWER) / 2.0
CENTRE = (UPPER + LOWER) / 2.0
LANES = 128
SUBLANES = 8


def ring_weights(length):
    weights = [0.0] * length
    for offset in range(1, 7):
        weights[offset % length] += COEFFICIENTS[offset]
        weights[-offset % length] += COEFFICIENTS[offset]
    return weights


def pair_weights(length):
    weights = ring_weights(length)
    pairs = []
    for distance in range(1, length // 2 + 1):
        if weights[distance] != 0.0:
            pairs.append((sorted({distance, length - distance}), weights[distance]))
    return weights[0], pairs


def apply(field, diagonal, hop, before, twice_ref):
    ys = len(field)
    planes, xs = field[0].shape
    along_y, along_planes, along_x = [pair_weights(length)[1] for length in (ys, planes, xs)]
    for y in range(ys):
        twice_ref[y, pl.ds(0, planes), :] = field[y]
        twice_ref[y, pl.ds(planes, planes), :] = field[y]
    results = []
    for y in range(ys):
        tile = field[y]
        total = diagonal[y] * tile
        if before is not None:
            total = total - before[y]
        for shifts, weight in along_y:
            total = total + (hop * weight) * functools.reduce(jnp.add, [field[(y - shift) % ys] for shift in shifts])
        for shifts, weight in along_planes:
            total = total + (hop * weight) * functools.reduce(
                jnp.add, [twice_ref[y, pl.ds(planes - shift, planes), :] for shift in shifts]
            )
        for shifts, weight in along_x:
            total = total + (hop * weight) * functools.reduce(jnp.add, [pltpu.roll(tile, shift, 1) for shift in shifts])
        results.append(total)
    return results


def filter_kernel(ng, copies, rows, run, width, cores, order, *refs):
    sources, out_ref, held, sems, natural_ref, twice_ref = refs[:5], refs[5], refs[6:11], *refs[11:]
    orb_ref, region_ref, table_ref, counts_ref, ritz_ref = held
    transfers = [
        pltpu.make_async_copy(source, target, sems.at[index])
        for index, (source, target) in enumerate(zip(sources, held))
    ]
    for transfer in transfers:
        transfer.start()
    for transfer in transfers:
        transfer.wait()
    ys, planes, xs = orb_ref.shape
    columns, panel = ritz_ref.shape
    per_row = LANES // width
    for row in range(-(-columns // per_row)):
        line = jnp.zeros((1, LANES), jnp.float32)
        for slot in range(min(per_row, columns - row * per_row)):
            piece = jnp.concatenate(
                [ritz_ref[pl.ds(row * per_row + slot, 1), :], jnp.zeros((1, LANES - panel), jnp.float32)], axis=1
            )
            line = line + (pltpu.roll(piece, slot * width, 1) if slot else piece)
        natural_ref[pl.ds(run + row, ng, stride=rows), :] = jnp.broadcast_to(line, (ng, LANES))

    centre_weight = 3.0 * COEFFICIENTS[0] + sum(pair_weights(n)[0] for n in (planes, ys, xs))
    scale = 2.0 / HALF
    hop = -0.5 / (SPACING * SPACING) * scale
    diagonal = []
    for y in range(ys):
        region = region_ref[y]
        potential = jnp.zeros((planes, xs), jnp.float32)
        for index in range(table_ref.shape[0]):
            potential = jnp.where(region == index, table_ref[index], potential)
        diagonal.append(scale * potential + (hop * centre_weight - scale * CENTRE))
    band_pos = lax.axis_index("row") * cores + lax.axis_index("core")
    live = (lax.axis_index("grid") < counts_ref[band_pos]).astype(jnp.float32)
    previous = [live * orb_ref[y] for y in range(ys)]
    current = apply(previous, [0.5 * value for value in diagonal], 0.5 * hop, None, twice_ref)
    for _ in range(DEGREE - 1):
        previous, current = current, apply(current, diagonal, hop, previous, twice_ref)

    blocks = ys // run
    for y in range(ys):
        natural_ref[pl.ds((y // run) * rows + y % run, planes, stride=blocks * rows), :] = current[y]
    for copy in range(copies):
        for tile in range(ng):
            place = order.index(copy * ng + tile)
            out_ref[pl.ds(place * rows, rows), :] = natural_ref[pl.ds(tile * rows, rows), :]


def partial_kernel(nrow, ng, run, width, columns, cores, order, distance, got_ref, out_ref, ritz_ref):
    for place, source in enumerate(order):
        ritz_ref[source] = got_ref[place, pl.ds(run, 1), :]
    wanted = out_ref.shape[0]
    holders = wanted // columns
    sublane = lax.broadcasted_iota(jnp.int32, (wanted, LANES), 0)
    block = lax.axis_index("row") * cores + lax.rem(lax.axis_index("core") + distance, cores)
    acc = [jnp.zeros((wanted, LANES), jnp.float32) for _ in range(run)]
    for row in range(nrow):
        lines = jnp.zeros((wanted, LANES), jnp.float32)
        for k in range(holders):
            line = ritz_ref[row * ng + block * holders + k]
            lines = jnp.where(sublane // columns == k, jnp.broadcast_to(line, (wanted, LANES)), lines)
        for r in range(ng):
            weight = jnp.take_along_axis(lines, sublane % columns * width + r, axis=1)
            for y in range(run):
                acc[y] = acc[y] + weight * got_ref[order.index(row * ng + r), pl.ds(y, 1), :]
    for y in range(run):
        out_ref[:, pl.ds(y * LANES, LANES)] = acc[y]


def shards(nrow, cores, ng, orbitals, region, potential_table, counts, ritz):
    _, planes, ys, xs = orbitals.shape
    cells = planes * ys * xs
    panel, columns = ritz.shape
    run = cells // ng // xs
    width = 1
    while width < panel:
        width *= 2
    per_row = LANES // width
    ritz_rows = -(-columns // per_row)
    rows = -(-(run + ritz_rows) // SUBLANES) * SUBLANES
    tiles = nrow * ng
    vmem = pl.BlockSpec(memory_space=pltpu.VMEM)
    hbm = pl.BlockSpec(memory_space=pltpu.HBM)
    inputs = [
        pltpu.with_memory_space_constraint(value, pltpu.HBM)
        for value in (
            jnp.transpose(orbitals[0], (1, 0, 2)), jnp.transpose(region, (1, 0, 2)), potential_table, counts, ritz.T
        )
    ]
    late = sorted(range(tiles), key=lambda place: (place % ng // (ng // 2), place // ng, place % ng), reverse=True)
    order = [place for pair in zip(late, late[::-1]) for place in pair][:tiles]
    packed_bytes = 4 * tiles * rows * LANES
    packed = pl.pallas_call(
        functools.partial(filter_kernel, ng, nrow, rows, run, width, cores, order),
        out_shape=jax.ShapeDtypeStruct((tiles * rows, LANES), jnp.float32),
        in_specs=[hbm] * 5,
        out_specs=vmem,
        scratch_shapes=[
            pltpu.VMEM((ys, planes, xs), jnp.float32),
            pltpu.VMEM((ys, planes, xs), jnp.int32),
            pltpu.SMEM(potential_table.shape, jnp.float32),
            pltpu.SMEM(counts.shape, jnp.int32),
            pltpu.VMEM((columns, panel), jnp.float32),
            pltpu.SemaphoreType.DMA((5,)),
            pltpu.VMEM((ng * rows, LANES), jnp.float32),
            pltpu.VMEM((ys, 2 * planes, xs), jnp.float32),
        ],
        compiler_params=pltpu.CompilerParams(vmem_limit_bytes=2 * packed_bytes + 64 * cells + 2**20),
        name="chebyshev_filter",
    )(*inputs)
    got = lax.all_to_all(
        packed.reshape(tiles, rows, LANES), ("row", "grid"), split_axis=0, concat_axis=0, tiled=True,
        axis_index_groups=[order],
    )
    sum_shape = jax.ShapeDtypeStruct((panel, run * LANES), jnp.float32)
    if columns * width <= LANES and tiles <= 64 and panel == ng and panel <= 16:
        def partial_sums(distance):
            return pl.pallas_call(
                functools.partial(partial_kernel, nrow, ng, run, width, columns, cores, order, distance),
                out_shape=sum_shape,
                in_specs=[vmem],
                out_specs=vmem,
                scratch_shapes=[pltpu.VMEM((tiles, 1, LANES), jnp.float32)],
                compiler_params=pltpu.CompilerParams(vmem_limit_bytes=packed_bytes + 2**20),
                name="ritz_partial_sums",
            )(got)

    else:
        holders = panel // columns
        by_source = got[jnp.argsort(jnp.array(order))].reshape(nrow, ng, rows, LANES)
        fields = by_source[:, :, :run].reshape(tiles, run * LANES)
        blocks = by_source[:, :, run : run + ritz_rows].reshape(nrow, ng, ritz_rows * per_row, width)

        def partial_sums(distance):
            block = lax.axis_index("row") * cores + lax.rem(lax.axis_index("core") + distance, cores)
            mine = lax.dynamic_slice_in_dim(blocks, block * holders, holders, axis=1)
            return lax.dot_general(
                jnp.transpose(mine[:, :, :columns, :panel], (0, 3, 1, 2)).reshape(tiles, panel),
                fields,
                (((0,), (0,)), ((), ())),
                precision=lax.Precision.HIGHEST,
                preferred_element_type=jnp.float32,
            )

    terms = []
    for distance in range(1, cores):
        pairs = [(core, (core + distance) % cores) for core in range(cores)]
        terms.append(lax.ppermute(partial_sums(distance), "core", pairs))
    terms.append(partial_sums(0))
    return functools.reduce(jnp.add, terms)


def solution(mesh):
    bands, ng = mesh.shape["band"], mesh.shape["grid"]
    cores = 2 if bands % 2 == 0 else 1
    nrow = bands // cores
    split = jax.sharding.Mesh(mesh.devices.reshape(nrow, cores, ng), ("row", "core", "grid"))
    return jax.shard_map(
        functools.partial(shards, nrow, cores, ng),
        mesh=split,
        in_specs=(P(("row", "core", "grid"), None, None, None), P(), P(), P(), P(("row", "core"), "grid")),
        out_specs=P(("row", "core"), "grid"),
        check_vma=False,
    )
```

```python
import functools

import jax
import jax.numpy as jnp
from jax import lax
from jax.experimental import pallas as pl
from jax.experimental.pallas import tpu as pltpu
from jax.sharding import PartitionSpec as P

DEGREE = 4

COEFFICIENTS = (
    -5369.0 / 1800.0,
    12.0 / 7.0,
    -15.0 / 56.0,
    10.0 / 189.0,
    -1.0 / 112.0,
    2.0 / 1925.0,
    -1.0 / 16632.0,
)
SPACING = 0.5
LOWER = 6.0
UPPER = 46.0
HALF = (UPPER - LOWER) / 2.0
CENTRE = (UPPER + LOWER) / 2.0
SCALE = 2.0 / HALF
HOP = -0.5 / (SPACING * SPACING) * SCALE
LANES = 128
SUBLANES = 8


def ring_weights(length):
    weights = [0.0] * length
    for offset in range(1, 7):
        weights[offset % length] += COEFFICIENTS[offset]
        weights[-offset % length] += COEFFICIENTS[offset]
    return weights


def pair_weights(length):
    weights = ring_weights(length)
    pairs = []
    for distance in range(1, length // 2 + 1):
        if weights[distance] != 0.0:
            pairs.append((sorted({distance, length - distance}), weights[distance]))
    return weights[0], pairs


def apply(field, diagonal, hop, before):
    ys = len(field)
    planes, xs = field[0].shape
    along_y, along_planes, along_x = [pair_weights(length)[1] for length in (ys, planes, xs)]
    results = []
    for y in range(ys):
        tile = field[y]
        total = diagonal[y] * tile
        if before is not None:
            total = total - before[y]
        for shifts, weight in along_y:
            total = total + (hop * weight) * functools.reduce(jnp.add, [field[(y - shift) % ys] for shift in shifts])
        for pairs, axis in ((along_planes, 0), (along_x, 1)):
            for shifts, weight in pairs:
                total = total + (hop * weight) * functools.reduce(
                    jnp.add, [pltpu.roll(tile, shift, axis) for shift in shifts]
                )
        results.append(total)
    return results


def pack_ritz(ritz_ref, natural_ref, ng, rows, run, width):
    columns, panel = ritz_ref.shape
    per_row = LANES // width
    for row in range(-(-columns // per_row)):
        line = jnp.zeros((1, LANES), jnp.float32)
        for slot in range(min(per_row, columns - row * per_row)):
            piece = jnp.concatenate(
                [ritz_ref[pl.ds(row * per_row + slot, 1), :], jnp.zeros((1, LANES - panel), jnp.float32)], axis=1
            )
            line = line + (pltpu.roll(piece, slot * width, 1) if slot else piece)
        natural_ref[pl.ds(run + row, ng, stride=rows), :] = jnp.broadcast_to(line, (ng, LANES))


def filter_into(field, diagonal, natural_ref, rows, run):
    ys, planes = len(field), field[0].shape[0]
    previous = field
    current = apply(previous, [0.5 * value for value in diagonal], 0.5 * HOP, None)
    for _ in range(DEGREE - 1):
        previous, current = current, apply(current, diagonal, HOP, previous)
    blocks = ys // run
    for y in range(ys):
        natural_ref[pl.ds((y // run) * rows + y % run, planes, stride=blocks * rows), :] = current[y]


def load_and_filter(ng, rows, run, width, cores, sources, held, sems, natural_ref):
    orb_ref, region_ref, table_ref, counts_ref, ritz_ref = held
    transfers = [
        pltpu.make_async_copy(source, target, sems.at[index])
        for index, (source, target) in enumerate(zip(sources, held))
    ]
    for transfer in transfers:
        transfer.start()
    for transfer in transfers:
        transfer.wait()
    pack_ritz(ritz_ref, natural_ref, ng, rows, run, width)
    ys, planes, xs = orb_ref.shape
    centre_weight = 3.0 * COEFFICIENTS[0] + sum(pair_weights(n)[0] for n in (planes, ys, xs))
    diagonal = []
    for y in range(ys):
        region = region_ref[y]
        potential = jnp.zeros((planes, xs), jnp.float32)
        for index in range(table_ref.shape[0]):
            potential = jnp.where(region == index, table_ref[index], potential)
        diagonal.append(SCALE * potential + (HOP * centre_weight - SCALE * CENTRE))

    def live(core):
        band_pos = lax.axis_index("row") * cores + core
        return (lax.axis_index("grid") < counts_ref[band_pos]).astype(jnp.float32)

    mask = live(lax.axis_index("core"))
    filter_into([mask * orb_ref[y] for y in range(ys)], diagonal, natural_ref, rows, run)
    return diagonal, live


def filter_kernel(ng, rows, run, width, cores, order, *refs):
    sources, out_ref, held, sems, natural_ref = refs[:5], refs[5], refs[6:11], refs[11], refs[12]
    load_and_filter(ng, rows, run, width, cores, sources, held, sems, natural_ref)
    for place, chip in enumerate(order):
        out_ref[pl.ds(place * rows, rows), :] = natural_ref[pl.ds(chip % ng * rows, rows), :]


def own_kernel(ng, rows, run, width, cores, *refs):
    sources, (natural_ref, diagonal_ref, mask_ref), held, sems = refs[:5], refs[5:8], refs[8:13], refs[13]
    diagonal, live = load_and_filter(ng, rows, run, width, cores, sources, held, sems, natural_ref)
    for y, value in enumerate(diagonal):
        diagonal_ref[y] = value
    mask_ref[...] = jnp.broadcast_to(live(1 - lax.axis_index("core")), mask_ref.shape)


def other_kernel(ng, rows, run, width, order, orb_ref, ritz_ref, natural_ref, diagonal_ref, mask_ref, out_ref, held_ref):
    pack_ritz(ritz_ref, held_ref, ng, rows, run, width)
    ys = orb_ref.shape[0]
    filter_into([mask_ref[...] * orb_ref[y] for y in range(ys)], [diagonal_ref[y] for y in range(ys)], held_ref, rows, run)
    for place, chip in enumerate(order):
        tile = pl.ds(chip % ng * rows, rows)
        out_ref[pl.ds(2 * place * rows, rows), :] = natural_ref[tile, :]
        out_ref[pl.ds((2 * place + 1) * rows, rows), :] = held_ref[tile, :]


def rotate_kernel(nrow, ng, rows, run, width, columns, cores, order, got_ref, out_ref, ritz_ref):
    wanted = out_ref.shape[0]
    holders = wanted // columns
    sublane = lax.broadcasted_iota(jnp.int32, (wanted, LANES), 0)
    block = lax.axis_index("row") * cores + lax.axis_index("core")
    for tile in range(2):
        for place, source in enumerate(order):
            ritz_ref[tile, source] = got_ref[place, pl.ds(tile * rows + run, 1), :]
    acc = [jnp.zeros((wanted, LANES), jnp.float32) for _ in range(run)]
    for tile in range(2):
        for row in range(nrow):
            lines = jnp.zeros((wanted, LANES), jnp.float32)
            for k in range(holders):
                line = ritz_ref[tile, row * ng + block * holders + k]
                lines = jnp.where(sublane // columns == k, jnp.broadcast_to(line, (wanted, LANES)), lines)
            for r in range(ng):
                weight = jnp.take_along_axis(lines, sublane % columns * width + r, axis=1)
                for y in range(run):
                    acc[y] = acc[y] + weight * got_ref[order.index(row * ng + r), pl.ds(tile * rows + y, 1), :]
    for y in range(run):
        out_ref[:, pl.ds(y * LANES, LANES)] = acc[y]


def shards(nrow, cores, ng, orbitals, region, potential_table, counts, ritz):
    _, planes, ys, xs = orbitals.shape
    cells = planes * ys * xs
    panel, columns = ritz.shape
    run = cells // ng // xs
    width = 1
    while width < panel:
        width *= 2
    per_row = LANES // width
    ritz_rows = -(-columns // per_row)
    rows = -(-(run + ritz_rows) // SUBLANES) * SUBLANES
    tiles = nrow * ng
    vmem = pl.BlockSpec(memory_space=pltpu.VMEM)
    hbm = pl.BlockSpec(memory_space=pltpu.HBM)
    inputs = [
        pltpu.with_memory_space_constraint(value, pltpu.HBM)
        for value in (
            jnp.transpose(orbitals[0], (1, 0, 2)), jnp.transpose(region, (1, 0, 2)), potential_table, counts, ritz.T
        )
    ]
    late = sorted(range(tiles), key=lambda place: (place % ng // (ng // 2), place // ng, place % ng), reverse=True)
    order = [place for pair in zip(late, late[::-1]) for place in pair][:tiles]
    packed_bytes = 4 * tiles * rows * LANES
    loaded = [
        pltpu.VMEM((ys, planes, xs), jnp.float32),
        pltpu.VMEM((ys, planes, xs), jnp.int32),
        pltpu.SMEM(potential_table.shape, jnp.float32),
        pltpu.SMEM(counts.shape, jnp.int32),
        pltpu.VMEM((columns, panel), jnp.float32),
        pltpu.SemaphoreType.DMA((5,)),
    ]
    limit = pltpu.CompilerParams(vmem_limit_bytes=4 * packed_bytes + 64 * cells + 2**20)
    natural = jax.ShapeDtypeStruct((ng * rows, LANES), jnp.float32)
    across = [(core, cores - 1 - core) for core in range(cores)]

    def exchange(packed, height):
        return lax.all_to_all(
            packed.reshape(tiles, height, LANES), ("row", "grid"), split_axis=0, concat_axis=0, tiled=True,
            axis_index_groups=[order],
        )

    if cores == 2 and columns * width <= LANES and tiles <= 64 and panel == ng and panel <= 16:
        other_orb = jnp.transpose(lax.ppermute(orbitals, "core", across)[0], (1, 0, 2))
        other_ritz = lax.ppermute(ritz, "core", across).T
        own, diagonal, mask = pl.pallas_call(
            functools.partial(own_kernel, ng, rows, run, width, cores),
            out_shape=[
                natural,
                jax.ShapeDtypeStruct((ys, planes, xs), jnp.float32),
                jax.ShapeDtypeStruct((planes, xs), jnp.float32),
            ],
            in_specs=[hbm] * 5,
            out_specs=[vmem] * 3,
            scratch_shapes=loaded,
            compiler_params=limit,
            name="own_filter",
        )(*inputs)
        packed = pl.pallas_call(
            functools.partial(other_kernel, ng, rows, run, width, order),
            out_shape=jax.ShapeDtypeStruct((2 * tiles * rows, LANES), jnp.float32),
            in_specs=[vmem] * 5,
            out_specs=vmem,
            scratch_shapes=[pltpu.VMEM((ng * rows, LANES), jnp.float32)],
            compiler_params=limit,
            name="other_filter",
        )(other_orb, other_ritz, own, diagonal, mask)
        return pl.pallas_call(
            functools.partial(rotate_kernel, nrow, ng, rows, run, width, columns, cores, order),
            out_shape=jax.ShapeDtypeStruct((panel, run * LANES), jnp.float32),
            in_specs=[vmem],
            out_specs=vmem,
            scratch_shapes=[pltpu.VMEM((2, tiles, 1, LANES), jnp.float32)],
            compiler_params=limit,
            name="ritz_rotation",
        )(exchange(packed, 2 * rows))

    packed = pl.pallas_call(
        functools.partial(filter_kernel, ng, rows, run, width, cores, order),
        out_shape=jax.ShapeDtypeStruct((tiles * rows, LANES), jnp.float32),
        in_specs=[hbm] * 5,
        out_specs=vmem,
        scratch_shapes=loaded + [pltpu.VMEM((ng * rows, LANES), jnp.float32)],
        compiler_params=limit,
        name="chebyshev_filter",
    )(*inputs)
    by_source = exchange(packed, rows)[jnp.argsort(jnp.array(order))].reshape(nrow, ng, rows, LANES)
    fields = by_source[:, :, :run].reshape(tiles, run * LANES)
    blocks = by_source[:, :, run : run + ritz_rows].reshape(nrow, ng, ritz_rows * per_row, width)

    def partial_sums(distance):
        holders = panel // columns
        block = lax.axis_index("row") * cores + lax.rem(lax.axis_index("core") + distance, cores)
        mine = lax.dynamic_slice_in_dim(blocks, block * holders, holders, axis=1)
        return lax.dot_general(
            jnp.transpose(mine[:, :, :columns, :panel], (0, 3, 1, 2)).reshape(tiles, panel),
            fields,
            (((0,), (0,)), ((), ())),
            precision=lax.Precision.HIGHEST,
            preferred_element_type=jnp.float32,
        )

    total = partial_sums(0)
    if cores == 2:
        total = lax.ppermute(partial_sums(1), "core", across) + total
    return total


def solution(mesh):
    bands, ng = mesh.shape["band"], mesh.shape["grid"]
    cores = 2 if bands % 2 == 0 else 1
    nrow = bands // cores
    split = jax.sharding.Mesh(mesh.devices.reshape(nrow, cores, ng), ("row", "core", "grid"))
    return jax.shard_map(
        functools.partial(shards, nrow, cores, ng),
        mesh=split,
        in_specs=(P(("row", "core", "grid"), None, None, None), P(), P(), P(), P(("row", "core"), "grid")),
        out_specs=P(("row", "core"), "grid"),
        check_vma=False,
    )
```

```python
import functools

import jax
import jax.numpy as jnp
from jax import lax
from jax.experimental import pallas as pl
from jax.experimental.pallas import tpu as pltpu
from jax.sharding import PartitionSpec as P

DEGREE = 4

COEFFICIENTS = (
    -5369.0 / 1800.0,
    12.0 / 7.0,
    -15.0 / 56.0,
    10.0 / 189.0,
    -1.0 / 112.0,
    2.0 / 1925.0,
    -1.0 / 16632.0,
)
SPACING = 0.5
LOWER = 6.0
UPPER = 46.0
HALF = (UPPER - LOWER) / 2.0
CENTRE = (UPPER + LOWER) / 2.0
LANES = 128
SUBLANES = 8


def ring_weights(length):
    weights = [0.0] * length
    for offset in range(1, 7):
        weights[offset % length] += COEFFICIENTS[offset]
        weights[-offset % length] += COEFFICIENTS[offset]
    return weights


def pair_weights(length):
    weights = ring_weights(length)
    pairs = []
    for distance in range(1, length // 2 + 1):
        if weights[distance] != 0.0:
            pairs.append((sorted({distance, length - distance}), weights[distance]))
    return weights[0], pairs


def apply(field, diagonal, hop, before):
    ys = len(field)
    planes, xs = field[0].shape
    along_y, along_planes, along_x = [pair_weights(length)[1] for length in (ys, planes, xs)]
    results = []
    for y in range(ys):
        tile = field[y]
        total = diagonal[y] * tile
        if before is not None:
            total = total - before[y]
        for shifts, weight in along_y:
            total = total + (hop * weight) * functools.reduce(jnp.add, [field[(y - shift) % ys] for shift in shifts])
        for pairs, axis in ((along_planes, 0), (along_x, 1)):
            for shifts, weight in pairs:
                total = total + (hop * weight) * functools.reduce(
                    jnp.add, [pltpu.roll(tile, shift, axis) for shift in shifts]
                )
        results.append(total)
    return results


def filter_kernel(ng, copies, rows, used, run, width, cores, order, *refs):
    sources, out_ref, held, sems, natural_ref = refs[:5], refs[5], refs[6:11], refs[11], refs[12]
    orb_ref, region_ref, table_ref, counts_ref, ritz_ref = held
    transfers = [
        pltpu.make_async_copy(source, target, sems.at[index])
        for index, (source, target) in enumerate(zip(sources, held))
    ]
    for transfer in transfers:
        transfer.start()
    for transfer in transfers:
        transfer.wait()
    ys, planes, xs = orb_ref.shape
    columns, panel = ritz_ref.shape
    per_row = LANES // width
    for row in range(-(-columns // per_row)):
        line = jnp.zeros((1, LANES), jnp.float32)
        for slot in range(min(per_row, columns - row * per_row)):
            piece = jnp.concatenate(
                [ritz_ref[pl.ds(row * per_row + slot, 1), :], jnp.zeros((1, LANES - panel), jnp.float32)], axis=1
            )
            line = line + (pltpu.roll(piece, slot * width, 1) if slot else piece)
        natural_ref[pl.ds(run + row, ng, stride=rows), :] = jnp.broadcast_to(line, (ng, LANES))

    centre_weight = 3.0 * COEFFICIENTS[0] + sum(pair_weights(n)[0] for n in (planes, ys, xs))
    scale = 2.0 / HALF
    hop = -0.5 / (SPACING * SPACING) * scale
    diagonal = []
    for y in range(ys):
        region = region_ref[y]
        potential = jnp.zeros((planes, xs), jnp.float32)
        for index in range(table_ref.shape[0]):
            potential = jnp.where(region == index, table_ref[index], potential)
        diagonal.append(scale * potential + (hop * centre_weight - scale * CENTRE))
    band_pos = lax.axis_index("row") * cores + lax.axis_index("core")
    live = (lax.axis_index("grid") < counts_ref[band_pos]).astype(jnp.float32)
    previous = [live * orb_ref[y] for y in range(ys)]
    current = apply(previous, [0.5 * value for value in diagonal], 0.5 * hop, None)
    for _ in range(DEGREE - 1):
        previous, current = current, apply(current, diagonal, hop, previous)

    blocks = ys // run
    for y in range(ys):
        natural_ref[pl.ds((y // run) * rows + y % run, planes, stride=blocks * rows), :] = current[y]
    for copy in range(copies):
        for tile in range(ng):
            place = order.index(copy * ng + tile)
            out_ref[pl.ds(place * used, used), :] = natural_ref[pl.ds(tile * rows, used), :]


def partial_kernel(nrow, ng, used, run, width, columns, cores, order, distance, got_ref, out_ref, ritz_ref):
    for place, source in enumerate(order):
        ritz_ref[source] = got_ref[pl.ds(place * used + run, 1), :]
    wanted = out_ref.shape[0]
    holders = wanted // columns
    sublane = lax.broadcasted_iota(jnp.int32, (wanted, LANES), 0)
    block = lax.axis_index("row") * cores + lax.rem(lax.axis_index("core") + distance, cores)
    acc = [jnp.zeros((wanted, LANES), jnp.float32) for _ in range(run)]
    for row in range(nrow):
        lines = jnp.zeros((wanted, LANES), jnp.float32)
        for k in range(holders):
            line = ritz_ref[row * ng + block * holders + k]
            lines = jnp.where(sublane // columns == k, jnp.broadcast_to(line, (wanted, LANES)), lines)
        for r in range(ng):
            weight = jnp.take_along_axis(lines, sublane % columns * width + r, axis=1)
            for y in range(run):
                acc[y] = acc[y] + weight * got_ref[pl.ds(order.index(row * ng + r) * used + y, 1), :]
    for y in range(run):
        out_ref[:, pl.ds(y * LANES, LANES)] = acc[y]


def shards(nrow, cores, ng, orbitals, region, potential_table, counts, ritz):
    _, planes, ys, xs = orbitals.shape
    cells = planes * ys * xs
    panel, columns = ritz.shape
    run = cells // ng // xs
    width = 1
    while width < panel:
        width *= 2
    per_row = LANES // width
    ritz_rows = -(-columns // per_row)
    used = run + ritz_rows
    rows = -(-used // SUBLANES) * SUBLANES
    tiles = nrow * ng
    vmem = pl.BlockSpec(memory_space=pltpu.VMEM)
    hbm = pl.BlockSpec(memory_space=pltpu.HBM)
    inputs = [
        pltpu.with_memory_space_constraint(value, pltpu.HBM)
        for value in (
            jnp.transpose(orbitals[0], (1, 0, 2)), jnp.transpose(region, (1, 0, 2)), potential_table, counts, ritz.T
        )
    ]
    late = sorted(range(tiles), key=lambda place: (place % ng // (ng // 2), place // ng, place % ng), reverse=True)
    order = [place for pair in zip(late, late[::-1]) for place in pair][:tiles]
    packed_bytes = 4 * tiles * rows * LANES
    packed = pl.pallas_call(
        functools.partial(filter_kernel, ng, nrow, rows, used, run, width, cores, order),
        out_shape=jax.ShapeDtypeStruct((tiles * used, LANES), jnp.float32),
        in_specs=[hbm] * 5,
        out_specs=vmem,
        scratch_shapes=[
            pltpu.VMEM((ys, planes, xs), jnp.float32),
            pltpu.VMEM((ys, planes, xs), jnp.int32),
            pltpu.SMEM(potential_table.shape, jnp.float32),
            pltpu.SMEM(counts.shape, jnp.int32),
            pltpu.VMEM((columns, panel), jnp.float32),
            pltpu.SemaphoreType.DMA((5,)),
            pltpu.VMEM((ng * rows, LANES), jnp.float32),
        ],
        compiler_params=pltpu.CompilerParams(vmem_limit_bytes=2 * packed_bytes + 64 * cells + 2**20),
        name="chebyshev_filter",
    )(*inputs)
    got = lax.all_to_all(
        packed.reshape(tiles * used, 1, LANES), ("row", "grid"), split_axis=0, concat_axis=0, tiled=True,
        axis_index_groups=[order],
    ).reshape(tiles * used, LANES)
    sum_shape = jax.ShapeDtypeStruct((panel, run * LANES), jnp.float32)
    if columns * width <= LANES and tiles <= 64 and panel == ng and panel <= 16:
        def partial_sums(distance):
            return pl.pallas_call(
                functools.partial(partial_kernel, nrow, ng, used, run, width, columns, cores, order, distance),
                out_shape=sum_shape,
                in_specs=[vmem],
                out_specs=vmem,
                scratch_shapes=[pltpu.VMEM((tiles, 1, LANES), jnp.float32)],
                compiler_params=pltpu.CompilerParams(vmem_limit_bytes=packed_bytes + 2**20),
                name="ritz_partial_sums",
            )(got)

    else:
        holders = panel // columns
        by_source = got.reshape(tiles, used, LANES)[jnp.argsort(jnp.array(order))].reshape(nrow, ng, used, LANES)
        fields = by_source[:, :, :run].reshape(tiles, run * LANES)
        blocks = by_source[:, :, run : run + ritz_rows].reshape(nrow, ng, ritz_rows * per_row, width)

        def partial_sums(distance):
            block = lax.axis_index("row") * cores + lax.rem(lax.axis_index("core") + distance, cores)
            mine = lax.dynamic_slice_in_dim(blocks, block * holders, holders, axis=1)
            return lax.dot_general(
                jnp.transpose(mine[:, :, :columns, :panel], (0, 3, 1, 2)).reshape(tiles, panel),
                fields,
                (((0,), (0,)), ((), ())),
                precision=lax.Precision.HIGHEST,
                preferred_element_type=jnp.float32,
            )

    terms = []
    for distance in range(1, cores):
        pairs = [(core, (core + distance) % cores) for core in range(cores)]
        terms.append(lax.ppermute(partial_sums(distance), "core", pairs))
    terms.append(partial_sums(0))
    return functools.reduce(jnp.add, terms)


def solution(mesh):
    bands, ng = mesh.shape["band"], mesh.shape["grid"]
    cores = 2 if bands % 2 == 0 else 1
    nrow = bands // cores
    split = jax.sharding.Mesh(mesh.devices.reshape(nrow, cores, ng), ("row", "core", "grid"))
    return jax.shard_map(
        functools.partial(shards, nrow, cores, ng),
        mesh=split,
        in_specs=(P(("row", "core", "grid"), None, None, None), P(), P(), P(), P(("row", "core"), "grid")),
        out_specs=P(("row", "core"), "grid"),
        check_vma=False,
    )
```

```python
import functools

import jax
import jax.numpy as jnp
from jax import lax
from jax.experimental import pallas as pl
from jax.experimental.pallas import tpu as pltpu
from jax.sharding import PartitionSpec as P

DEGREE = 4

COEFFICIENTS = (
    -5369.0 / 1800.0,
    12.0 / 7.0,
    -15.0 / 56.0,
    10.0 / 189.0,
    -1.0 / 112.0,
    2.0 / 1925.0,
    -1.0 / 16632.0,
)
SPACING = 0.5
LOWER = 6.0
UPPER = 46.0
HALF = (UPPER - LOWER) / 2.0
CENTRE = (UPPER + LOWER) / 2.0
LANES = 128
SUBLANES = 8


def ring_weights(length):
    weights = [0.0] * length
    for offset in range(1, 7):
        weights[offset % length] += COEFFICIENTS[offset]
        weights[-offset % length] += COEFFICIENTS[offset]
    return weights


def pair_weights(length):
    weights = ring_weights(length)
    pairs = []
    for distance in range(1, length // 2 + 1):
        if weights[distance] != 0.0:
            pairs.append((sorted({distance, length - distance}), weights[distance]))
    return weights[0], pairs


def apply(field, diagonal, hop, before):
    ys = len(field)
    planes, xs = field[0].shape
    along_y, along_planes, along_x = [pair_weights(length)[1] for length in (ys, planes, xs)]
    results = []
    for y in range(ys):
        tile = field[y]
        total = diagonal[y] * tile
        if before is not None:
            total = total - before[y]
        for shifts, weight in along_y:
            total = total + (hop * weight) * functools.reduce(jnp.add, [field[(y - shift) % ys] for shift in shifts])
        for pairs, axis in ((along_planes, 0), (along_x, 1)):
            for shifts, weight in pairs:
                total = total + (hop * weight) * functools.reduce(
                    jnp.add, [pltpu.roll(tile, shift, axis) for shift in shifts]
                )
        results.append(total)
    return results


def place_of(chip, order):
    place = order.index(chip)
    if place == 0:
        return place
    return jnp.where(lax.axis_index("core") == 0, place, len(order) - place)


def filter_kernel(ng, copies, rows, used, run, width, cores, order, *refs):
    sources, out_ref, held, sems, natural_ref = refs[:5], refs[5], refs[6:11], refs[11], refs[12]
    orb_ref, region_ref, table_ref, counts_ref, ritz_ref = held
    transfers = [
        pltpu.make_async_copy(source, target, sems.at[index])
        for index, (source, target) in enumerate(zip(sources, held))
    ]
    for transfer in transfers:
        transfer.start()
    for transfer in transfers:
        transfer.wait()
    ys, planes, xs = orb_ref.shape
    columns, panel = ritz_ref.shape
    per_row = LANES // width
    for row in range(-(-columns // per_row)):
        line = jnp.zeros((1, LANES), jnp.float32)
        for slot in range(min(per_row, columns - row * per_row)):
            piece = jnp.concatenate(
                [ritz_ref[pl.ds(row * per_row + slot, 1), :], jnp.zeros((1, LANES - panel), jnp.float32)], axis=1
            )
            line = line + (pltpu.roll(piece, slot * width, 1) if slot else piece)
        natural_ref[pl.ds(run + row, ng, stride=rows), :] = jnp.broadcast_to(line, (ng, LANES))

    centre_weight = 3.0 * COEFFICIENTS[0] + sum(pair_weights(n)[0] for n in (planes, ys, xs))
    scale = 2.0 / HALF
    hop = -0.5 / (SPACING * SPACING) * scale
    diagonal = []
    for y in range(ys):
        region = region_ref[y]
        potential = jnp.zeros((planes, xs), jnp.float32)
        for index in range(table_ref.shape[0]):
            potential = jnp.where(region == index, table_ref[index], potential)
        diagonal.append(scale * potential + (hop * centre_weight - scale * CENTRE))
    band_pos = lax.axis_index("row") * cores + lax.axis_index("core")
    live = (lax.axis_index("grid") < counts_ref[band_pos]).astype(jnp.float32)
    previous = [live * orb_ref[y] for y in range(ys)]
    current = apply(previous, [0.5 * value for value in diagonal], 0.5 * hop, None)
    for _ in range(DEGREE - 1):
        previous, current = current, apply(current, diagonal, hop, previous)

    blocks = ys // run
    for y in range(ys):
        natural_ref[pl.ds((y // run) * rows + y % run, planes, stride=blocks * rows), :] = current[y]
    for copy in range(copies):
        for tile in range(ng):
            place = place_of(copy * ng + tile, order)
            out_ref[pl.ds(place * used, used), :] = natural_ref[pl.ds(tile * rows, used), :]


def partial_kernel(nrow, ng, used, run, width, columns, cores, order, distance, got_ref, out_ref, ritz_ref):
    places = [place_of(chip, order) for chip in range(nrow * ng)]
    for chip, place in enumerate(places):
        ritz_ref[chip] = got_ref[pl.ds(place * used + run, 1), :]
    wanted = out_ref.shape[0]
    holders = wanted // columns
    sublane = lax.broadcasted_iota(jnp.int32, (wanted, LANES), 0)
    block = lax.axis_index("row") * cores + lax.rem(lax.axis_index("core") + distance, cores)
    acc = [jnp.zeros((wanted, LANES), jnp.float32) for _ in range(run)]
    for row in range(nrow):
        lines = jnp.zeros((wanted, LANES), jnp.float32)
        for k in range(holders):
            line = ritz_ref[row * ng + block * holders + k]
            lines = jnp.where(sublane // columns == k, jnp.broadcast_to(line, (wanted, LANES)), lines)
        for r in range(ng):
            weight = jnp.take_along_axis(lines, sublane % columns * width + r, axis=1)
            for y in range(run):
                acc[y] = acc[y] + weight * got_ref[pl.ds(places[row * ng + r] * used + y, 1), :]
    for y in range(run):
        out_ref[:, pl.ds(y * LANES, LANES)] = acc[y]


def shards(nrow, cores, ng, orbitals, region, potential_table, counts, ritz):
    _, planes, ys, xs = orbitals.shape
    cells = planes * ys * xs
    panel, columns = ritz.shape
    run = cells // ng // xs
    width = 1
    while width < panel:
        width *= 2
    per_row = LANES // width
    ritz_rows = -(-columns // per_row)
    used = run + ritz_rows
    rows = -(-used // SUBLANES) * SUBLANES
    tiles = nrow * ng
    vmem = pl.BlockSpec(memory_space=pltpu.VMEM)
    hbm = pl.BlockSpec(memory_space=pltpu.HBM)
    inputs = [
        pltpu.with_memory_space_constraint(value, pltpu.HBM)
        for value in (
            jnp.transpose(orbitals[0], (1, 0, 2)), jnp.transpose(region, (1, 0, 2)), potential_table, counts, ritz.T
        )
    ]
    late = sorted(range(tiles), key=lambda place: (place % ng // (ng // 2), place // ng, place % ng), reverse=True)
    order = [place for pair in zip(late, late[::-1]) for place in pair][:tiles]
    packed_bytes = 4 * tiles * rows * LANES
    packed = pl.pallas_call(
        functools.partial(filter_kernel, ng, nrow, rows, used, run, width, cores, order),
        out_shape=jax.ShapeDtypeStruct((tiles * used, LANES), jnp.float32),
        in_specs=[hbm] * 5,
        out_specs=vmem,
        scratch_shapes=[
            pltpu.VMEM((ys, planes, xs), jnp.float32),
            pltpu.VMEM((ys, planes, xs), jnp.int32),
            pltpu.SMEM(potential_table.shape, jnp.float32),
            pltpu.SMEM(counts.shape, jnp.int32),
            pltpu.VMEM((columns, panel), jnp.float32),
            pltpu.SemaphoreType.DMA((5,)),
            pltpu.VMEM((ng * rows, LANES), jnp.float32),
        ],
        compiler_params=pltpu.CompilerParams(vmem_limit_bytes=2 * packed_bytes + 64 * cells + 2**20),
        name="chebyshev_filter",
    )(*inputs)
    got = lax.all_to_all(
        packed.reshape(tiles * used, 1, LANES), ("row", "core", "grid"), split_axis=0, concat_axis=0, tiled=True,
        axis_index_groups=[
            [(chip // ng * cores + core) * ng + chip % ng for chip in (order[:1] + order[:0:-1] if core else order)]
            for core in range(cores)
        ],
    ).reshape(tiles * used, LANES)
    sum_shape = jax.ShapeDtypeStruct((panel, run * LANES), jnp.float32)
    if columns * width <= LANES and tiles <= 64 and panel == ng and panel <= 16:
        def partial_sums(distance):
            return pl.pallas_call(
                functools.partial(partial_kernel, nrow, ng, used, run, width, columns, cores, order, distance),
                out_shape=sum_shape,
                in_specs=[vmem],
                out_specs=vmem,
                scratch_shapes=[pltpu.VMEM((tiles, 1, LANES), jnp.float32)],
                compiler_params=pltpu.CompilerParams(vmem_limit_bytes=packed_bytes + 2**20),
                name="ritz_partial_sums",
            )(got)

    else:
        holders = panel // columns
        by_source = got.reshape(tiles, used, LANES)[jnp.stack([place_of(chip, order) for chip in range(tiles)])].reshape(nrow, ng, used, LANES)
        fields = by_source[:, :, :run].reshape(tiles, run * LANES)
        blocks = by_source[:, :, run : run + ritz_rows].reshape(nrow, ng, ritz_rows * per_row, width)

        def partial_sums(distance):
            block = lax.axis_index("row") * cores + lax.rem(lax.axis_index("core") + distance, cores)
            mine = lax.dynamic_slice_in_dim(blocks, block * holders, holders, axis=1)
            return lax.dot_general(
                jnp.transpose(mine[:, :, :columns, :panel], (0, 3, 1, 2)).reshape(tiles, panel),
                fields,
                (((0,), (0,)), ((), ())),
                precision=lax.Precision.HIGHEST,
                preferred_element_type=jnp.float32,
            )

    terms = []
    for distance in range(1, cores):
        pairs = [(core, (core + distance) % cores) for core in range(cores)]
        terms.append(lax.ppermute(partial_sums(distance), "core", pairs))
    terms.append(partial_sums(0))
    return functools.reduce(jnp.add, terms)


def solution(mesh):
    bands, ng = mesh.shape["band"], mesh.shape["grid"]
    cores = 2 if bands % 2 == 0 else 1
    nrow = bands // cores
    split = jax.sharding.Mesh(mesh.devices.reshape(nrow, cores, ng), ("row", "core", "grid"))
    return jax.shard_map(
        functools.partial(shards, nrow, cores, ng),
        mesh=split,
        in_specs=(P(("row", "core", "grid"), None, None, None), P(), P(), P(), P(("row", "core"), "grid")),
        out_specs=P(("row", "core"), "grid"),
        check_vma=False,
    )
```

```python
import functools

import jax
import jax.numpy as jnp
from jax import lax
from jax.experimental import pallas as pl
from jax.experimental.pallas import tpu as pltpu
from jax.sharding import PartitionSpec as P

DEGREE = 4

COEFFICIENTS = (
    -5369.0 / 1800.0,
    12.0 / 7.0,
    -15.0 / 56.0,
    10.0 / 189.0,
    -1.0 / 112.0,
    2.0 / 1925.0,
    -1.0 / 16632.0,
)
SPACING = 0.5
LOWER = 6.0
UPPER = 46.0
HALF = (UPPER - LOWER) / 2.0
CENTRE = (UPPER + LOWER) / 2.0
LANES = 128
SUBLANES = 8


def ring_weights(length):
    weights = [0.0] * length
    for offset in range(1, 7):
        weights[offset % length] += COEFFICIENTS[offset]
        weights[-offset % length] += COEFFICIENTS[offset]
    return weights


def pair_weights(length):
    weights = ring_weights(length)
    pairs = []
    for distance in range(1, length // 2 + 1):
        if weights[distance] != 0.0:
            pairs.append((sorted({distance, length - distance}), weights[distance]))
    return weights[0], pairs


def apply(field, diagonal, hop, before):
    ys = len(field)
    planes, xs = field[0].shape
    along_y, along_planes, along_x = [pair_weights(length)[1] for length in (ys, planes, xs)]
    results = []
    for y in range(ys):
        tile = field[y]
        total = diagonal[y] * tile
        if before is not None:
            total = total - before[y]
        for shifts, weight in along_y:
            total = total + (hop * weight) * functools.reduce(jnp.add, [field[(y - shift) % ys] for shift in shifts])
        for pairs, axis in ((along_planes, 0), (along_x, 1)):
            for shifts, weight in pairs:
                total = total + (hop * weight) * functools.reduce(
                    jnp.add, [pltpu.roll(tile, shift, axis) for shift in shifts]
                )
        results.append(total)
    return results


def filter_kernel(ng, copies, rows, used, run, width, cores, order, *refs):
    sources, out_ref, held, sems, natural_ref = refs[:5], refs[5], refs[6:11], refs[11], refs[12]
    orb_ref, region_ref, table_ref, counts_ref, ritz_ref = held
    transfers = [
        pltpu.make_async_copy(source, target, sems.at[index])
        for index, (source, target) in enumerate(zip(sources, held))
    ]
    for transfer in transfers:
        transfer.start()
    for transfer in transfers:
        transfer.wait()
    ys, planes, xs = orb_ref.shape
    columns, panel = ritz_ref.shape
    per_row = LANES // width
    for row in range(-(-columns // per_row)):
        line = jnp.zeros((1, LANES), jnp.float32)
        for slot in range(min(per_row, columns - row * per_row)):
            piece = jnp.concatenate(
                [ritz_ref[pl.ds(row * per_row + slot, 1), :], jnp.zeros((1, LANES - panel), jnp.float32)], axis=1
            )
            line = line + (pltpu.roll(piece, slot * width, 1) if slot else piece)
        natural_ref[pl.ds(run + row, ng, stride=rows), :] = jnp.broadcast_to(line, (ng, LANES))

    centre_weight = 3.0 * COEFFICIENTS[0] + sum(pair_weights(n)[0] for n in (planes, ys, xs))
    scale = 2.0 / HALF
    hop = -0.5 / (SPACING * SPACING) * scale
    regions = table_ref.shape[1]
    values = jnp.concatenate([table_ref[...], jnp.zeros((1, xs - regions), jnp.float32)], axis=1)
    values = jnp.broadcast_to(values, (planes, xs))
    diagonal = []
    for y in range(ys):
        potential = jnp.take_along_axis(values, region_ref[y], axis=1)
        diagonal.append(scale * potential + (hop * centre_weight - scale * CENTRE))
    band_pos = lax.axis_index("row") * cores + lax.axis_index("core")
    band = lax.broadcasted_iota(jnp.int32, counts_ref.shape, 1)
    count = jnp.sum(jnp.where(band == band_pos, counts_ref[...], 0), axis=1, keepdims=True)
    live = (lax.axis_index("grid") < count).astype(jnp.float32)
    previous = [orb_ref[y] for y in range(ys)]
    current = apply(previous, [0.5 * value for value in diagonal], 0.5 * hop, None)
    for _ in range(DEGREE - 1):
        previous, current = current, apply(current, diagonal, hop, previous)

    blocks = ys // run
    for y in range(ys):
        natural_ref[pl.ds((y // run) * rows + y % run, planes, stride=blocks * rows), :] = live * current[y]
    for copy in range(copies):
        for tile in range(ng):
            place = order.index(copy * ng + tile)
            out_ref[pl.ds(place * used, used), :] = natural_ref[pl.ds(tile * rows, used), :]


def partial_kernel(nrow, ng, used, run, width, columns, cores, order, distance, got_ref, out_ref, ritz_ref):
    for place, source in enumerate(order):
        ritz_ref[source] = got_ref[pl.ds(place * used + run, 1), :]
    wanted = out_ref.shape[0]
    holders = wanted // columns
    sublane = lax.broadcasted_iota(jnp.int32, (wanted, LANES), 0)
    block = lax.axis_index("row") * cores + lax.rem(lax.axis_index("core") + distance, cores)
    acc = [jnp.zeros((wanted, LANES), jnp.float32) for _ in range(run)]
    for row in range(nrow):
        lines = jnp.zeros((wanted, LANES), jnp.float32)
        for k in range(holders):
            line = ritz_ref[row * ng + block * holders + k]
            lines = jnp.where(sublane // columns == k, jnp.broadcast_to(line, (wanted, LANES)), lines)
        for r in range(ng):
            weight = jnp.take_along_axis(lines, sublane % columns * width + r, axis=1)
            for y in range(run):
                acc[y] = acc[y] + weight * got_ref[pl.ds(order.index(row * ng + r) * used + y, 1), :]
    for y in range(run):
        out_ref[:, pl.ds(y * LANES, LANES)] = acc[y]


def shards(nrow, cores, ng, orbitals, region, potential_table, counts, ritz):
    _, planes, ys, xs = orbitals.shape
    cells = planes * ys * xs
    panel, columns = ritz.shape
    run = cells // ng // xs
    width = 1
    while width < panel:
        width *= 2
    per_row = LANES // width
    ritz_rows = -(-columns // per_row)
    used = run + ritz_rows
    rows = -(-used // SUBLANES) * SUBLANES
    tiles = nrow * ng
    vmem = pl.BlockSpec(memory_space=pltpu.VMEM)
    hbm = pl.BlockSpec(memory_space=pltpu.HBM)
    inputs = [
        pltpu.with_memory_space_constraint(value, pltpu.HBM)
        for value in (
            jnp.transpose(orbitals[0], (1, 0, 2)), jnp.transpose(region, (1, 0, 2)), potential_table[None], counts[None], ritz.T
        )
    ]
    late = sorted(range(tiles), key=lambda place: (place % ng // (ng // 2), place // ng, place % ng), reverse=True)
    order = [place for pair in zip(late, late[::-1]) for place in pair][:tiles]
    packed_bytes = 4 * tiles * rows * LANES
    packed = pl.pallas_call(
        functools.partial(filter_kernel, ng, nrow, rows, used, run, width, cores, order),
        out_shape=jax.ShapeDtypeStruct((tiles * used, LANES), jnp.float32),
        in_specs=[hbm] * 5,
        out_specs=vmem,
        scratch_shapes=[
            pltpu.VMEM((ys, planes, xs), jnp.float32),
            pltpu.VMEM((ys, planes, xs), jnp.int32),
            pltpu.VMEM((1,) + potential_table.shape, jnp.float32),
            pltpu.VMEM((1,) + counts.shape, jnp.int32),
            pltpu.VMEM((columns, panel), jnp.float32),
            pltpu.SemaphoreType.DMA((5,)),
            pltpu.VMEM((ng * rows, LANES), jnp.float32),
        ],
        compiler_params=pltpu.CompilerParams(vmem_limit_bytes=2 * packed_bytes + 64 * cells + 2**20),
        name="chebyshev_filter",
    )(*inputs)
    got = lax.all_to_all(
        packed.reshape(tiles * used, 1, LANES), ("row", "grid"), split_axis=0, concat_axis=0, tiled=True,
        axis_index_groups=[order],
    ).reshape(tiles * used, LANES)
    sum_shape = jax.ShapeDtypeStruct((panel, run * LANES), jnp.float32)
    if columns * width <= LANES and tiles <= 64 and panel == ng and panel <= 16:
        def partial_sums(distance):
            return pl.pallas_call(
                functools.partial(partial_kernel, nrow, ng, used, run, width, columns, cores, order, distance),
                out_shape=sum_shape,
                in_specs=[vmem],
                out_specs=vmem,
                scratch_shapes=[pltpu.VMEM((tiles, 1, LANES), jnp.float32)],
                compiler_params=pltpu.CompilerParams(vmem_limit_bytes=packed_bytes + 2**20),
                name="ritz_partial_sums",
            )(got)

    else:
        holders = panel // columns
        by_source = got.reshape(tiles, used, LANES)[jnp.argsort(jnp.array(order))].reshape(nrow, ng, used, LANES)
        fields = by_source[:, :, :run].reshape(tiles, run * LANES)
        blocks = by_source[:, :, run : run + ritz_rows].reshape(nrow, ng, ritz_rows * per_row, width)

        def partial_sums(distance):
            block = lax.axis_index("row") * cores + lax.rem(lax.axis_index("core") + distance, cores)
            mine = lax.dynamic_slice_in_dim(blocks, block * holders, holders, axis=1)
            return lax.dot_general(
                jnp.transpose(mine[:, :, :columns, :panel], (0, 3, 1, 2)).reshape(tiles, panel),
                fields,
                (((0,), (0,)), ((), ())),
                precision=lax.Precision.HIGHEST,
                preferred_element_type=jnp.float32,
            )

    terms = []
    for distance in range(1, cores):
        pairs = [(core, (core + distance) % cores) for core in range(cores)]
        terms.append(lax.ppermute(partial_sums(distance), "core", pairs))
    terms.append(partial_sums(0))
    return functools.reduce(jnp.add, terms)


def solution(mesh):
    bands, ng = mesh.shape["band"], mesh.shape["grid"]
    cores = 2 if bands % 2 == 0 else 1
    nrow = bands // cores
    split = jax.sharding.Mesh(mesh.devices.reshape(nrow, cores, ng), ("row", "core", "grid"))
    return jax.shard_map(
        functools.partial(shards, nrow, cores, ng),
        mesh=split,
        in_specs=(P(("row", "core", "grid"), None, None, None), P(), P(), P(), P(("row", "core"), "grid")),
        out_specs=P(("row", "core"), "grid"),
        check_vma=False,
    )
```

```python
import functools

import jax
import jax.numpy as jnp
from jax import lax
from jax.experimental import pallas as pl
from jax.experimental.pallas import tpu as pltpu
from jax.sharding import PartitionSpec as P

DEGREE = 4

COEFFICIENTS = (
    -5369.0 / 1800.0,
    12.0 / 7.0,
    -15.0 / 56.0,
    10.0 / 189.0,
    -1.0 / 112.0,
    2.0 / 1925.0,
    -1.0 / 16632.0,
)
SPACING = 0.5
LOWER = 6.0
UPPER = 46.0
HALF = (UPPER - LOWER) / 2.0
CENTRE = (UPPER + LOWER) / 2.0
LANES = 128
SUBLANES = 8


def ring_weights(length):
    weights = [0.0] * length
    for offset in range(1, 7):
        weights[offset % length] += COEFFICIENTS[offset]
        weights[-offset % length] += COEFFICIENTS[offset]
    return weights


def pair_weights(length):
    weights = ring_weights(length)
    pairs = []
    for distance in range(1, length // 2 + 1):
        if weights[distance] != 0.0:
            pairs.append((sorted({distance, length - distance}), weights[distance]))
    return weights[0], pairs


def apply(field, diagonal, hop, before):
    ys = len(field)
    planes, xs = field[0].shape
    along_y, along_planes, along_x = [pair_weights(length)[1] for length in (ys, planes, xs)]
    results = []
    for y in range(ys):
        tile = field[y]
        total = diagonal[y] * tile
        if before is not None:
            total = total - before[y]
        for shifts, weight in along_y:
            total = total + (hop * weight) * functools.reduce(jnp.add, [field[(y - shift) % ys] for shift in shifts])
        for pairs, axis in ((along_planes, 0), (along_x, 1)):
            for shifts, weight in pairs:
                total = total + (hop * weight) * functools.reduce(
                    jnp.add, [pltpu.roll(tile, shift, axis) for shift in shifts]
                )
        results.append(total)
    return results


def filter_kernel(ng, copies, rows, used, run, width, cores, order, *refs):
    sources, out_ref, held, sems, natural_ref = refs[:5], refs[5], refs[6:11], refs[11], refs[12]
    orb_ref, region_ref, table_ref, counts_ref, ritz_ref = held
    transfers = [
        pltpu.make_async_copy(source, target, sems.at[index])
        for index, (source, target) in enumerate(zip(sources, held))
    ]
    for transfer in transfers:
        transfer.start()
    for transfer in transfers[:3]:
        transfer.wait()
    ys, planes, xs = orb_ref.shape

    centre_weight = 3.0 * COEFFICIENTS[0] + sum(pair_weights(n)[0] for n in (planes, ys, xs))
    scale = 2.0 / HALF
    hop = -0.5 / (SPACING * SPACING) * scale
    regions = table_ref.shape[1]
    values = jnp.concatenate([table_ref[...], jnp.zeros((1, xs - regions), jnp.float32)], axis=1)
    values = jnp.broadcast_to(values, (planes, xs))
    diagonal = []
    for y in range(ys):
        potential = jnp.take_along_axis(values, region_ref[y], axis=1)
        diagonal.append(scale * potential + (hop * centre_weight - scale * CENTRE))
    previous = [orb_ref[y] for y in range(ys)]
    current = apply(previous, [0.5 * value for value in diagonal], 0.5 * hop, None)
    for transfer in transfers[3:]:
        transfer.wait()
    columns, panel = ritz_ref.shape
    per_row = LANES // width
    for row in range(-(-columns // per_row)):
        line = jnp.zeros((1, LANES), jnp.float32)
        for slot in range(min(per_row, columns - row * per_row)):
            piece = jnp.concatenate(
                [ritz_ref[pl.ds(row * per_row + slot, 1), :], jnp.zeros((1, LANES - panel), jnp.float32)], axis=1
            )
            line = line + (pltpu.roll(piece, slot * width, 1) if slot else piece)
        natural_ref[pl.ds(run + row, ng, stride=rows), :] = jnp.broadcast_to(line, (ng, LANES))
    band_pos = lax.axis_index("row") * cores + lax.axis_index("core")
    band = lax.broadcasted_iota(jnp.int32, counts_ref.shape, 1)
    count = jnp.sum(jnp.where(band == band_pos, counts_ref[...], 0), axis=1, keepdims=True)
    live = (lax.axis_index("grid") < count).astype(jnp.float32)
    for _ in range(DEGREE - 1):
        previous, current = current, apply(current, diagonal, hop, previous)

    blocks = ys // run
    for y in range(ys):
        natural_ref[pl.ds((y // run) * rows + y % run, planes, stride=blocks * rows), :] = live * current[y]
    for copy in range(copies):
        for tile in range(ng):
            place = order.index(copy * ng + tile)
            out_ref[pl.ds(place * used, used), :] = natural_ref[pl.ds(tile * rows, used), :]


def partial_kernel(nrow, ng, used, run, width, columns, cores, order, distance, got_ref, out_ref, ritz_ref):
    for place, source in enumerate(order):
        ritz_ref[source] = got_ref[pl.ds(place * used + run, 1), :]
    wanted = out_ref.shape[0]
    holders = wanted // columns
    sublane = lax.broadcasted_iota(jnp.int32, (wanted, LANES), 0)
    block = lax.axis_index("row") * cores + lax.rem(lax.axis_index("core") + distance, cores)
    acc = [jnp.zeros((wanted, LANES), jnp.float32) for _ in range(run)]
    for row in range(nrow):
        lines = jnp.zeros((wanted, LANES), jnp.float32)
        for k in range(holders):
            line = ritz_ref[row * ng + block * holders + k]
            lines = jnp.where(sublane // columns == k, jnp.broadcast_to(line, (wanted, LANES)), lines)
        for r in range(ng):
            weight = jnp.take_along_axis(lines, sublane % columns * width + r, axis=1)
            for y in range(run):
                acc[y] = acc[y] + weight * got_ref[pl.ds(order.index(row * ng + r) * used + y, 1), :]
    for y in range(run):
        out_ref[:, pl.ds(y * LANES, LANES)] = acc[y]


def shards(nrow, cores, ng, orbitals, region, potential_table, counts, ritz):
    _, planes, ys, xs = orbitals.shape
    cells = planes * ys * xs
    panel, columns = ritz.shape
    run = cells // ng // xs
    width = 1
    while width < panel:
        width *= 2
    per_row = LANES // width
    ritz_rows = -(-columns // per_row)
    used = run + ritz_rows
    rows = -(-used // SUBLANES) * SUBLANES
    tiles = nrow * ng
    vmem = pl.BlockSpec(memory_space=pltpu.VMEM)
    hbm = pl.BlockSpec(memory_space=pltpu.HBM)
    inputs = [
        pltpu.with_memory_space_constraint(value, pltpu.HBM)
        for value in (
            jnp.transpose(orbitals[0], (1, 0, 2)), jnp.transpose(region, (1, 0, 2)), potential_table[None], counts[None], ritz.T
        )
    ]
    late = sorted(range(tiles), key=lambda place: (place % ng // (ng // 2), place // ng, place % ng), reverse=True)
    order = [place for pair in zip(late, late[::-1]) for place in pair][:tiles]
    packed_bytes = 4 * tiles * rows * LANES
    packed = pl.pallas_call(
        functools.partial(filter_kernel, ng, nrow, rows, used, run, width, cores, order),
        out_shape=jax.ShapeDtypeStruct((tiles * used, LANES), jnp.float32),
        in_specs=[hbm] * 5,
        out_specs=vmem,
        scratch_shapes=[
            pltpu.VMEM((ys, planes, xs), jnp.float32),
            pltpu.VMEM((ys, planes, xs), jnp.int32),
            pltpu.VMEM((1,) + potential_table.shape, jnp.float32),
            pltpu.VMEM((1,) + counts.shape, jnp.int32),
            pltpu.VMEM((columns, panel), jnp.float32),
            pltpu.SemaphoreType.DMA((5,)),
            pltpu.VMEM((ng * rows, LANES), jnp.float32),
        ],
        compiler_params=pltpu.CompilerParams(vmem_limit_bytes=2 * packed_bytes + 64 * cells + 2**20),
        name="chebyshev_filter",
    )(*inputs)
    got = lax.all_to_all(
        packed.reshape(tiles * used, 1, LANES), ("row", "grid"), split_axis=0, concat_axis=0, tiled=True,
        axis_index_groups=[order],
    ).reshape(tiles * used, LANES)
    sum_shape = jax.ShapeDtypeStruct((panel, run * LANES), jnp.float32)
    if columns * width <= LANES and tiles <= 64 and panel == ng and panel <= 16:
        def partial_sums(distance):
            return pl.pallas_call(
                functools.partial(partial_kernel, nrow, ng, used, run, width, columns, cores, order, distance),
                out_shape=sum_shape,
                in_specs=[vmem],
                out_specs=vmem,
                scratch_shapes=[pltpu.VMEM((tiles, 1, LANES), jnp.float32)],
                compiler_params=pltpu.CompilerParams(vmem_limit_bytes=packed_bytes + 2**20),
                name="ritz_partial_sums",
            )(got)

    else:
        holders = panel // columns
        by_source = got.reshape(tiles, used, LANES)[jnp.argsort(jnp.array(order))].reshape(nrow, ng, used, LANES)
        fields = by_source[:, :, :run].reshape(tiles, run * LANES)
        blocks = by_source[:, :, run : run + ritz_rows].reshape(nrow, ng, ritz_rows * per_row, width)

        def partial_sums(distance):
            block = lax.axis_index("row") * cores + lax.rem(lax.axis_index("core") + distance, cores)
            mine = lax.dynamic_slice_in_dim(blocks, block * holders, holders, axis=1)
            return lax.dot_general(
                jnp.transpose(mine[:, :, :columns, :panel], (0, 3, 1, 2)).reshape(tiles, panel),
                fields,
                (((0,), (0,)), ((), ())),
                precision=lax.Precision.HIGHEST,
                preferred_element_type=jnp.float32,
            )

    terms = []
    for distance in range(1, cores):
        pairs = [(core, (core + distance) % cores) for core in range(cores)]
        terms.append(lax.ppermute(partial_sums(distance), "core", pairs))
    terms.append(partial_sums(0))
    return functools.reduce(jnp.add, terms)


def solution(mesh):
    bands, ng = mesh.shape["band"], mesh.shape["grid"]
    cores = 2 if bands % 2 == 0 else 1
    nrow = bands // cores
    split = jax.sharding.Mesh(mesh.devices.reshape(nrow, cores, ng), ("row", "core", "grid"))
    return jax.shard_map(
        functools.partial(shards, nrow, cores, ng),
        mesh=split,
        in_specs=(P(("row", "core", "grid"), None, None, None), P(), P(), P(), P(("row", "core"), "grid")),
        out_specs=P(("row", "core"), "grid"),
        check_vma=False,
    )
```

```python
import functools

import jax
import jax.numpy as jnp
from jax import lax
from jax.experimental import pallas as pl
from jax.experimental.pallas import tpu as pltpu
from jax.sharding import PartitionSpec as P

DEGREE = 4

COEFFICIENTS = (
    -5369.0 / 1800.0,
    12.0 / 7.0,
    -15.0 / 56.0,
    10.0 / 189.0,
    -1.0 / 112.0,
    2.0 / 1925.0,
    -1.0 / 16632.0,
)
SPACING = 0.5
LOWER = 6.0
UPPER = 46.0
HALF = (UPPER - LOWER) / 2.0
CENTRE = (UPPER + LOWER) / 2.0
LANES = 128
SUBLANES = 8


def ring_weights(length):
    weights = [0.0] * length
    for offset in range(1, 7):
        weights[offset % length] += COEFFICIENTS[offset]
        weights[-offset % length] += COEFFICIENTS[offset]
    return weights


def pair_weights(length):
    weights = ring_weights(length)
    pairs = []
    for distance in range(1, length // 2 + 1):
        if weights[distance] != 0.0:
            pairs.append((sorted({distance, length - distance}), weights[distance]))
    return weights[0], pairs


def apply(field, diagonal, hop, before):
    ys = len(field)
    planes, xs = field[0].shape
    along_y, along_planes, along_x = [pair_weights(length)[1] for length in (ys, planes, xs)]
    results = []
    for y in range(ys):
        tile = field[y]
        total = diagonal[y] * tile
        if before is not None:
            total = total - before[y]
        for shifts, weight in along_y:
            total = total + (hop * weight) * functools.reduce(jnp.add, [field[(y - shift) % ys] for shift in shifts])
        for pairs, axis in ((along_planes, 0), (along_x, 1)):
            for shifts, weight in pairs:
                total = total + (hop * weight) * functools.reduce(
                    jnp.add, [pltpu.roll(tile, shift, axis) for shift in shifts]
                )
        results.append(total)
    return results


def filter_kernel(ng, copies, rows, used, run, width, cores, order, *refs):
    orb_ref, region_ref, table_ref, counts_ref, ritz_ref, out_ref, natural_ref = refs
    ys, planes, xs = orb_ref.shape
    columns, panel = ritz_ref.shape
    per_row = LANES // width
    for row in range(-(-columns // per_row)):
        line = jnp.zeros((1, LANES), jnp.float32)
        for slot in range(min(per_row, columns - row * per_row)):
            piece = jnp.concatenate(
                [ritz_ref[pl.ds(row * per_row + slot, 1), :], jnp.zeros((1, LANES - panel), jnp.float32)], axis=1
            )
            line = line + (pltpu.roll(piece, slot * width, 1) if slot else piece)
        natural_ref[pl.ds(run + row, ng, stride=rows), :] = jnp.broadcast_to(line, (ng, LANES))

    centre_weight = 3.0 * COEFFICIENTS[0] + sum(pair_weights(n)[0] for n in (planes, ys, xs))
    scale = 2.0 / HALF
    hop = -0.5 / (SPACING * SPACING) * scale
    regions = table_ref.shape[1]
    values = jnp.concatenate([table_ref[...], jnp.zeros((1, xs - regions), jnp.float32)], axis=1)
    values = jnp.broadcast_to(values, (planes, xs))
    diagonal = []
    for y in range(ys):
        potential = jnp.take_along_axis(values, region_ref[y], axis=1)
        diagonal.append(scale * potential + (hop * centre_weight - scale * CENTRE))
    band_pos = lax.axis_index("row") * cores + lax.axis_index("core")
    band = lax.broadcasted_iota(jnp.int32, counts_ref.shape, 1)
    count = jnp.sum(jnp.where(band == band_pos, counts_ref[...], 0), axis=1, keepdims=True)
    live = (lax.axis_index("grid") < count).astype(jnp.float32)
    previous = [orb_ref[y] for y in range(ys)]
    current = apply(previous, [0.5 * value for value in diagonal], 0.5 * hop, None)
    for _ in range(DEGREE - 1):
        previous, current = current, apply(current, diagonal, hop, previous)

    blocks = ys // run
    for y in range(ys):
        natural_ref[pl.ds((y // run) * rows + y % run, planes, stride=blocks * rows), :] = live * current[y]
    for copy in range(copies):
        for tile in range(ng):
            place = order.index(copy * ng + tile)
            out_ref[pl.ds(place * used, used), :] = natural_ref[pl.ds(tile * rows, used), :]


def partial_kernel(nrow, ng, used, run, width, columns, cores, order, distance, got_ref, out_ref, ritz_ref):
    for place, source in enumerate(order):
        ritz_ref[source] = got_ref[pl.ds(place * used + run, 1), :]
    wanted = out_ref.shape[0]
    holders = wanted // columns
    sublane = lax.broadcasted_iota(jnp.int32, (wanted, LANES), 0)
    block = lax.axis_index("row") * cores + lax.rem(lax.axis_index("core") + distance, cores)
    acc = [jnp.zeros((wanted, LANES), jnp.float32) for _ in range(run)]
    for row in range(nrow):
        lines = jnp.zeros((wanted, LANES), jnp.float32)
        for k in range(holders):
            line = ritz_ref[row * ng + block * holders + k]
            lines = jnp.where(sublane // columns == k, jnp.broadcast_to(line, (wanted, LANES)), lines)
        for r in range(ng):
            weight = jnp.take_along_axis(lines, sublane % columns * width + r, axis=1)
            for y in range(run):
                acc[y] = acc[y] + weight * got_ref[pl.ds(order.index(row * ng + r) * used + y, 1), :]
    for y in range(run):
        out_ref[:, pl.ds(y * LANES, LANES)] = acc[y]


def shards(nrow, cores, ng, orbitals, region, potential_table, counts, ritz):
    _, planes, ys, xs = orbitals.shape
    cells = planes * ys * xs
    panel, columns = ritz.shape
    run = cells // ng // xs
    width = 1
    while width < panel:
        width *= 2
    per_row = LANES // width
    ritz_rows = -(-columns // per_row)
    used = run + ritz_rows
    rows = -(-used // SUBLANES) * SUBLANES
    tiles = nrow * ng
    vmem = pl.BlockSpec(memory_space=pltpu.VMEM)
    inputs = [
        pltpu.with_memory_space_constraint(value, pltpu.HBM)
        for value in (
            jnp.transpose(orbitals[0], (1, 0, 2)), jnp.transpose(region, (1, 0, 2)), potential_table[None], counts[None], ritz.T
        )
    ]
    late = sorted(range(tiles), key=lambda place: (place % ng // (ng // 2), place // ng, place % ng), reverse=True)
    order = [place for pair in zip(late, late[::-1]) for place in pair][:tiles]
    packed_bytes = 4 * tiles * rows * LANES
    packed = pl.pallas_call(
        functools.partial(filter_kernel, ng, nrow, rows, used, run, width, cores, order),
        out_shape=jax.ShapeDtypeStruct((tiles * used, LANES), jnp.float32),
        in_specs=[vmem] * 5,
        out_specs=vmem,
        scratch_shapes=[
            pltpu.VMEM((ng * rows, LANES), jnp.float32),
        ],
        compiler_params=pltpu.CompilerParams(vmem_limit_bytes=2 * packed_bytes + 64 * cells + 2**20),
        name="chebyshev_filter",
    )(*inputs)
    got = lax.all_to_all(
        packed.reshape(tiles * used, 1, LANES), ("row", "grid"), split_axis=0, concat_axis=0, tiled=True,
        axis_index_groups=[order],
    ).reshape(tiles * used, LANES)
    sum_shape = jax.ShapeDtypeStruct((panel, run * LANES), jnp.float32)
    if columns * width <= LANES and tiles <= 64 and panel == ng and panel <= 16:
        def partial_sums(distance):
            return pl.pallas_call(
                functools.partial(partial_kernel, nrow, ng, used, run, width, columns, cores, order, distance),
                out_shape=sum_shape,
                in_specs=[vmem],
                out_specs=vmem,
                scratch_shapes=[pltpu.VMEM((tiles, 1, LANES), jnp.float32)],
                compiler_params=pltpu.CompilerParams(vmem_limit_bytes=packed_bytes + 2**20),
                name="ritz_partial_sums",
            )(got)

    else:
        holders = panel // columns
        by_source = got.reshape(tiles, used, LANES)[jnp.argsort(jnp.array(order))].reshape(nrow, ng, used, LANES)
        fields = by_source[:, :, :run].reshape(tiles, run * LANES)
        blocks = by_source[:, :, run : run + ritz_rows].reshape(nrow, ng, ritz_rows * per_row, width)

        def partial_sums(distance):
            block = lax.axis_index("row") * cores + lax.rem(lax.axis_index("core") + distance, cores)
            mine = lax.dynamic_slice_in_dim(blocks, block * holders, holders, axis=1)
            return lax.dot_general(
                jnp.transpose(mine[:, :, :columns, :panel], (0, 3, 1, 2)).reshape(tiles, panel),
                fields,
                (((0,), (0,)), ((), ())),
                precision=lax.Precision.HIGHEST,
                preferred_element_type=jnp.float32,
            )

    terms = []
    for distance in range(1, cores):
        pairs = [(core, (core + distance) % cores) for core in range(cores)]
        terms.append(lax.ppermute(partial_sums(distance), "core", pairs))
    terms.append(partial_sums(0))
    return functools.reduce(jnp.add, terms)


def solution(mesh):
    bands, ng = mesh.shape["band"], mesh.shape["grid"]
    cores = 2 if bands % 2 == 0 else 1
    nrow = bands // cores
    split = jax.sharding.Mesh(mesh.devices.reshape(nrow, cores, ng), ("row", "core", "grid"))
    return jax.shard_map(
        functools.partial(shards, nrow, cores, ng),
        mesh=split,
        in_specs=(P(("row", "core", "grid"), None, None, None), P(), P(), P(), P(("row", "core"), "grid")),
        out_specs=P(("row", "core"), "grid"),
        check_vma=False,
    )
```

```python
import functools

import jax
import jax.numpy as jnp
from jax import lax
from jax.experimental import pallas as pl
from jax.experimental.pallas import tpu as pltpu
from jax.sharding import PartitionSpec as P

DEGREE = 4

COEFFICIENTS = (
    -5369.0 / 1800.0,
    12.0 / 7.0,
    -15.0 / 56.0,
    10.0 / 189.0,
    -1.0 / 112.0,
    2.0 / 1925.0,
    -1.0 / 16632.0,
)
SPACING = 0.5
LOWER = 6.0
UPPER = 46.0
HALF = (UPPER - LOWER) / 2.0
CENTRE = (UPPER + LOWER) / 2.0
LANES = 128
SUBLANES = 8


def ring_weights(length):
    weights = [0.0] * length
    for offset in range(1, 7):
        weights[offset % length] += COEFFICIENTS[offset]
        weights[-offset % length] += COEFFICIENTS[offset]
    return weights


def pair_weights(length):
    weights = ring_weights(length)
    pairs = []
    for distance in range(1, length // 2 + 1):
        if weights[distance] != 0.0:
            pairs.append((sorted({distance, length - distance}), weights[distance]))
    return weights[0], pairs


def apply(field, diagonal, hop, before):
    ys = len(field)
    planes, xs = field[0].shape
    along_y, along_planes, along_x = [pair_weights(length)[1] for length in (ys, planes, xs)]
    results = []
    for y in range(ys):
        tile = field[y]
        total = diagonal[y] * tile
        if before is not None:
            total = total - before[y]
        for shifts, weight in along_y:
            total = total + (hop * weight) * functools.reduce(jnp.add, [field[(y - shift) % ys] for shift in shifts])
        for pairs, axis in ((along_planes, 0), (along_x, 1)):
            for shifts, weight in pairs:
                total = total + (hop * weight) * functools.reduce(
                    jnp.add, [pltpu.roll(tile, shift, axis) for shift in shifts]
                )
        results.append(total)
    return results


def filter_kernel(ng, copies, rows, used, run, width, cores, order, *refs):
    orb_ref, region_ref, table_ref, counts_ref, ritz_ref, out_ref, natural_ref = refs
    ys, planes, xs = orb_ref.shape
    columns, panel = ritz_ref.shape
    per_row = LANES // width
    for row in range(-(-columns // per_row)):
        line = jnp.zeros((1, LANES), jnp.float32)
        for slot in range(min(per_row, columns - row * per_row)):
            piece = jnp.concatenate(
                [ritz_ref[pl.ds(row * per_row + slot, 1), :], jnp.zeros((1, LANES - panel), jnp.float32)], axis=1
            )
            line = line + (pltpu.roll(piece, slot * width, 1) if slot else piece)
        natural_ref[pl.ds(run + row, ng, stride=rows), :] = jnp.broadcast_to(line, (ng, LANES))

    centre_weight = 3.0 * COEFFICIENTS[0] + sum(pair_weights(n)[0] for n in (planes, ys, xs))
    scale = 2.0 / HALF
    hop = -0.5 / (SPACING * SPACING) * scale
    diagonal = []
    for y in range(ys):
        region = region_ref[y]
        potential = jnp.zeros((planes, xs), jnp.float32)
        for index in range(table_ref.shape[0]):
            potential = jnp.where(region == index, table_ref[index], potential)
        diagonal.append(scale * potential + (hop * centre_weight - scale * CENTRE))
    band_pos = lax.axis_index("row") * cores + lax.axis_index("core")
    live = (lax.axis_index("grid") < counts_ref[band_pos]).astype(jnp.float32)
    previous = [live * orb_ref[y] for y in range(ys)]
    current = apply(previous, [0.5 * value for value in diagonal], 0.5 * hop, None)
    for _ in range(DEGREE - 1):
        previous, current = current, apply(current, diagonal, hop, previous)

    blocks = ys // run
    for y in range(ys):
        natural_ref[pl.ds((y // run) * rows + y % run, planes, stride=blocks * rows), :] = current[y]
    for copy in range(copies):
        for tile in range(ng):
            place = order.index(copy * ng + tile)
            out_ref[pl.ds(place * used, used), :] = natural_ref[pl.ds(tile * rows, used), :]


def partial_kernel(nrow, ng, used, run, width, columns, cores, order, distance, got_ref, out_ref):
    wanted = out_ref.shape[0]
    holders = wanted // columns
    sublane = lax.broadcasted_iota(jnp.int32, (wanted, LANES), 0)
    block = lax.axis_index("row") * cores + lax.rem(lax.axis_index("core") + distance, cores)
    acc = [jnp.zeros((wanted, LANES), jnp.float32) for _ in range(run)]
    for row in range(nrow):
        lines = jnp.zeros((wanted, LANES), jnp.float32)
        for k in range(holders):
            place = order.index(row * ng) - block * holders - k
            line = got_ref[pl.ds(place * used + run, 1), :]
            lines = jnp.where(sublane // columns == k, jnp.broadcast_to(line, (wanted, LANES)), lines)
        for r in range(ng):
            weight = jnp.take_along_axis(lines, sublane % columns * width + r, axis=1)
            for y in range(run):
                acc[y] = acc[y] + weight * got_ref[pl.ds(order.index(row * ng + r) * used + y, 1), :]
    for y in range(run):
        out_ref[:, pl.ds(y * LANES, LANES)] = acc[y]


def shards(nrow, cores, ng, orbitals, region, potential_table, counts, ritz):
    _, planes, ys, xs = orbitals.shape
    cells = planes * ys * xs
    panel, columns = ritz.shape
    run = cells // ng // xs
    width = 1
    while width < panel:
        width *= 2
    per_row = LANES // width
    ritz_rows = -(-columns // per_row)
    used = run + ritz_rows
    rows = -(-used // SUBLANES) * SUBLANES
    tiles = nrow * ng
    vmem = pl.BlockSpec(memory_space=pltpu.VMEM)
    smem = pl.BlockSpec(memory_space=pltpu.SMEM)
    inputs = [
        pltpu.with_memory_space_constraint(value, pltpu.HBM)
        for value in (
            jnp.transpose(orbitals[0], (1, 0, 2)), jnp.transpose(region, (1, 0, 2)), potential_table, counts, ritz.T
        )
    ]
    order = list(range(tiles))[::-1]
    packed_bytes = 4 * tiles * rows * LANES
    packed = pl.pallas_call(
        functools.partial(filter_kernel, ng, nrow, rows, used, run, width, cores, order),
        out_shape=jax.ShapeDtypeStruct((tiles * used, LANES), jnp.float32),
        in_specs=[vmem, vmem, smem, smem, vmem],
        out_specs=vmem,
        scratch_shapes=[
            pltpu.VMEM((ng * rows, LANES), jnp.float32),
        ],
        compiler_params=pltpu.CompilerParams(vmem_limit_bytes=2 * packed_bytes + 64 * cells + 2**20),
        name="chebyshev_filter",
    )(*inputs)
    got = lax.all_to_all(
        packed.reshape(tiles * used, 1, LANES), ("row", "grid"), split_axis=0, concat_axis=0, tiled=True,
        axis_index_groups=[order],
    ).reshape(tiles * used, LANES)
    sum_shape = jax.ShapeDtypeStruct((panel, run * LANES), jnp.float32)
    if columns * width <= LANES and tiles <= 64 and panel == ng and panel <= 16:
        def partial_sums(distance):
            return pl.pallas_call(
                functools.partial(partial_kernel, nrow, ng, used, run, width, columns, cores, order, distance),
                out_shape=sum_shape,
                in_specs=[vmem],
                out_specs=vmem,
                compiler_params=pltpu.CompilerParams(vmem_limit_bytes=packed_bytes + 2**20),
                name="ritz_partial_sums",
            )(got)

    else:
        holders = panel // columns
        by_source = got.reshape(tiles, used, LANES)[jnp.argsort(jnp.array(order))].reshape(nrow, ng, used, LANES)
        fields = by_source[:, :, :run].reshape(tiles, run * LANES)
        blocks = by_source[:, :, run : run + ritz_rows].reshape(nrow, ng, ritz_rows * per_row, width)

        def partial_sums(distance):
            block = lax.axis_index("row") * cores + lax.rem(lax.axis_index("core") + distance, cores)
            mine = lax.dynamic_slice_in_dim(blocks, block * holders, holders, axis=1)
            return lax.dot_general(
                jnp.transpose(mine[:, :, :columns, :panel], (0, 3, 1, 2)).reshape(tiles, panel),
                fields,
                (((0,), (0,)), ((), ())),
                precision=lax.Precision.HIGHEST,
                preferred_element_type=jnp.float32,
            )

    terms = []
    for distance in range(1, cores):
        pairs = [(core, (core + distance) % cores) for core in range(cores)]
        terms.append(lax.ppermute(partial_sums(distance), "core", pairs))
    terms.append(partial_sums(0))
    return functools.reduce(jnp.add, terms)


def solution(mesh):
    bands, ng = mesh.shape["band"], mesh.shape["grid"]
    cores = 2 if bands % 2 == 0 else 1
    nrow = bands // cores
    split = jax.sharding.Mesh(mesh.devices.reshape(nrow, cores, ng), ("row", "core", "grid"))
    return jax.shard_map(
        functools.partial(shards, nrow, cores, ng),
        mesh=split,
        in_specs=(P(("row", "core", "grid"), None, None, None), P(), P(), P(), P(("row", "core"), "grid")),
        out_specs=P(("row", "core"), "grid"),
        check_vma=False,
    )
```

```python
import functools

import jax
import jax.numpy as jnp
from jax import lax
from jax.experimental import pallas as pl
from jax.experimental.pallas import tpu as pltpu
from jax.sharding import PartitionSpec as P

DEGREE = 4

COEFFICIENTS = (
    -5369.0 / 1800.0,
    12.0 / 7.0,
    -15.0 / 56.0,
    10.0 / 189.0,
    -1.0 / 112.0,
    2.0 / 1925.0,
    -1.0 / 16632.0,
)
SPACING = 0.5
LOWER = 6.0
UPPER = 46.0
HALF = (UPPER - LOWER) / 2.0
CENTRE = (UPPER + LOWER) / 2.0
LANES = 128
SUBLANES = 8


def ring_weights(length):
    weights = [0.0] * length
    for offset in range(1, 7):
        weights[offset % length] += COEFFICIENTS[offset]
        weights[-offset % length] += COEFFICIENTS[offset]
    return weights


def pair_weights(length):
    weights = ring_weights(length)
    pairs = []
    for distance in range(1, length // 2 + 1):
        if weights[distance] != 0.0:
            pairs.append((sorted({distance, length - distance}), weights[distance]))
    return weights[0], pairs


def apply(field, diagonal, hop, before):
    ys = len(field)
    planes, xs = field[0].shape
    along_y, along_planes, along_x = [pair_weights(length)[1] for length in (ys, planes, xs)]
    results = []
    for y in range(ys):
        tile = field[y]
        total = diagonal[y] * tile
        if before is not None:
            total = total - before[y]
        for shifts, weight in along_y:
            total = total + (hop * weight) * functools.reduce(jnp.add, [field[(y - shift) % ys] for shift in shifts])
        for pairs, axis in ((along_planes, 0), (along_x, 1)):
            for shifts, weight in pairs:
                total = total + (hop * weight) * functools.reduce(
                    jnp.add, [pltpu.roll(tile, shift, axis) for shift in shifts]
                )
        results.append(total)
    return results


def filter_kernel(ng, copies, used, run, width, cores, *refs):
    orb_ref, region_ref, table_ref, counts_ref, ritz_ref, out_ref = refs
    ys, planes, xs = orb_ref.shape
    columns, panel = ritz_ref.shape
    per_row = LANES // width
    for row in range(-(-columns // per_row)):
        line = jnp.zeros((1, LANES), jnp.float32)
        for slot in range(min(per_row, columns - row * per_row)):
            piece = jnp.concatenate(
                [ritz_ref[pl.ds(row * per_row + slot, 1), :], jnp.zeros((1, LANES - panel), jnp.float32)], axis=1
            )
            line = line + (pltpu.roll(piece, slot * width, 1) if slot else piece)
        out_ref[pl.ds(run + row, copies * ng, stride=used), :] = jnp.broadcast_to(line, (copies * ng, LANES))

    centre_weight = 3.0 * COEFFICIENTS[0] + sum(pair_weights(n)[0] for n in (planes, ys, xs))
    scale = 2.0 / HALF
    hop = -0.5 / (SPACING * SPACING) * scale
    regions = table_ref.shape[1]
    values = jnp.concatenate([table_ref[...], jnp.zeros((1, xs - regions), jnp.float32)], axis=1)
    values = jnp.broadcast_to(values, (planes, xs))
    diagonal = []
    for y in range(ys):
        potential = jnp.take_along_axis(values, region_ref[y], axis=1)
        diagonal.append(scale * potential + (hop * centre_weight - scale * CENTRE))
    band_pos = lax.axis_index("row") * cores + lax.axis_index("core")
    band = lax.broadcasted_iota(jnp.int32, counts_ref.shape, 1)
    count = jnp.sum(jnp.where(band == band_pos, counts_ref[...], 0), axis=1, keepdims=True)
    live = (lax.axis_index("grid") < count).astype(jnp.float32)
    previous = [orb_ref[y] for y in range(ys)]
    current = apply(previous, [0.5 * value for value in diagonal], 0.5 * hop, None)
    for _ in range(DEGREE - 1):
        previous, current = current, apply(current, diagonal, hop, previous)

    blocks = ys // run
    for y in range(ys):
        masked = live * current[y]
        for copy in range(copies):
            first = (copy * ng + y // run + 1) * used + y % run
            count = planes if copy < copies - 1 or y // run < blocks - 1 else planes - 1
            out_ref[pl.ds(first, count, stride=blocks * used), :] = masked[:count]
            if count < planes:
                out_ref[pl.ds(y % run, 1), :] = masked[count:]


def partial_kernel(nrow, ng, used, run, width, columns, cores, order, distance, got_ref, out_ref, ritz_ref):
    for place, source in enumerate(order):
        ritz_ref[source] = got_ref[pl.ds(place * used + run, 1), :]
    wanted = out_ref.shape[0]
    holders = wanted // columns
    sublane = lax.broadcasted_iota(jnp.int32, (wanted, LANES), 0)
    block = lax.axis_index("row") * cores + lax.rem(lax.axis_index("core") + distance, cores)
    acc = [jnp.zeros((wanted, LANES), jnp.float32) for _ in range(run)]
    for row in range(nrow):
        lines = jnp.zeros((wanted, LANES), jnp.float32)
        for k in range(holders):
            line = ritz_ref[row * ng + block * holders + k]
            lines = jnp.where(sublane // columns == k, jnp.broadcast_to(line, (wanted, LANES)), lines)
        for r in range(ng):
            weight = jnp.take_along_axis(lines, sublane % columns * width + r, axis=1)
            for y in range(run):
                acc[y] = acc[y] + weight * got_ref[pl.ds(order.index(row * ng + r) * used + y, 1), :]
    for y in range(run):
        out_ref[:, pl.ds(y * LANES, LANES)] = acc[y]


def shards(nrow, cores, ng, orbitals, region, potential_table, counts, ritz):
    _, planes, ys, xs = orbitals.shape
    cells = planes * ys * xs
    panel, columns = ritz.shape
    run = cells // ng // xs
    width = 1
    while width < panel:
        width *= 2
    per_row = LANES // width
    ritz_rows = -(-columns // per_row)
    used = run + ritz_rows
    tiles = nrow * ng
    vmem = pl.BlockSpec(memory_space=pltpu.VMEM)
    inputs = [
        pltpu.with_memory_space_constraint(value, pltpu.HBM)
        for value in (
            jnp.transpose(orbitals[0], (1, 0, 2)), jnp.transpose(region, (1, 0, 2)), potential_table[None], counts[None], ritz.T
        )
    ]
    order = [tiles - 1] + list(range(tiles - 1))
    packed_bytes = 4 * tiles * used * LANES
    packed = pl.pallas_call(
        functools.partial(filter_kernel, ng, nrow, used, run, width, cores),
        out_shape=jax.ShapeDtypeStruct((tiles * used, LANES), jnp.float32),
        in_specs=[vmem] * 5,
        out_specs=vmem,
        compiler_params=pltpu.CompilerParams(vmem_limit_bytes=2 * packed_bytes + 64 * cells + 2**20),
        name="chebyshev_filter",
    )(*inputs)
    got = lax.all_to_all(
        packed.reshape(tiles * used, 1, LANES), ("row", "grid"), split_axis=0, concat_axis=0, tiled=True,
        axis_index_groups=[order],
    ).reshape(tiles * used, LANES)
    sum_shape = jax.ShapeDtypeStruct((panel, run * LANES), jnp.float32)
    if columns * width <= LANES and tiles <= 64 and panel == ng and panel <= 16:
        def partial_sums(distance):
            return pl.pallas_call(
                functools.partial(partial_kernel, nrow, ng, used, run, width, columns, cores, order, distance),
                out_shape=sum_shape,
                in_specs=[vmem],
                out_specs=vmem,
                scratch_shapes=[pltpu.VMEM((tiles, 1, LANES), jnp.float32)],
                compiler_params=pltpu.CompilerParams(vmem_limit_bytes=packed_bytes + 2**20),
                name="ritz_partial_sums",
            )(got)

    else:
        holders = panel // columns
        by_source = got.reshape(tiles, used, LANES)[jnp.argsort(jnp.array(order))].reshape(nrow, ng, used, LANES)
        fields = by_source[:, :, :run].reshape(tiles, run * LANES)
        blocks = by_source[:, :, run : run + ritz_rows].reshape(nrow, ng, ritz_rows * per_row, width)

        def partial_sums(distance):
            block = lax.axis_index("row") * cores + lax.rem(lax.axis_index("core") + distance, cores)
            mine = lax.dynamic_slice_in_dim(blocks, block * holders, holders, axis=1)
            return lax.dot_general(
                jnp.transpose(mine[:, :, :columns, :panel], (0, 3, 1, 2)).reshape(tiles, panel),
                fields,
                (((0,), (0,)), ((), ())),
                precision=lax.Precision.HIGHEST,
                preferred_element_type=jnp.float32,
            )

    terms = []
    for distance in range(1, cores):
        pairs = [(core, (core + distance) % cores) for core in range(cores)]
        terms.append(lax.ppermute(partial_sums(distance), "core", pairs))
    terms.append(partial_sums(0))
    return functools.reduce(jnp.add, terms)


def solution(mesh):
    bands, ng = mesh.shape["band"], mesh.shape["grid"]
    cores = 2 if bands % 2 == 0 else 1
    nrow = bands // cores
    split = jax.sharding.Mesh(mesh.devices.reshape(nrow, cores, ng), ("row", "core", "grid"))
    return jax.shard_map(
        functools.partial(shards, nrow, cores, ng),
        mesh=split,
        in_specs=(P(("row", "core", "grid"), None, None, None), P(), P(), P(), P(("row", "core"), "grid")),
        out_specs=P(("row", "core"), "grid"),
        check_vma=False,
    )
```

```python
import functools

import jax
import jax.numpy as jnp
from jax import lax
from jax.experimental import pallas as pl
from jax.experimental.pallas import tpu as pltpu
from jax.sharding import PartitionSpec as P

DEGREE = 4

COEFFICIENTS = (
    -5369.0 / 1800.0,
    12.0 / 7.0,
    -15.0 / 56.0,
    10.0 / 189.0,
    -1.0 / 112.0,
    2.0 / 1925.0,
    -1.0 / 16632.0,
)
SPACING = 0.5
LOWER = 6.0
UPPER = 46.0
HALF = (UPPER - LOWER) / 2.0
CENTRE = (UPPER + LOWER) / 2.0
LANES = 128
SUBLANES = 8


def ring_weights(length):
    weights = [0.0] * length
    for offset in range(1, 7):
        weights[offset % length] += COEFFICIENTS[offset]
        weights[-offset % length] += COEFFICIENTS[offset]
    return weights


def pair_weights(length):
    weights = ring_weights(length)
    pairs = []
    for distance in range(1, length // 2 + 1):
        if weights[distance] != 0.0:
            pairs.append((sorted({distance, length - distance}), weights[distance]))
    return weights[0], pairs


def apply(field, diagonal, hop, before):
    ys = len(field)
    planes, xs = field[0].shape
    along_y, along_planes, along_x = [pair_weights(length)[1] for length in (ys, planes, xs)]
    results = []
    for y in range(ys):
        tile = field[y]
        total = diagonal[y] * tile
        if before is not None:
            total = total - before[y]
        for shifts, weight in along_y:
            total = total + (hop * weight) * functools.reduce(jnp.add, [field[(y - shift) % ys] for shift in shifts])
        for pairs, axis in ((along_planes, 0), (along_x, 1)):
            for shifts, weight in pairs:
                total = total + (hop * weight) * functools.reduce(
                    jnp.add, [pltpu.roll(tile, shift, axis) for shift in shifts]
                )
        results.append(total)
    return results


def filter_kernel(ng, copies, rows, used, run, width, cores, order, *refs):
    orb_ref, region_ref, table_ref, counts_ref, ritz_ref, out_ref, natural_ref = refs
    ys, planes, xs = orb_ref.shape
    columns, panel = ritz_ref.shape
    per_row = LANES // width
    for row in range(-(-columns // per_row)):
        line = jnp.zeros((1, LANES), jnp.float32)
        for slot in range(min(per_row, columns - row * per_row)):
            piece = jnp.concatenate(
                [ritz_ref[pl.ds(row * per_row + slot, 1), :], jnp.zeros((1, LANES - panel), jnp.float32)], axis=1
            )
            line = line + (pltpu.roll(piece, slot * width, 1) if slot else piece)
        natural_ref[pl.ds(run + row, ng, stride=rows), :] = jnp.broadcast_to(line, (ng, LANES))

    centre_weight = 3.0 * COEFFICIENTS[0] + sum(pair_weights(n)[0] for n in (planes, ys, xs))
    scale = 2.0 / HALF
    hop = -0.5 / (SPACING * SPACING) * scale
    regions = table_ref.shape[1]
    values = jnp.concatenate([table_ref[...], jnp.zeros((1, xs - regions), jnp.float32)], axis=1)
    values = jnp.broadcast_to(values, (planes, xs))
    diagonal = []
    for y in range(ys):
        potential = jnp.take_along_axis(values, region_ref[y], axis=1)
        diagonal.append(scale * potential + (hop * centre_weight - scale * CENTRE))
    band_pos = lax.axis_index("row") * cores + lax.axis_index("core")
    band = lax.broadcasted_iota(jnp.int32, counts_ref.shape, 1)
    count = jnp.sum(jnp.where(band == band_pos, counts_ref[...], 0), axis=1, keepdims=True)
    live = (lax.axis_index("grid") < count).astype(jnp.float32)
    previous = [orb_ref[y] for y in range(ys)]
    current = apply(previous, [0.5 * value for value in diagonal], 0.5 * hop, None)
    for _ in range(DEGREE - 1):
        previous, current = current, apply(current, diagonal, hop, previous)

    blocks = ys // run
    for y in range(ys):
        natural_ref[pl.ds((y // run) * rows + y % run, planes, stride=blocks * rows), :] = live * current[y]
    for tile in range(ng):
        value = natural_ref[pl.ds(tile * rows, used), :]
        for copy in range(copies):
            out_ref[pl.ds(order.index(copy * ng + tile) * used, used), :] = value


def partial_kernel(nrow, ng, used, run, width, columns, cores, order, distance, got_ref, out_ref, ritz_ref):
    for place, source in enumerate(order):
        ritz_ref[source] = got_ref[pl.ds(place * used + run, 1), :]
    wanted = out_ref.shape[0]
    holders = wanted // columns
    sublane = lax.broadcasted_iota(jnp.int32, (wanted, LANES), 0)
    block = lax.axis_index("row") * cores + lax.rem(lax.axis_index("core") + distance, cores)
    acc = [jnp.zeros((wanted, LANES), jnp.float32) for _ in range(run)]
    for row in range(nrow):
        lines = jnp.zeros((wanted, LANES), jnp.float32)
        for k in range(holders):
            line = ritz_ref[row * ng + block * holders + k]
            lines = jnp.where(sublane // columns == k, jnp.broadcast_to(line, (wanted, LANES)), lines)
        for r in range(ng):
            weight = jnp.take_along_axis(lines, sublane % columns * width + r, axis=1)
            for y in range(run):
                acc[y] = acc[y] + weight * got_ref[pl.ds(order.index(row * ng + r) * used + y, 1), :]
    for y in range(run):
        out_ref[:, pl.ds(y * LANES, LANES)] = acc[y]


def shards(nrow, cores, ng, orbitals, region, potential_table, counts, ritz):
    _, planes, ys, xs = orbitals.shape
    cells = planes * ys * xs
    panel, columns = ritz.shape
    run = cells // ng // xs
    width = 1
    while width < panel:
        width *= 2
    per_row = LANES // width
    ritz_rows = -(-columns // per_row)
    used = run + ritz_rows
    rows = -(-used // SUBLANES) * SUBLANES
    tiles = nrow * ng
    vmem = pl.BlockSpec(memory_space=pltpu.VMEM)
    inputs = [
        pltpu.with_memory_space_constraint(value, pltpu.HBM)
        for value in (
            jnp.transpose(orbitals[0], (1, 0, 2)), jnp.transpose(region, (1, 0, 2)), potential_table[None], counts[None], ritz.T
        )
    ]
    late = sorted(range(tiles), key=lambda place: (place % ng // (ng // 2), place // ng, place % ng), reverse=True)
    order = [place for pair in zip(late, late[::-1]) for place in pair][:tiles]
    packed_bytes = 4 * tiles * rows * LANES
    packed = pl.pallas_call(
        functools.partial(filter_kernel, ng, nrow, rows, used, run, width, cores, order),
        out_shape=jax.ShapeDtypeStruct((tiles * used, LANES), jnp.float32),
        in_specs=[vmem] * 5,
        out_specs=vmem,
        scratch_shapes=[
            pltpu.VMEM((ng * rows, LANES), jnp.float32),
        ],
        compiler_params=pltpu.CompilerParams(vmem_limit_bytes=2 * packed_bytes + 64 * cells + 2**20),
        name="chebyshev_filter",
    )(*inputs)
    got = lax.all_to_all(
        packed.reshape(tiles * used, 1, LANES), ("row", "grid"), split_axis=0, concat_axis=0, tiled=True,
        axis_index_groups=[order],
    ).reshape(tiles * used, LANES)
    sum_shape = jax.ShapeDtypeStruct((panel, run * LANES), jnp.float32)
    if columns * width <= LANES and tiles <= 64 and panel == ng and panel <= 16:
        def partial_sums(distance):
            return pl.pallas_call(
                functools.partial(partial_kernel, nrow, ng, used, run, width, columns, cores, order, distance),
                out_shape=sum_shape,
                in_specs=[vmem],
                out_specs=vmem,
                scratch_shapes=[pltpu.VMEM((tiles, 1, LANES), jnp.float32)],
                compiler_params=pltpu.CompilerParams(vmem_limit_bytes=packed_bytes + 2**20),
                name="ritz_partial_sums",
            )(got)

    else:
        holders = panel // columns
        by_source = got.reshape(tiles, used, LANES)[jnp.argsort(jnp.array(order))].reshape(nrow, ng, used, LANES)
        fields = by_source[:, :, :run].reshape(tiles, run * LANES)
        blocks = by_source[:, :, run : run + ritz_rows].reshape(nrow, ng, ritz_rows * per_row, width)

        def partial_sums(distance):
            block = lax.axis_index("row") * cores + lax.rem(lax.axis_index("core") + distance, cores)
            mine = lax.dynamic_slice_in_dim(blocks, block * holders, holders, axis=1)
            return lax.dot_general(
                jnp.transpose(mine[:, :, :columns, :panel], (0, 3, 1, 2)).reshape(tiles, panel),
                fields,
                (((0,), (0,)), ((), ())),
                precision=lax.Precision.HIGHEST,
                preferred_element_type=jnp.float32,
            )

    terms = []
    for distance in range(1, cores):
        pairs = [(core, (core + distance) % cores) for core in range(cores)]
        terms.append(lax.ppermute(partial_sums(distance), "core", pairs))
    terms.append(partial_sums(0))
    return functools.reduce(jnp.add, terms)


def solution(mesh):
    bands, ng = mesh.shape["band"], mesh.shape["grid"]
    cores = 2 if bands % 2 == 0 else 1
    nrow = bands // cores
    split = jax.sharding.Mesh(mesh.devices.reshape(nrow, cores, ng), ("row", "core", "grid"))
    return jax.shard_map(
        functools.partial(shards, nrow, cores, ng),
        mesh=split,
        in_specs=(P(("row", "core", "grid"), None, None, None), P(), P(), P(), P(("row", "core"), "grid")),
        out_specs=P(("row", "core"), "grid"),
        check_vma=False,
    )
```

```python
import functools

import jax
import jax.numpy as jnp
from jax import lax
from jax.experimental import pallas as pl
from jax.experimental.pallas import tpu as pltpu
from jax.sharding import PartitionSpec as P

DEGREE = 4

COEFFICIENTS = (
    -5369.0 / 1800.0,
    12.0 / 7.0,
    -15.0 / 56.0,
    10.0 / 189.0,
    -1.0 / 112.0,
    2.0 / 1925.0,
    -1.0 / 16632.0,
)
SPACING = 0.5
LOWER = 6.0
UPPER = 46.0
HALF = (UPPER - LOWER) / 2.0
CENTRE = (UPPER + LOWER) / 2.0
LANES = 128
SUBLANES = 8


def ring_weights(length):
    weights = [0.0] * length
    for offset in range(1, 7):
        weights[offset % length] += COEFFICIENTS[offset]
        weights[-offset % length] += COEFFICIENTS[offset]
    return weights


def pair_weights(length):
    weights = ring_weights(length)
    pairs = []
    for distance in range(1, length // 2 + 1):
        if weights[distance] != 0.0:
            pairs.append((sorted({distance, length - distance}), weights[distance]))
    return weights[0], pairs


def apply(field, diagonal, hop, before, twice_ref):
    ys = len(field)
    planes, xs = field[0].shape
    along_y, along_planes, along_x = [pair_weights(length)[1] for length in (ys, planes, xs)]
    for y in range(ys):
        twice_ref[y, pl.ds(0, planes), :] = field[y]
        twice_ref[y, pl.ds(planes, planes), :] = field[y]
    results = []
    for y in range(ys):
        tile = field[y]
        total = diagonal[y] * tile
        if before is not None:
            total = total - before[y]
        for shifts, weight in along_y:
            total = total + (hop * weight) * functools.reduce(jnp.add, [field[(y - shift) % ys] for shift in shifts])
        for shifts, weight in along_planes:
            total = total + (hop * weight) * functools.reduce(
                jnp.add, [twice_ref[y, pl.ds(planes - shift, planes), :] for shift in shifts]
            )
        for shifts, weight in along_x:
            total = total + (hop * weight) * functools.reduce(jnp.add, [pltpu.roll(tile, shift, 1) for shift in shifts])
        results.append(total)
    return results


def filter_kernel(ng, copies, rows, used, run, width, cores, order, *refs):
    orb_ref, region_ref, table_ref, counts_ref, ritz_ref, out_ref, natural_ref, twice_ref = refs
    ys, planes, xs = orb_ref.shape
    columns, panel = ritz_ref.shape
    per_row = LANES // width
    for row in range(-(-columns // per_row)):
        line = jnp.zeros((1, LANES), jnp.float32)
        for slot in range(min(per_row, columns - row * per_row)):
            piece = jnp.concatenate(
                [ritz_ref[pl.ds(row * per_row + slot, 1), :], jnp.zeros((1, LANES - panel), jnp.float32)], axis=1
            )
            line = line + (pltpu.roll(piece, slot * width, 1) if slot else piece)
        natural_ref[pl.ds(run + row, ng, stride=rows), :] = jnp.broadcast_to(line, (ng, LANES))

    centre_weight = 3.0 * COEFFICIENTS[0] + sum(pair_weights(n)[0] for n in (planes, ys, xs))
    scale = 2.0 / HALF
    hop = -0.5 / (SPACING * SPACING) * scale
    regions = table_ref.shape[1]
    values = jnp.concatenate([table_ref[...], jnp.zeros((1, xs - regions), jnp.float32)], axis=1)
    values = jnp.broadcast_to(values, (planes, xs))
    diagonal = []
    for y in range(ys):
        potential = jnp.take_along_axis(values, region_ref[y], axis=1)
        diagonal.append(scale * potential + (hop * centre_weight - scale * CENTRE))
    band_pos = lax.axis_index("row") * cores + lax.axis_index("core")
    band = lax.broadcasted_iota(jnp.int32, counts_ref.shape, 1)
    count = jnp.sum(jnp.where(band == band_pos, counts_ref[...], 0), axis=1, keepdims=True)
    live = (lax.axis_index("grid") < count).astype(jnp.float32)
    previous = [orb_ref[y] for y in range(ys)]
    current = apply(previous, [0.5 * value for value in diagonal], 0.5 * hop, None, twice_ref)
    for _ in range(DEGREE - 1):
        previous, current = current, apply(current, diagonal, hop, previous, twice_ref)

    blocks = ys // run
    for y in range(ys):
        natural_ref[pl.ds((y // run) * rows + y % run, planes, stride=blocks * rows), :] = live * current[y]
    for tile in range(ng):
        value = natural_ref[pl.ds(tile * rows, used), :]
        for copy in range(copies):
            out_ref[pl.ds(order.index(copy * ng + tile) * used, used), :] = value


def partial_kernel(nrow, ng, used, run, width, columns, cores, order, distance, got_ref, out_ref, ritz_ref):
    for place, source in enumerate(order):
        ritz_ref[source] = got_ref[pl.ds(place * used + run, 1), :]
    wanted = out_ref.shape[0]
    holders = wanted // columns
    sublane = lax.broadcasted_iota(jnp.int32, (wanted, LANES), 0)
    block = lax.axis_index("row") * cores + lax.rem(lax.axis_index("core") + distance, cores)
    acc = [jnp.zeros((wanted, LANES), jnp.float32) for _ in range(run)]
    for row in range(nrow):
        lines = jnp.zeros((wanted, LANES), jnp.float32)
        for k in range(holders):
            line = ritz_ref[row * ng + block * holders + k]
            lines = jnp.where(sublane // columns == k, jnp.broadcast_to(line, (wanted, LANES)), lines)
        for r in range(ng):
            weight = jnp.take_along_axis(lines, sublane % columns * width + r, axis=1)
            for y in range(run):
                acc[y] = acc[y] + weight * got_ref[pl.ds(order.index(row * ng + r) * used + y, 1), :]
    for y in range(run):
        out_ref[:, pl.ds(y * LANES, LANES)] = acc[y]


def shards(nrow, cores, ng, orbitals, region, potential_table, counts, ritz):
    _, planes, ys, xs = orbitals.shape
    cells = planes * ys * xs
    panel, columns = ritz.shape
    run = cells // ng // xs
    width = 1
    while width < panel:
        width *= 2
    per_row = LANES // width
    ritz_rows = -(-columns // per_row)
    used = run + ritz_rows
    rows = -(-used // SUBLANES) * SUBLANES
    tiles = nrow * ng
    vmem = pl.BlockSpec(memory_space=pltpu.VMEM)
    inputs = [
        pltpu.with_memory_space_constraint(value, pltpu.HBM)
        for value in (
            jnp.transpose(orbitals[0], (1, 0, 2)), jnp.transpose(region, (1, 0, 2)), potential_table[None], counts[None], ritz.T
        )
    ]
    late = sorted(range(tiles), key=lambda place: (place % ng // (ng // 2), place // ng, place % ng), reverse=True)
    order = [place for pair in zip(late, late[::-1]) for place in pair][:tiles]
    packed_bytes = 4 * tiles * rows * LANES
    packed = pl.pallas_call(
        functools.partial(filter_kernel, ng, nrow, rows, used, run, width, cores, order),
        out_shape=jax.ShapeDtypeStruct((tiles * used, LANES), jnp.float32),
        in_specs=[vmem] * 5,
        out_specs=vmem,
        scratch_shapes=[
            pltpu.VMEM((ng * rows, LANES), jnp.float32),
            pltpu.VMEM((ys, 2 * planes, xs), jnp.float32),
        ],
        compiler_params=pltpu.CompilerParams(vmem_limit_bytes=2 * packed_bytes + 64 * cells + 2**20),
        name="chebyshev_filter",
    )(*inputs)
    got = lax.all_to_all(
        packed.reshape(tiles * used, 1, LANES), ("row", "grid"), split_axis=0, concat_axis=0, tiled=True,
        axis_index_groups=[order],
    ).reshape(tiles * used, LANES)
    sum_shape = jax.ShapeDtypeStruct((panel, run * LANES), jnp.float32)
    if columns * width <= LANES and tiles <= 64 and panel == ng and panel <= 16:
        def partial_sums(distance):
            return pl.pallas_call(
                functools.partial(partial_kernel, nrow, ng, used, run, width, columns, cores, order, distance),
                out_shape=sum_shape,
                in_specs=[vmem],
                out_specs=vmem,
                scratch_shapes=[pltpu.VMEM((tiles, 1, LANES), jnp.float32)],
                compiler_params=pltpu.CompilerParams(vmem_limit_bytes=packed_bytes + 2**20),
                name="ritz_partial_sums",
            )(got)

    else:
        holders = panel // columns
        by_source = got.reshape(tiles, used, LANES)[jnp.argsort(jnp.array(order))].reshape(nrow, ng, used, LANES)
        fields = by_source[:, :, :run].reshape(tiles, run * LANES)
        blocks = by_source[:, :, run : run + ritz_rows].reshape(nrow, ng, ritz_rows * per_row, width)

        def partial_sums(distance):
            block = lax.axis_index("row") * cores + lax.rem(lax.axis_index("core") + distance, cores)
            mine = lax.dynamic_slice_in_dim(blocks, block * holders, holders, axis=1)
            return lax.dot_general(
                jnp.transpose(mine[:, :, :columns, :panel], (0, 3, 1, 2)).reshape(tiles, panel),
                fields,
                (((0,), (0,)), ((), ())),
                precision=lax.Precision.HIGHEST,
                preferred_element_type=jnp.float32,
            )

    terms = []
    for distance in range(1, cores):
        pairs = [(core, (core + distance) % cores) for core in range(cores)]
        terms.append(lax.ppermute(partial_sums(distance), "core", pairs))
    terms.append(partial_sums(0))
    return functools.reduce(jnp.add, terms)


def solution(mesh):
    bands, ng = mesh.shape["band"], mesh.shape["grid"]
    cores = 2 if bands % 2 == 0 else 1
    nrow = bands // cores
    split = jax.sharding.Mesh(mesh.devices.reshape(nrow, cores, ng), ("row", "core", "grid"))
    return jax.shard_map(
        functools.partial(shards, nrow, cores, ng),
        mesh=split,
        in_specs=(P(("row", "core", "grid"), None, None, None), P(), P(), P(), P(("row", "core"), "grid")),
        out_specs=P(("row", "core"), "grid"),
        check_vma=False,
    )
```

```python
import functools

import jax
import jax.numpy as jnp
from jax import lax
from jax.experimental import pallas as pl
from jax.experimental.pallas import tpu as pltpu
from jax.sharding import PartitionSpec as P

DEGREE = 4

COEFFICIENTS = (
    -5369.0 / 1800.0,
    12.0 / 7.0,
    -15.0 / 56.0,
    10.0 / 189.0,
    -1.0 / 112.0,
    2.0 / 1925.0,
    -1.0 / 16632.0,
)
SPACING = 0.5
LOWER = 6.0
UPPER = 46.0
HALF = (UPPER - LOWER) / 2.0
CENTRE = (UPPER + LOWER) / 2.0
LANES = 128
SUBLANES = 8


def ring_weights(length):
    weights = [0.0] * length
    for offset in range(1, 7):
        weights[offset % length] += COEFFICIENTS[offset]
        weights[-offset % length] += COEFFICIENTS[offset]
    return weights


def pair_weights(length):
    weights = ring_weights(length)
    pairs = []
    for distance in range(1, length // 2 + 1):
        if weights[distance] != 0.0:
            pairs.append((sorted({distance, length - distance}), weights[distance]))
    return weights[0], pairs


def apply(field, diagonal, hop, before):
    ys = len(field)
    planes, xs = field[0].shape
    along_y, along_planes, along_x = [pair_weights(length)[1] for length in (ys, planes, xs)]
    results = []
    for y in range(ys):
        tile = field[y]
        total = diagonal[y] * tile
        if before is not None:
            total = total - before[y]
        for shifts, weight in along_y:
            total = total + (hop * weight) * functools.reduce(jnp.add, [field[(y - shift) % ys] for shift in shifts])
        for pairs, axis in ((along_planes, 0), (along_x, 1)):
            for shifts, weight in pairs:
                total = total + (hop * weight) * functools.reduce(
                    jnp.add, [pltpu.roll(tile, shift, axis) for shift in shifts]
                )
        results.append(total)
    return results


def filter_kernel(ng, copies, used, run, width, cores, *refs):
    orb_ref, region_ref, table_ref, counts_ref, ritz_ref, out_ref = refs
    ys, planes, xs = orb_ref.shape
    columns, panel = ritz_ref.shape
    per_row = LANES // width
    for row in range(-(-columns // per_row)):
        line = jnp.zeros((1, LANES), jnp.float32)
        for slot in range(min(per_row, columns - row * per_row)):
            piece = jnp.concatenate(
                [ritz_ref[pl.ds(row * per_row + slot, 1), :], jnp.zeros((1, LANES - panel), jnp.float32)], axis=1
            )
            line = line + (pltpu.roll(piece, slot * width, 1) if slot else piece)
        out_ref[pl.ds(run + row, copies * ng, stride=used), :] = jnp.broadcast_to(line, (copies * ng, LANES))

    centre_weight = 3.0 * COEFFICIENTS[0] + sum(pair_weights(n)[0] for n in (planes, ys, xs))
    scale = 2.0 / HALF
    hop = -0.5 / (SPACING * SPACING) * scale
    regions = table_ref.shape[1]
    values = jnp.concatenate([table_ref[...], jnp.zeros((1, xs - regions), jnp.float32)], axis=1)
    values = jnp.broadcast_to(values, (planes, xs))
    diagonal = []
    for y in range(ys):
        potential = jnp.take_along_axis(values, region_ref[y], axis=1)
        diagonal.append(scale * potential + (hop * centre_weight - scale * CENTRE))
    band_pos = lax.axis_index("row") * cores + lax.axis_index("core")
    band = lax.broadcasted_iota(jnp.int32, counts_ref.shape, 1)
    count = jnp.sum(jnp.where(band == band_pos, counts_ref[...], 0), axis=1, keepdims=True)
    live = (lax.axis_index("grid") < count).astype(jnp.float32)
    previous = [orb_ref[y] for y in range(ys)]
    current = apply(previous, [0.5 * value for value in diagonal], 0.5 * hop, None)
    previous = [live * value for value in previous]
    current = [live * value for value in current]
    for _ in range(DEGREE - 1):
        previous, current = current, apply(current, diagonal, hop, previous)

    blocks = ys // run
    for y in range(ys):
        masked = current[y]
        for copy in range(copies):
            first = (copy * ng + y // run + 1) * used + y % run
            count = planes if copy < copies - 1 or y // run < blocks - 1 else planes - 1
            out_ref[pl.ds(first, count, stride=blocks * used), :] = masked[:count]
            if count < planes:
                out_ref[pl.ds(y % run, 1), :] = masked[count:]


def partial_kernel(nrow, ng, used, run, width, columns, cores, order, distance, got_ref, out_ref, ritz_ref):
    for place, source in enumerate(order):
        ritz_ref[source] = got_ref[pl.ds(place * used + run, 1), :]
    wanted = out_ref.shape[0]
    holders = wanted // columns
    sublane = lax.broadcasted_iota(jnp.int32, (wanted, LANES), 0)
    block = lax.axis_index("row") * cores + lax.rem(lax.axis_index("core") + distance, cores)
    acc = [jnp.zeros((wanted, LANES), jnp.float32) for _ in range(run)]
    for row in range(nrow):
        lines = jnp.zeros((wanted, LANES), jnp.float32)
        for k in range(holders):
            line = ritz_ref[row * ng + block * holders + k]
            lines = jnp.where(sublane // columns == k, jnp.broadcast_to(line, (wanted, LANES)), lines)
        for r in range(ng):
            weight = jnp.take_along_axis(lines, sublane % columns * width + r, axis=1)
            for y in range(run):
                acc[y] = acc[y] + weight * got_ref[pl.ds(order.index(row * ng + r) * used + y, 1), :]
    for y in range(run):
        out_ref[:, pl.ds(y * LANES, LANES)] = acc[y]


def shards(nrow, cores, ng, orbitals, region, potential_table, counts, ritz):
    _, planes, ys, xs = orbitals.shape
    cells = planes * ys * xs
    panel, columns = ritz.shape
    run = cells // ng // xs
    width = 1
    while width < panel:
        width *= 2
    per_row = LANES // width
    ritz_rows = -(-columns // per_row)
    used = run + ritz_rows
    tiles = nrow * ng
    vmem = pl.BlockSpec(memory_space=pltpu.VMEM)
    inputs = [
        pltpu.with_memory_space_constraint(value, pltpu.HBM)
        for value in (
            jnp.transpose(orbitals[0], (1, 0, 2)), jnp.transpose(region, (1, 0, 2)), potential_table[None], counts[None], ritz.T
        )
    ]
    order = [tiles - 1] + list(range(tiles - 1))
    packed_bytes = 4 * tiles * used * LANES
    packed = pl.pallas_call(
        functools.partial(filter_kernel, ng, nrow, used, run, width, cores),
        out_shape=jax.ShapeDtypeStruct((tiles * used, LANES), jnp.float32),
        in_specs=[vmem] * 5,
        out_specs=vmem,
        compiler_params=pltpu.CompilerParams(vmem_limit_bytes=2 * packed_bytes + 64 * cells + 2**20),
        name="chebyshev_filter",
    )(*inputs)
    got = lax.all_to_all(
        packed.reshape(tiles * used, 1, LANES), ("row", "grid"), split_axis=0, concat_axis=0, tiled=True,
        axis_index_groups=[order],
    ).reshape(tiles * used, LANES)
    sum_shape = jax.ShapeDtypeStruct((panel, run * LANES), jnp.float32)
    if columns * width <= LANES and tiles <= 64 and panel == ng and panel <= 16:
        def partial_sums(distance):
            return pl.pallas_call(
                functools.partial(partial_kernel, nrow, ng, used, run, width, columns, cores, order, distance),
                out_shape=sum_shape,
                in_specs=[vmem],
                out_specs=vmem,
                scratch_shapes=[pltpu.VMEM((tiles, 1, LANES), jnp.float32)],
                compiler_params=pltpu.CompilerParams(vmem_limit_bytes=packed_bytes + 2**20),
                name="ritz_partial_sums",
            )(got)

    else:
        holders = panel // columns
        by_source = got.reshape(tiles, used, LANES)[jnp.argsort(jnp.array(order))].reshape(nrow, ng, used, LANES)
        fields = by_source[:, :, :run].reshape(tiles, run * LANES)
        blocks = by_source[:, :, run : run + ritz_rows].reshape(nrow, ng, ritz_rows * per_row, width)

        def partial_sums(distance):
            block = lax.axis_index("row") * cores + lax.rem(lax.axis_index("core") + distance, cores)
            mine = lax.dynamic_slice_in_dim(blocks, block * holders, holders, axis=1)
            return lax.dot_general(
                jnp.transpose(mine[:, :, :columns, :panel], (0, 3, 1, 2)).reshape(tiles, panel),
                fields,
                (((0,), (0,)), ((), ())),
                precision=lax.Precision.HIGHEST,
                preferred_element_type=jnp.float32,
            )

    terms = []
    for distance in range(1, cores):
        pairs = [(core, (core + distance) % cores) for core in range(cores)]
        terms.append(lax.ppermute(partial_sums(distance), "core", pairs))
    terms.append(partial_sums(0))
    return functools.reduce(jnp.add, terms)


def solution(mesh):
    bands, ng = mesh.shape["band"], mesh.shape["grid"]
    cores = 2 if bands % 2 == 0 else 1
    nrow = bands // cores
    split = jax.sharding.Mesh(mesh.devices.reshape(nrow, cores, ng), ("row", "core", "grid"))
    return jax.shard_map(
        functools.partial(shards, nrow, cores, ng),
        mesh=split,
        in_specs=(P(("row", "core", "grid"), None, None, None), P(), P(), P(), P(("row", "core"), "grid")),
        out_specs=P(("row", "core"), "grid"),
        check_vma=False,
    )
```
